128 devices in a mesh: grp: 8 (over z_lo, x), tp: 16 (over y, z_hi, core).
Axes of the slice: x: 4, y: 4, z: 4 (z_hi: 2, z_lo: 2; z = z_hi * 2 + z_lo), core: 2. Of those that a mesh axis runs over, the one named last changes fastest.
Arguments:
- old_weight: bfloat16 [8192, 8192], P(None, 'tp'), may hold values from -0.0625 to 0.0625
- delta_codes: int32 [8192, 8192], P(('grp', 'tp')), may hold values from -120 to 120
- delta_exps: int32 [8192, 64], P(('grp', 'tp')), may hold values from -14 to -12
- state_in: float32 [192, 128, 64, 128], P('grp', 'tp'), may hold values from -6 to 6
- x_in: bfloat16 [4, 192, 8192], P(None, 'grp', 'tp'), may hold values from -6 to 6
- z_in: bfloat16 [4, 192, 8192], P(None, 'grp', 'tp'), may hold values from -6 to 6
- b_in: bfloat16 [4, 192, 512], P(None, 'grp'), may hold values from -6 to 6
- c_in: bfloat16 [4, 192, 512], P(None, 'grp'), may hold values from -0.5 to 0.5
- dt_in: bfloat16 [4, 192, 128], P(None, 'grp', 'tp'), may hold values from -4 to 4
- dt_bias: float32 [128], P('tp'), may hold values from -3 to 0.5
- a_rate: float32 [128], P('tp'), may hold values from 0.05 to 4
- skip_gain: float32 [128], P('tp'), may hold values from 0.5 to 1.5
- norm_gain: float32 [8192], P('tp'), may hold values from 0.5 to 1.5
Outputs:
- mixed: bfloat16 [4, 192, 8192], P(None, 'grp', 'tp')
- final_state: float32 [192, 128, 64, 128], P('grp', 'tp')
The draws below stay inside these ranges and needn't reach their ends.
All inputs are finite; a program needn't handle non-finite values.
Results may differ from the reference program's by a relative error of at most 0.0058.
Values may be sent and summed in bfloat16 or wider, within the bound.
A program may use at most 128 MiB of HBM per device.

```python
import math
import jax
import jax.numpy as jnp
from jax import lax

D = 8192
HEADS = 128
HEAD_P = 64
STATE = 128
GROUPS = 4
BLOCK = 128
STEPS = 4
INNER = 8192
ROWS = 192


def touch_ends(array, key, low, top_value):
    shape = array.shape
    index_at = [jax.random.randint(jax.random.fold_in(key, axis), (), 0, shape[axis]) for axis in range(len(shape))]
    array = array.at[tuple(index_at)].set(low)
    longest = shape.index(max(shape))
    index_at[longest] = (index_at[longest] + 1) % shape[longest]
    return array.at[tuple(index_at)].set(top_value)


def level_of(own_key, shape, shards, smallest, largest):
    def one(axis_at, blocks):
        heights = jax.random.uniform(jax.random.fold_in(jax.random.fold_in(own_key, 6), axis_at), (blocks,), jnp.float32, smallest / len(shards), largest / len(shards))
        return jnp.repeat(jnp.exp(heights), shape[axis_at] // blocks).reshape((-1,) + (1,) * (len(shape) - axis_at - 1))

    gain = one(*shards[0])
    for cut in shards[1:]:
        gain = gain * one(*cut)
    return gain


def bell_draw(own_key, dims, scale, most, split=(), dtype=jnp.bfloat16):
    drawn = jax.random.normal(own_key, dims, jnp.float32) * scale
    if len(split) > 0:
        drawn = level_of(own_key, dims, split, -0.22, 0.18) * drawn
    return jnp.clip(drawn, min=-most, max=most).astype(dtype)


def setup_inputs(seed: int = 0) -> dict:
    key_list = jax.random.split(jax.random.key(seed), 14)
    return {
        "old_weight": bell_draw(key_list[0], (D, INNER), INNER ** -0.5, 0.0625, ((1, 16),)),
        "delta_codes": touch_ends(jax.random.randint(key_list[1], (D, INNER), -120, 121), jax.random.fold_in(key_list[1], 1), -120, 120).astype(jnp.int32),
        "delta_exps": touch_ends(jax.random.randint(key_list[2], (D, INNER // BLOCK), -14, -11), jax.random.fold_in(key_list[2], 1), -14, (-11) - 1).astype(jnp.int32),
        "state_in": bell_draw(key_list[3], (ROWS, HEADS, HEAD_P, STATE), 1.0, 6.0, ((0, 8), (1, 16)), jnp.float32),
        "x_in": bell_draw(key_list[4], (STEPS, ROWS, INNER), 1.0, 6.0, ((1, 8), (2, 16))),
        "z_in": bell_draw(key_list[5], (STEPS, ROWS, INNER), 1.0, 6.0, ((1, 8), (2, 16))),
        "b_in": bell_draw(key_list[6], (STEPS, ROWS, GROUPS * STATE), 1.0, 6.0, ((1, 8),)),
        "c_in": bell_draw(key_list[7], (STEPS, ROWS, GROUPS * STATE), STATE ** -0.5, 0.5, ((1, 8),)),
        "dt_in": bell_draw(key_list[8], (STEPS, ROWS, HEADS), 1.0, 4.0, ((1, 8), (2, 16))),
        "dt_bias": jnp.clip(-3.0 + 3.5 * jax.random.uniform(key_list[9], (HEADS,), jnp.float32) ** level_of(key_list[9], (HEADS,), ((0, 16),), -0.2, 0.2), -3.0, 0.5),
        "a_rate": jnp.clip(jnp.exp(math.log(4.0) - 4.3820266 * jax.random.uniform(key_list[10], (HEADS,), jnp.float32) ** level_of(key_list[10], (HEADS,), ((0, 16),), -0.2, 0.2)), 0.05, 4.0),
        "skip_gain": jnp.clip(0.5 + 1.0 * jax.random.uniform(key_list[11], (HEADS,), jnp.float32) ** level_of(key_list[11], (HEADS,), ((0, 16),), -0.2, 0.2), 0.5, 1.5),
        "norm_gain": jnp.clip(1.0 + 0.1 * jax.random.normal(key_list[12], (INNER,), jnp.float32), 0.5, 1.5),
    }


def reference(old_weight, delta_codes, delta_exps, state_in, x_in, z_in, b_in, c_in, dt_in, dt_bias, a_rate, skip_gain, norm_gain):
    inner_width = HEADS * HEAD_P
    block_count = inner_width // BLOCK
    block_scale = jnp.exp2(delta_exps.astype(jnp.float32))
    delta_value = (delta_codes.astype(jnp.float32).reshape(D, block_count, BLOCK) * block_scale[:, :, None]).reshape(D, inner_width).astype(jnp.bfloat16)
    new_weight = (old_weight.astype(jnp.float32) + delta_value.astype(jnp.float32)).astype(jnp.bfloat16)
    row_count = state_in.shape[0]
    per_group = HEADS // GROUPS

    def advance(carried, inputs):
        x_step, z_step, b_step, c_step, dt_step = inputs
        step_size = jax.nn.softplus(dt_step.astype(jnp.float32) + dt_bias)
        decay_factor = jnp.exp(-step_size * a_rate)
        x_heads = x_step.astype(jnp.float32).reshape(row_count, HEADS, HEAD_P)
        b_heads = jnp.repeat(b_step.astype(jnp.float32).reshape(row_count, GROUPS, STATE), per_group, axis=1)
        c_heads = jnp.repeat(c_step.astype(jnp.float32).reshape(row_count, GROUPS, STATE), per_group, axis=1)
        carried = decay_factor[:, :, None, None] * carried + (step_size[:, :, None] * x_heads)[:, :, :, None] * b_heads[:, :, None, :]
        read_out = jnp.einsum('rhpn,rhn->rhp', carried, c_heads, precision=lax.Precision.HIGHEST) + skip_gain[None, :, None] * x_heads
        gated_value = read_out.reshape(row_count, inner_width) * jax.nn.silu(z_step.astype(jnp.float32))
        grouped = gated_value.reshape(row_count, GROUPS, inner_width // GROUPS)
        mean_square = lax.optimization_barrier(jnp.mean(grouped * grouped, axis=2, keepdims=True))
        normed = (grouped * lax.rsqrt(mean_square + 1e-05)).reshape(row_count, inner_width) * norm_gain
        mixed_step = jnp.dot(normed.astype(jnp.bfloat16), new_weight.T, preferred_element_type=jnp.float32)
        return (carried, mixed_step.astype(jnp.bfloat16))
    final_state, mixed = lax.scan(advance, state_in, (x_in, z_in, b_in, c_in, dt_in))
    return (mixed, final_state)
```

```python
import functools

import jax
import jax.numpy as jnp
from jax import lax
from jax.experimental import pallas as pl
from jax.experimental.pallas import tpu as pltpu
from jax.sharding import PartitionSpec as P

MESH = pl.DeviceIdType.MESH
F32 = jnp.float32
BF16 = jnp.bfloat16
STEPS = 4
ROWS = 24
ALL = STEPS * ROWS
LOCAL = 512
STATE = 128
GROUP_WIDTH = 2048
ROW_BLOCK = 4
CONTRACT_LAST = (((1,), (1,)), ((), ()))
CONTRACT_FIRST = (((0,), (0,)), ((), ()))


def split3(value):
    first = value.astype(BF16)
    rest = value - first.astype(F32)
    second = rest.astype(BF16)
    third = (rest - second.astype(F32)).astype(BF16)
    return first, second, third


def expand_heads(value, spread):
    parts = split3(value)
    total = jnp.dot(parts[2], spread, preferred_element_type=F32)
    total = total + jnp.dot(parts[1], spread, preferred_element_type=F32)
    return total + jnp.dot(parts[0], spread, preferred_element_type=F32)


def put(ref, first, value):
    for j in range(value.shape[1] // 128):
        ref[j, first:first + value.shape[0], :] = value[:, j * 128:(j + 1) * 128]


def pick_rows(ref, row, count):
    return jnp.concatenate(
        [ref[j, pl.ds(row, count, stride=ROWS), :] for j in range(ref.shape[0])], axis=1
    )


def step_kernel(
    state_ref, x_ref, z_ref, b_ref, c_ref, dt_ref, bias_ref, rate_ref, skip_ref, gain_ref,
    final_ref, act_ref, square_ref,
    left_rows, right_rows, read_rows, read_state, decay_rows, direct_rows,
):
    at = pl.program_id(0)
    group = lax.axis_index("tp") // 4
    lanes = pl.ds(pl.multiple_of(group * STATE, STATE), STATE)

    @pl.when(at == 0)
    def _():
        heads = bias_ref.shape[1]
        head_of = lax.broadcasted_iota(jnp.int32, (heads, LOCAL), 1) // (LOCAL // heads)
        spread = (head_of == lax.broadcasted_iota(jnp.int32, (heads, LOCAL), 0)).astype(BF16)
        raw = jnp.concatenate([dt_ref[s].astype(F32) for s in range(STEPS)], axis=0)
        raw = raw + bias_ref[...]
        soft = jnp.maximum(raw, 0.0) + jnp.log1p(jnp.exp(-jnp.abs(raw)))
        rate = expand_heads(jnp.broadcast_to(rate_ref[...], (8, heads)), spread)[0:1]
        skip = expand_heads(jnp.broadcast_to(skip_ref[...], (8, heads)), spread)[0:1]
        size = expand_heads(soft, spread)
        sizes = [size[s * ROWS:(s + 1) * ROWS] for s in range(STEPS)]
        logs = []
        for s in range(STEPS):
            own = sizes[s] * rate
            logs.append(own if s == 0 else logs[-1] + own)
        xs = [x_ref[s].astype(F32) for s in range(STEPS)]
        bs = [b_ref[s, :, lanes].astype(F32) for s in range(STEPS)]
        cs = [c_ref[s, :, lanes].astype(F32) for s in range(STEPS)]
        for s in range(STEPS):
            decay_rows[s * ROWS:(s + 1) * ROWS, :] = jnp.exp(-logs[s])
            direct = skip * xs[s]
            for u in range(s + 1):
                coef = sizes[u] if u == s else sizes[u] * jnp.exp(logs[u] - logs[s])
                term = coef * xs[u]
                direct = direct + term * jnp.sum(bs[u] * cs[s], axis=1, keepdims=True)
                if s == STEPS - 1:
                    high = term.astype(BF16).astype(F32)
                    put(left_rows, u * ROWS, high)
                    put(left_rows, (4 + u) * ROWS, term - high)
            direct_rows[s * ROWS:(s + 1) * ROWS, :] = direct
        last = decay_rows[3 * ROWS:4 * ROWS, :]
        for at_row, part in enumerate(split3(last)):
            put(left_rows, (8 + at_row) * ROWS, part.astype(F32))
        put(left_rows, 11 * ROWS, jnp.zeros((5 * ROWS, LOCAL), F32))
        right_rows[...] = jnp.zeros(right_rows.shape, F32)
        read_rows[...] = jnp.zeros(read_rows.shape, F32)
        for s in range(STEPS):
            right_rows[0, s * ROWS:(s + 1) * ROWS, :] = bs[s]
            right_rows[0, (4 + s) * ROWS:(5 + s) * ROWS, :] = bs[s]
            read_rows[0, s * ROWS:(s + 1) * ROWS, :] = cs[s]
        right_rows[1, 8 * ROWS:11 * ROWS, :] = jnp.ones((3 * ROWS, STATE), F32)

    for i in range(ROW_BLOCK):
        row = at * ROW_BLOCK + i
        held = state_ref[i].reshape(LOCAL, STATE)
        high = held.astype(BF16)
        low = (held - high.astype(F32)).astype(BF16)
        both = jnp.concatenate([high, low], axis=1)
        reader = pick_rows(read_rows, row, 8).astype(BF16)
        reader = jnp.concatenate([reader, reader], axis=1)
        read = lax.dot_general(reader, both, CONTRACT_LAST, preferred_element_type=F32)
        for j in range(LOCAL // 128):
            read_state[j, pl.ds(row, 8, stride=ROWS), :] = read[:, j * 128:(j + 1) * 128]
        left = pick_rows(left_rows, row, 16).astype(BF16)
        right = pick_rows(right_rows, row, 16).astype(BF16)
        update = lax.dot_general(left, right, CONTRACT_FIRST, preferred_element_type=F32)
        final_ref[i] = (update[:, STATE:] * held + update[:, :STATE]).reshape(final_ref.shape[1:])

    @pl.when(at == pl.num_programs(0) - 1)
    def _():
        z = jnp.concatenate([z_ref[s].astype(F32) for s in range(STEPS)], axis=0)
        read = jnp.concatenate([read_state[j, 0:ALL, :] for j in range(LOCAL // 128)], axis=1)
        read_out = decay_rows[...] * read + direct_rows[...]
        gated = read_out * (z / (1.0 + jnp.exp(-z)))
        act_ref[...] = (gated * gain_ref[...]).astype(BF16)
        total = jnp.sum(gated * gated, axis=1, keepdims=True)
        total = jnp.concatenate([total, jnp.zeros((128 - ALL, 1), F32)], axis=0)
        square_ref[...] = jnp.transpose(jnp.broadcast_to(total, (128, 128)))[0:8]


def run_steps(state_in, x_in, z_in, b_in, c_in, dt_in, dt_bias, a_rate, skip_gain, norm_gain):
    whole = lambda a: pl.BlockSpec(a.shape, lambda i, nd=a.ndim: (0,) * nd)
    vectors = [v.reshape(1, -1) for v in (dt_bias, a_rate, skip_gain, norm_gain)]
    block = pl.BlockSpec((ROW_BLOCK,) + state_in.shape[1:], lambda i: (i, 0, 0, 0))
    others = [x_in, z_in, b_in, c_in, dt_in] + vectors
    return pl.pallas_call(
        step_kernel,
        grid=(ROWS // ROW_BLOCK,),
        out_shape=(
            jax.ShapeDtypeStruct(state_in.shape, F32),
            jax.ShapeDtypeStruct((ALL, LOCAL), BF16),
            jax.ShapeDtypeStruct((8, 128), F32),
        ),
        in_specs=[block] + [whole(a) for a in others],
        out_specs=(
            block,
            pl.BlockSpec((ALL, LOCAL), lambda i: (0, 0)),
            pl.BlockSpec((8, 128), lambda i: (0, 0)),
        ),
        scratch_shapes=[
            pltpu.VMEM((LOCAL // 128, 16 * ROWS, 128), F32),
            pltpu.VMEM((2, 16 * ROWS, STATE), F32),
            pltpu.VMEM((1, 8 * ROWS, STATE), F32),
            pltpu.VMEM((LOCAL // 128, 8 * ROWS, 128), F32),
            pltpu.VMEM((ALL, LOCAL), F32),
            pltpu.VMEM((ALL, LOCAL), F32),
        ],
        compiler_params=pltpu.CompilerParams(vmem_limit_bytes=60 * 1024 * 1024),
        cost_estimate=pl.CostEstimate(flops=10**8, bytes_accessed=13 * 10**6, transcendentals=0),
    )(state_in, *others)


OFFSETS = ((2, 1), (1, 1), (3, 1), (2, 0), (1, 0), (3, 0), (0, 1), (0, 0))
GATHER = ((0, 2), (1, 2), (0, 1), (0, 3), (1, 1), (1, 3), (1, 0))


def mix_kernel(
    codes_ref, exps_ref, old_ref, act_ref, square_ref, out_ref,
    codes, delta, weight, arrived, acts, parts, sums, squares,
    codes_sem, own_sem, old_send, old_recv, delta_send, delta_recv,
    act_send, act_recv, fwd_send, fwd_recv, own_act_sem,
    part_send, part_recv, square_send, square_recv,
):
    grp, tp = lax.axis_index("grp"), lax.axis_index("tp")
    z_lo, x = grp // 4, grp % 4
    y, z_hi, core = tp // 4, (tp // 2) % 2, tp % 2
    other = 1 - core
    chip = tp // 2
    partner = (grp, tp - core + other)
    mine = chip == grp
    crossed = chip == (1 - z_lo) * 4 + x

    def place(lo, xx, yy, hi, cc):
        return (lo * 4 + xx, yy * 4 + hi * 2 + cc)

    for k in range(8):
        dy, dz = OFFSETS[k]
        column = ((y + dy) % 4) * 2 + (z_hi + dz) % 2
        pltpu.make_async_copy(
            codes_ref.at[:, pl.ds(pl.multiple_of(column * 1024, 1024), 1024)], codes.at[k], codes_sem.at[k]
        ).start()

    barrier = pltpu.get_barrier_semaphore()

    def greet(where):
        pl.semaphore_signal(barrier, inc=1, device_id=where, device_id_type=MESH)

    greet(partner)
    for cc in range(2):
        for yl in range(2):
            for dz in range(2):
                where = place((z_lo + dz) % 2, x, 2 * core + yl, (z_hi + dz) % 2, cc)
                if dz == 0:
                    @pl.when(jnp.logical_not((cc == core) & (2 * core + yl == y)))
                    def _():
                        greet(where)
                else:
                    greet(where)
    for dl, dx in GATHER:
        greet(((z_lo + dl) % 2 * 4 + (x + dx) % 4, tp))
    for dt in range(1, 16):
        greet((grp, (tp + dt) % 16))
    for lo in range(2):
        for yy in range(4):
            for hi in range(2):
                where = place(lo, chip % 4, yy, hi, core)

                @pl.when(jnp.logical_not((where[0] == grp) & (where[1] == tp)))
                def _():
                    greet(where)
    own_delta = core == y // 2
    expected = (
        1 + 8 - own_delta.astype(jnp.int32) + 7 + 15 + 16 - mine.astype(jnp.int32) - crossed.astype(jnp.int32)
    )
    pl.semaphore_wait(barrier, expected)

    def act_copy(k):
        dl, dx = GATHER[k]
        return pltpu.make_async_remote_copy(
            src_ref=act_ref, dst_ref=acts.at[grp, :, pl.ds(pl.multiple_of(core * LOCAL, LOCAL), LOCAL)],
            send_sem=act_send.at[k], recv_sem=act_recv.at[k],
            device_id=((z_lo + dl) % 2 * 4 + (x + dx) % 4, tp), device_id_type=MESH,
        )

    def fwd_copy(k):
        if k == 7:
            source, slot = act_ref, grp
        else:
            dl, dx = GATHER[k]
            slot = (z_lo + dl) % 2 * 4 + (x + 4 - dx) % 4
            source = acts.at[slot, :, pl.ds(pl.multiple_of(core * LOCAL, LOCAL), LOCAL)]
        return pltpu.make_async_remote_copy(
            src_ref=source, dst_ref=acts.at[slot, :, pl.ds(pl.multiple_of(core * LOCAL, LOCAL), LOCAL)],
            send_sem=fwd_send.at[k], recv_sem=fwd_recv.at[k],
            device_id=partner, device_id_type=MESH,
        )

    def square_copy(k):
        return pltpu.make_async_remote_copy(
            src_ref=square_ref, dst_ref=squares.at[tp],
            send_sem=square_send.at[k], recv_sem=square_recv.at[k],
            device_id=(grp, (tp + k + 1) % 16), device_id_type=MESH,
        )

    def feature_row(slab, cc):
        dz, yl = slab // 2, slab % 2
        lo, hi = (z_lo + dz) % 2, (z_hi + dz) % 2
        row = ((lo * 4 + x) * 2 + cc) * 512 + yl * 256 + hi * 128
        return pl.ds(pl.multiple_of(row, 128), 128)

    def own_copy(slab):
        return pltpu.make_async_copy(
            old_ref.at[feature_row(slab, core)],
            weight.at[pl.ds(slab * 128, 128), pl.ds(pl.multiple_of(core * LOCAL, LOCAL), LOCAL)],
            own_sem.at[slab],
        )

    def old_copy(slab):
        return pltpu.make_async_remote_copy(
            src_ref=old_ref.at[feature_row(slab, other)],
            dst_ref=weight.at[pl.ds(slab * 128, 128), pl.ds(pl.multiple_of(core * LOCAL, LOCAL), LOCAL)],
            send_sem=old_send.at[slab], recv_sem=old_recv.at[slab],
            device_id=partner, device_id_type=MESH,
        )

    def delta_copy(k):
        dy, dz = OFFSETS[k]
        first = pl.multiple_of(dz * 256 + (y % 2) * 128 + core * 64, 64)
        slot = dz * 4 + (y % 2) * 2 + core
        return pltpu.make_async_remote_copy(
            src_ref=delta.at[k], dst_ref=arrived.at[pl.ds(first, 64)],
            send_sem=delta_send.at[k], recv_sem=delta_recv.at[slot],
            device_id=place((z_lo + dz) % 2, x, (y + dy) % 4, (z_hi + dz) % 2, y // 2), device_id_type=MESH,
        )

    def delta_self():
        first = pl.multiple_of((y % 2) * 128 + core * 64, 64)
        return pltpu.make_async_copy(
            delta.at[7], arrived.at[pl.ds(first, 64)], delta_recv.at[(y % 2) * 2 + core]
        )

    scale = jnp.where(
        exps_ref[...] == -14, 2.0**-14, jnp.where(exps_ref[...] == -13, 2.0**-13, 2.0**-12)
    ).astype(BF16)
    block_at = lax.broadcasted_iota(jnp.int32, (64, 1024), 0)
    lane_block = lax.broadcasted_iota(jnp.int32, (64, 1024), 1) // 128
    for k in range(8):
        dy, dz = OFFSETS[k]
        column = ((y + dy) % 4) * 2 + (z_hi + dz) % 2
        pltpu.make_async_copy(codes.at[k], codes.at[k], codes_sem.at[k]).wait()
        pick = (block_at == lane_block + column * 8).astype(BF16)
        wide = jnp.dot(scale, pick, preferred_element_type=F32)
        delta[k] = (codes[k].astype(F32) * wide).astype(BF16)
        if k < 7:
            delta_copy(k).start()
        else:
            @pl.when(own_delta)
            def _():
                delta_self().start()

            @pl.when(jnp.logical_not(own_delta))
            def _():
                delta_copy(7).start()
        if k < 7:
            act_copy(k).start()
    fwd_copy(7).start()
    own_act = pltpu.make_async_copy(
        act_ref, acts.at[grp, :, pl.ds(pl.multiple_of(core * LOCAL, LOCAL), LOCAL)], own_act_sem
    )
    own_act.start()
    for slab in range(4):
        own_copy(slab).start()
        old_copy(slab).start()
    for k in range(15):
        square_copy(k).start()
    squares[tp] = square_ref[...]

    for k in range(7):
        act_copy(k).wait_recv()
        fwd_copy(k).start()
    own_act.wait()
    for k in range(8):
        fwd_copy(k).wait_recv()

    def part_copy(half, g):
        lo = (z_lo + half) % 2
        dest = (g, (lo * 4 + x) * 2 + core)
        slot = ((z_hi + half) % 2) * 8 + y * 2 + half
        remote = lambda: pltpu.make_async_remote_copy(
            src_ref=parts.at[half * 8 + g], dst_ref=sums.at[slot],
            send_sem=part_send.at[half * 8 + g], recv_sem=part_recv.at[slot],
            device_id=dest, device_id_type=MESH,
        )
        local = lambda: pltpu.make_async_copy(parts.at[half * 8 + g], sums.at[slot], part_recv.at[slot])
        here = (dest[0] == grp) & (dest[1] == tp)
        return remote, local, here

    for half in range(2):
        for slab in (half * 2, half * 2 + 1):
            own_copy(slab).wait()
            old_copy(slab).wait_recv()
        for slot in range(half * 4, half * 4 + 4):
            rows = arrived.at[pl.ds(slot * 64, 64)]
            pltpu.make_async_copy(rows, rows, delta_recv.at[slot]).wait()
        span = slice(half * 256, half * 256 + 256)
        fresh = (weight[span, :].astype(F32) + arrived[span, :].astype(F32)).astype(BF16)
        for quarter in range(4):
            lhs = acts[quarter * 2:quarter * 2 + 2].reshape(2 * ALL, 1024)
            got = lax.dot_general(lhs, fresh, CONTRACT_LAST, preferred_element_type=F32)
            for part in range(2):
                g = quarter * 2 + part
                parts[half * 8 + g] = got[part * ALL:(part + 1) * ALL].astype(BF16)
                remote, local, here = part_copy(half, g)

                @pl.when(here)
                def _():
                    local().start()

                @pl.when(jnp.logical_not(here))
                def _():
                    remote().start()

    for k in range(15):
        square_copy(k).wait_recv()
    by_group = [
        squares[4 * yy] + squares[4 * yy + 1] + squares[4 * yy + 2] + squares[4 * yy + 3] for yy in range(4)
    ]
    factors = []
    for yy in range(4):
        inverse = lax.rsqrt(by_group[yy] * (1.0 / GROUP_WIDTH) + 1e-05)
        tall = jnp.concatenate([inverse] * 16, axis=0)
        factors.append(jnp.transpose(tall)[0:ALL, 0:1])
    for hi in range(2):
        total = None
        for yy in range(4):
            pair = None
            for half in range(2):
                slot = hi * 8 + yy * 2 + half
                pltpu.make_async_copy(sums.at[slot], sums.at[slot], part_recv.at[slot]).wait()
                value = sums[slot].astype(F32)
                pair = value if pair is None else pair + value
            pair = pair * factors[yy]
            total = pair if total is None else total + pair
        for s in range(STEPS):
            for yl in range(2):
                out_ref[s, :, yl * 256 + hi * 128:yl * 256 + hi * 128 + 128] = total[
                    s * ROWS:(s + 1) * ROWS, yl * 128:(yl + 1) * 128
                ].astype(BF16)

    for k in range(7):
        delta_copy(k).wait_send()
        act_copy(k).wait_send()
    for k in range(8):
        fwd_copy(k).wait_send()

    @pl.when(jnp.logical_not(own_delta))
    def _():
        delta_copy(7).wait_send()
    for slab in range(4):
        old_copy(slab).wait_send()
    for k in range(15):
        square_copy(k).wait_send()
    for half in range(2):
        for g in range(8):
            remote, local, here = part_copy(half, g)

            @pl.when(jnp.logical_not(here))
            def _():
                remote().wait_send()


def run_mix(delta_codes, delta_exps, old_weight, act, square):
    vmem = pl.BlockSpec(memory_space=pltpu.VMEM)
    hbm = pl.BlockSpec(memory_space=pltpu.HBM)
    dma = pltpu.SemaphoreType.DMA
    return pl.pallas_call(
        mix_kernel,
        out_shape=jax.ShapeDtypeStruct((STEPS, ROWS, LOCAL), BF16),
        in_specs=[hbm, vmem, hbm, vmem, vmem],
        out_specs=vmem,
        scratch_shapes=[
            pltpu.VMEM((8, 64, 1024), jnp.int32),
            pltpu.VMEM((8, 64, 1024), BF16),
            pltpu.VMEM((512, 1024), BF16),
            pltpu.VMEM((512, 1024), BF16),
            pltpu.VMEM((8, ALL, 1024), BF16),
            pltpu.VMEM((16, ALL, 256), BF16),
            pltpu.VMEM((16, ALL, 256), BF16),
            pltpu.VMEM((16, 8, 128), F32),
            dma((8,)), dma((4,)), dma((4,)), dma((4,)), dma((8,)), dma((8,)),
            dma((7,)), dma((7,)), dma((8,)), dma((8,)), dma,
            dma((16,)), dma((16,)), dma((15,)), dma((15,)),
        ],
        compiler_params=pltpu.CompilerParams(
            collective_id=0, has_side_effects=True, vmem_limit_bytes=60 * 1024 * 1024
        ),
        cost_estimate=pl.CostEstimate(flops=8 * 10**8, bytes_accessed=4 * 10**6, transcendentals=0),
    )(delta_codes, delta_exps, old_weight, act, square)


def local(
    old_weight, delta_codes, delta_exps, state_in, x_in, z_in, b_in, c_in, dt_in,
    dt_bias, a_rate, skip_gain, norm_gain,
):
    final_state, act, square = run_steps(
        state_in, x_in, z_in, b_in, c_in, dt_in, dt_bias, a_rate, skip_gain, norm_gain
    )
    mixed = run_mix(delta_codes, delta_exps, old_weight, act, square)
    return mixed, final_state


def solution(mesh):
    return jax.shard_map(
        local,
        mesh=mesh,
        in_specs=(
            P(None, "tp"),
            P(("grp", "tp"), None),
            P(("grp", "tp"), None),
            P("grp", "tp", None, None),
            P(None, "grp", "tp"),
            P(None, "grp", "tp"),
            P(None, "grp", None),
            P(None, "grp", None),
            P(None, "grp", "tp"),
            P("tp"),
            P("tp"),
            P("tp"),
            P("tp"),
        ),
        out_specs=(P(None, "grp", "tp"), P("grp", "tp", None, None)),
        check_vma=False,
    )
```

```python
import functools

import jax
import jax.numpy as jnp
from jax import lax
from jax.experimental import pallas as pl
from jax.experimental.pallas import tpu as pltpu
from jax.sharding import PartitionSpec as P

MESH = pl.DeviceIdType.MESH
F32 = jnp.float32
BF16 = jnp.bfloat16
STEPS = 4
ROWS = 24
ALL = STEPS * ROWS
LOCAL = 512
STATE = 128
GROUP_WIDTH = 2048
CHUNKS = 3
CHUNK_ROWS = ROWS // CHUNKS
SENT_ROWS = STEPS * CHUNK_ROWS
HEADS = 8
CONTRACT_LAST = (((1,), (1,)), ((), ()))
CONTRACT_FIRST = (((0,), (0,)), ((), ()))


def split3(value):
    first = value.astype(BF16)
    rest = value - first.astype(F32)
    second = rest.astype(BF16)
    third = (rest - second.astype(F32)).astype(BF16)
    return first, second, third


def expand_heads(value, spread):
    parts = split3(value)
    total = jnp.dot(parts[2], spread, preferred_element_type=F32)
    total = total + jnp.dot(parts[1], spread, preferred_element_type=F32)
    return total + jnp.dot(parts[0], spread, preferred_element_type=F32)


def put(ref, first, value):
    for j in range(value.shape[1] // 128):
        ref[j, first:first + value.shape[0], :] = value[:, j * 128:(j + 1) * 128]


def pick_rows(ref, row, count):
    return jnp.concatenate(
        [ref[j, pl.ds(row, count, stride=ROWS), :] for j in range(ref.shape[0])], axis=1
    )


UNROLL = 4
OFFSETS = ((2, 1), (1, 1), (3, 1), (2, 0), (1, 0), (3, 0), (0, 1), (0, 0))
GATHER = ((0, 2), (1, 2), (0, 1), (0, 3), (1, 1), (1, 3), (1, 0))


def mix_kernel(
    codes_ref, exps_ref, old_ref, state_ref, x_ref, z_ref, b_ref, c_ref, dt_ref,
    bias_ref, rate_ref, skip_ref, gain_ref,
    held, sums, squares,
    exps, xs_in, zs_in, bs_in, cs_in, dts_in, bias_in, rate_in, skip_in, gain_in,
    left_rows, right_rows, read_rows, read_state, decay_rows, direct_rows, square_rows,
    codes, delta, weight, arrived, acts, parts,
    small_sem, state_sem, codes_sem, own_sem, old_send, old_recv, delta_send, delta_recv,
    act_send, act_recv, fwd_send, fwd_recv, part_send, part_recv, square_send, square_recv,
):
    grp, tp = lax.axis_index("grp"), lax.axis_index("tp")
    z_lo, x = grp // 4, grp % 4
    y, z_hi, core = tp // 4, (tp // 2) % 2, tp % 2
    other = 1 - core
    chip = tp // 2
    partner = (grp, tp - core + other)
    mine = chip == grp
    crossed = chip == (1 - z_lo) * 4 + x

    def place(lo, xx, yy, hi, cc):
        return (lo * 4 + xx, yy * 4 + hi * 2 + cc)

    for k in range(8):
        dy, dz = OFFSETS[k]
        column = ((y + dy) % 4) * 2 + (z_hi + dz) % 2
        pltpu.make_async_copy(
            codes_ref.at[:, pl.ds(pl.multiple_of(column * 1024, 1024), 1024)], codes.at[k], codes_sem.at[k]
        ).start()

    small = [
        (exps_ref, exps), (dt_ref, dts_in), (bias_ref, bias_in), (rate_ref, rate_in), (skip_ref, skip_in),
        (x_ref, xs_in), (b_ref, bs_in), (c_ref, cs_in), (z_ref, zs_in), (gain_ref, gain_in),
    ]

    def small_copy(k):
        return pltpu.make_async_copy(small[k][0], small[k][1], small_sem.at[k])

    def state_copy(c):
        span = pl.ds(c * CHUNK_ROWS, CHUNK_ROWS)
        return pltpu.make_async_copy(state_ref.at[span], held.at[span], state_sem.at[c])

    for k in range(len(small)):
        small_copy(k).start()
    for c in range(CHUNKS):
        state_copy(c).start()

    barrier = pltpu.get_barrier_semaphore()

    def greet(where):
        pl.semaphore_signal(barrier, inc=1, device_id=where, device_id_type=MESH)

    greet(partner)
    for cc in range(2):
        for yl in range(2):
            for dz in range(2):
                where = place((z_lo + dz) % 2, x, 2 * core + yl, (z_hi + dz) % 2, cc)
                if dz == 0:
                    @pl.when(jnp.logical_not((cc == core) & (2 * core + yl == y)))
                    def _():
                        greet(where)
                else:
                    greet(where)
    for dl, dx in GATHER:
        greet(((z_lo + dl) % 2 * 4 + (x + dx) % 4, tp))
    for dt in range(1, 16):
        greet((grp, (tp + dt) % 16))
    for lo in range(2):
        for yy in range(4):
            for hi in range(2):
                where = place(lo, chip % 4, yy, hi, core)

                @pl.when(jnp.logical_not((where[0] == grp) & (where[1] == tp)))
                def _():
                    greet(where)
    own_delta = core == y // 2
    expected = (
        1 + 8 - own_delta.astype(jnp.int32) + 7 + 15 + 16 - mine.astype(jnp.int32) - crossed.astype(jnp.int32)
    )
    own_lanes = pl.ds(pl.multiple_of(core * LOCAL, LOCAL), LOCAL)

    def act_copy(c, k):
        dl, dx = GATHER[k]
        piece = acts.at[grp, pl.ds(c * SENT_ROWS, SENT_ROWS), own_lanes]
        return pltpu.make_async_remote_copy(
            src_ref=piece, dst_ref=piece,
            send_sem=act_send.at[c * 7 + k], recv_sem=act_recv.at[c * 7 + k],
            device_id=((z_lo + dl) % 2 * 4 + (x + dx) % 4, tp), device_id_type=MESH,
        )

    def fwd_copy(c, k):
        slot = grp
        if k < 7:
            dl, dx = GATHER[k]
            slot = (z_lo + dl) % 2 * 4 + (x + 4 - dx) % 4
        piece = acts.at[slot, pl.ds(c * SENT_ROWS, SENT_ROWS), own_lanes]
        return pltpu.make_async_remote_copy(
            src_ref=piece, dst_ref=piece,
            send_sem=fwd_send.at[c * 8 + k], recv_sem=fwd_recv.at[c * 8 + k],
            device_id=partner, device_id_type=MESH,
        )

    def square_copy(k):
        return pltpu.make_async_remote_copy(
            src_ref=squares.at[tp], dst_ref=squares.at[tp],
            send_sem=square_send.at[k], recv_sem=square_recv.at[k],
            device_id=(grp, (tp + k + 1) % 16), device_id_type=MESH,
        )

    def feature_row(slab, cc):
        dz, yl = slab // 2, slab % 2
        lo, hi = (z_lo + dz) % 2, (z_hi + dz) % 2
        row = ((lo * 4 + x) * 2 + cc) * 512 + yl * 256 + hi * 128
        return pl.ds(pl.multiple_of(row, 128), 128)

    def own_copy(slab):
        return pltpu.make_async_copy(
            old_ref.at[feature_row(slab, core)],
            weight.at[pl.ds(slab * 128, 128), pl.ds(pl.multiple_of(core * LOCAL, LOCAL), LOCAL)],
            own_sem.at[slab],
        )

    def old_copy(slab):
        return pltpu.make_async_remote_copy(
            src_ref=old_ref.at[feature_row(slab, other)],
            dst_ref=weight.at[pl.ds(slab * 128, 128), pl.ds(pl.multiple_of(core * LOCAL, LOCAL), LOCAL)],
            send_sem=old_send.at[slab], recv_sem=old_recv.at[slab],
            device_id=partner, device_id_type=MESH,
        )

    def delta_copy(k):
        dy, dz = OFFSETS[k]
        first = pl.multiple_of(dz * 256 + (y % 2) * 128 + core * 64, 64)
        slot = dz * 4 + (y % 2) * 2 + core
        return pltpu.make_async_remote_copy(
            src_ref=delta.at[k], dst_ref=arrived.at[pl.ds(first, 64)],
            send_sem=delta_send.at[k], recv_sem=delta_recv.at[slot],
            device_id=place((z_lo + dz) % 2, x, (y + dy) % 4, (z_hi + dz) % 2, y // 2), device_id_type=MESH,
        )

    def delta_self():
        first = pl.multiple_of((y % 2) * 128 + core * 64, 64)
        return pltpu.make_async_copy(
            delta.at[7], arrived.at[pl.ds(first, 64)], delta_recv.at[(y % 2) * 2 + core]
        )

    small_copy(0).wait()
    scale = jnp.where(
        exps[...] == -14, 2.0**-14, jnp.where(exps[...] == -13, 2.0**-13, 2.0**-12)
    ).astype(BF16)
    block_at = lax.broadcasted_iota(jnp.int32, (64, 1024), 0)
    lane_block = lax.broadcasted_iota(jnp.int32, (64, 1024), 1) // 128
    for k in range(8):
        dy, dz = OFFSETS[k]
        column = ((y + dy) % 4) * 2 + (z_hi + dz) % 2
        pltpu.make_async_copy(codes.at[k], codes.at[k], codes_sem.at[k]).wait()
        pick = (block_at == lane_block + column * 8).astype(BF16)
        wide = jnp.dot(scale, pick, preferred_element_type=F32)
        delta[k] = (codes[k].astype(F32) * wide).astype(BF16)
    pl.semaphore_wait(barrier, expected)
    for k in range(7):
        delta_copy(k).start()

    @pl.when(own_delta)
    def _():
        delta_self().start()

    @pl.when(jnp.logical_not(own_delta))
    def _():
        delta_copy(7).start()

    for slab in range(4):
        own_copy(slab).start()
        old_copy(slab).start()

    for k in range(1, len(small)):
        small_copy(k).wait()
    group = tp // 4
    group_lanes = pl.ds(pl.multiple_of(group * STATE, STATE), STATE)
    head_of = lax.broadcasted_iota(jnp.int32, (HEADS, LOCAL), 1) // (LOCAL // HEADS)
    spread = (head_of == lax.broadcasted_iota(jnp.int32, (HEADS, LOCAL), 0)).astype(BF16)
    bias = expand_heads(jnp.broadcast_to(bias_in[...], (8, HEADS)), spread)[0:1]
    rate = expand_heads(jnp.broadcast_to(rate_in[...], (8, HEADS)), spread)[0:1]
    skip = expand_heads(jnp.broadcast_to(skip_in[...], (8, HEADS)), spread)[0:1]
    sizes, logs = [], []
    for s in range(STEPS):
        raw = lax.dot_general(dts_in[s], spread, CONTRACT_FIRST, preferred_element_type=F32) + bias
        sizes.append(jnp.maximum(raw, 0.0) + jnp.log1p(jnp.exp(-jnp.abs(raw))))
        own = sizes[s] * rate
        logs.append(own if s == 0 else logs[-1] + own)
    xs = [xs_in[s].astype(F32) for s in range(STEPS)]
    bs = [bs_in[s, :, group_lanes].astype(F32) for s in range(STEPS)]
    cs = [cs_in[s, :, group_lanes].astype(F32) for s in range(STEPS)]
    right_rows[...] = jnp.zeros(right_rows.shape, F32)
    read_rows[...] = jnp.zeros(read_rows.shape, F32)
    for s in range(STEPS):
        right_rows[0, s * ROWS:(s + 1) * ROWS, :] = bs[s]
        right_rows[0, (4 + s) * ROWS:(5 + s) * ROWS, :] = bs[s]
        read_rows[0, s * ROWS:(s + 1) * ROWS, :] = cs[s]
    right_rows[1, 8 * ROWS:11 * ROWS, :] = jnp.ones((3 * ROWS, STATE), F32)
    for s in range(STEPS):
        decay_rows[s * ROWS:(s + 1) * ROWS, :] = jnp.exp(-logs[s])
        direct = skip * xs[s]
        for u in range(s + 1):
            coef = sizes[u] if u == s else sizes[u] * jnp.exp(logs[u] - logs[s])
            term = coef * xs[u]
            direct = direct + term * jnp.sum(bs[u] * cs[s], axis=1, keepdims=True)
            if s == STEPS - 1:
                high = term.astype(BF16).astype(F32)
                put(left_rows, u * ROWS, high)
                put(left_rows, (4 + u) * ROWS, term - high)
        direct_rows[s * ROWS:(s + 1) * ROWS, :] = direct
    last = decay_rows[3 * ROWS:4 * ROWS, :]
    for at_row, part in enumerate(split3(last)):
        put(left_rows, (8 + at_row) * ROWS, part.astype(F32))
    put(left_rows, 11 * ROWS, jnp.zeros((5 * ROWS, LOCAL), F32))
    square_rows[ALL:, :] = jnp.zeros((128 - ALL, 128), F32)

    def read_one(row):
        value = held[row].reshape(LOCAL, STATE)
        high = value.astype(BF16)
        low = (value - high.astype(F32)).astype(BF16)
        both = jnp.concatenate([high, low], axis=1)
        reader = pick_rows(read_rows, row, 8).astype(BF16)
        reader = jnp.concatenate([reader, reader], axis=1)
        read = lax.dot_general(reader, both, CONTRACT_LAST, preferred_element_type=F32)
        for j in range(LOCAL // 128):
            read_state[j, pl.ds(row, 8, stride=ROWS), :] = read[:, j * 128:(j + 1) * 128]

    def update_one(row):
        left = pick_rows(left_rows, row, 16).astype(BF16)
        right = pick_rows(right_rows, row, 16).astype(BF16)
        update = lax.dot_general(left, right, CONTRACT_FIRST, preferred_element_type=F32)
        value = held[row].reshape(LOCAL, STATE)
        held[row] = (update[:, STATE:] * value + update[:, :STATE]).reshape(held.shape[1:])

    def over_rows(first, count, unroll, one):
        def some(i, carry):
            for j in range(unroll):
                one(first + i * unroll + j)
            return carry

        lax.fori_loop(0, count // unroll, some, 0)

    for c in range(CHUNKS):
        state_copy(c).wait()
        over_rows(c * CHUNK_ROWS, CHUNK_ROWS, UNROLL, read_one)
        pieces = []
        for s in range(STEPS):
            span = slice(s * ROWS + c * CHUNK_ROWS, s * ROWS + (c + 1) * CHUNK_ROWS)
            read = jnp.concatenate([read_state[j, span, :] for j in range(LOCAL // 128)], axis=1)
            z = zs_in[s].astype(F32)[c * CHUNK_ROWS:(c + 1) * CHUNK_ROWS]
            read_out = decay_rows[span, :] * read + direct_rows[span, :]
            pieces.append(read_out * (z / (1.0 + jnp.exp(-z))))
        gated = jnp.concatenate(pieces, axis=0)
        acts[grp, c * SENT_ROWS:(c + 1) * SENT_ROWS, own_lanes] = (gated * gain_in[...]).astype(BF16)
        for k in range(7):
            act_copy(c, k).start()
        fwd_copy(c, 7).start()
        total = jnp.sum(gated * gated, axis=1, keepdims=True)
        square_rows[c * SENT_ROWS:(c + 1) * SENT_ROWS, :] = jnp.broadcast_to(total, (SENT_ROWS, 128))
    squares[tp] = jnp.transpose(square_rows[...])[0:8]
    for k in range(15):
        square_copy(k).start()

    for c in range(CHUNKS):
        over_rows(c * CHUNK_ROWS, CHUNK_ROWS, UNROLL, update_one)
        for k in range(7):
            act_copy(c, k).wait_recv()
            fwd_copy(c, k).start()
    for c in range(CHUNKS):
        for k in range(8):
            fwd_copy(c, k).wait_recv()

    def part_copy(half, g):
        lo = (z_lo + half) % 2
        dest = (g, (lo * 4 + x) * 2 + core)
        slot = ((z_hi + half) % 2) * 8 + y * 2 + half
        remote = lambda: pltpu.make_async_remote_copy(
            src_ref=parts.at[half * 8 + g], dst_ref=sums.at[slot],
            send_sem=part_send.at[half * 8 + g], recv_sem=part_recv.at[slot],
            device_id=dest, device_id_type=MESH,
        )
        local = lambda: pltpu.make_async_copy(parts.at[half * 8 + g], sums.at[slot], part_recv.at[slot])
        here = (dest[0] == grp) & (dest[1] == tp)
        return remote, local, here

    for half in range(2):
        for slab in (half * 2, half * 2 + 1):
            own_copy(slab).wait()
            old_copy(slab).wait_recv()
        for slot in range(half * 4, half * 4 + 4):
            rows = arrived.at[pl.ds(slot * 64, 64)]
            pltpu.make_async_copy(rows, rows, delta_recv.at[slot]).wait()
        span = slice(half * 256, half * 256 + 256)
        fresh = (weight[span, :].astype(F32) + arrived[span, :].astype(F32)).astype(BF16)
        for quarter in range(4):
            lhs = acts[quarter * 2:quarter * 2 + 2].reshape(2 * ALL, 1024)
            got = lax.dot_general(lhs, fresh, CONTRACT_LAST, preferred_element_type=F32)
            for part in range(2):
                g = quarter * 2 + part
                parts[half * 8 + g] = got[part * ALL:(part + 1) * ALL].astype(BF16)
                remote, local, here = part_copy(half, g)

                @pl.when(here)
                def _():
                    local().start()

                @pl.when(jnp.logical_not(here))
                def _():
                    remote().start()

    for k in range(15):
        square_copy(k).wait_recv()
    for slot in range(16):
        pltpu.make_async_copy(sums.at[slot], sums.at[slot], part_recv.at[slot]).wait()

    for k in range(7):
        delta_copy(k).wait_send()
    for c in range(CHUNKS):
        for k in range(7):
            act_copy(c, k).wait_send()
        for k in range(8):
            fwd_copy(c, k).wait_send()

    @pl.when(jnp.logical_not(own_delta))
    def _():
        delta_copy(7).wait_send()
    for slab in range(4):
        old_copy(slab).wait_send()
    for k in range(15):
        square_copy(k).wait_send()
    for half in range(2):
        for g in range(8):
            remote, local, here = part_copy(half, g)

            @pl.when(jnp.logical_not(here))
            def _():
                remote().wait_send()


def finish_kernel(held, sums, squares, out_ref, final_ref, sem):
    copies = [
        pltpu.make_async_copy(held.at[pl.ds(c * 6, 6)], final_ref.at[pl.ds(c * 6, 6)], sem.at[c])
        for c in range(4)
    ]
    for copy in copies:
        copy.start()
    factors = []
    for yy in range(4):
        total = squares[4 * yy] + squares[4 * yy + 1] + squares[4 * yy + 2] + squares[4 * yy + 3]
        inverse = lax.rsqrt(total * (1.0 / GROUP_WIDTH) + 1e-05)
        factors.append(jnp.transpose(jnp.concatenate([inverse] * 16, axis=0))[0:ALL, 0:1])
    for hi in range(2):
        total = None
        for yy in range(4):
            slot = hi * 8 + yy * 2
            pair = (sums[slot].astype(F32) + sums[slot + 1].astype(F32)) * factors[yy]
            total = pair if total is None else total + pair
        for s in range(STEPS):
            rows = jnp.concatenate(
                [
                    total[c * SENT_ROWS + s * CHUNK_ROWS:c * SENT_ROWS + (s + 1) * CHUNK_ROWS]
                    for c in range(CHUNKS)
                ],
                axis=0,
            ).astype(BF16)
            for yl in range(2):
                at = yl * 256 + hi * 128
                out_ref[s, :, at:at + 128] = rows[:, yl * 128:(yl + 1) * 128]
    for copy in copies:
        copy.wait()


def local(
    old_weight, delta_codes, delta_exps, state_in, x_in, z_in, b_in, c_in, dt_in,
    dt_bias, a_rate, skip_gain, norm_gain,
):
    vmem = pl.BlockSpec(memory_space=pltpu.VMEM)
    hbm = pl.BlockSpec(memory_space=pltpu.HBM)
    dma = pltpu.SemaphoreType.DMA
    vectors = [v.reshape(1, -1) for v in (dt_bias, a_rate, skip_gain, norm_gain)]
    held, sums, squares = pl.pallas_call(
        mix_kernel,
        out_shape=(
            pltpu.VMEM(state_in.shape, F32),
            pltpu.VMEM((16, ALL, 256), BF16),
            pltpu.VMEM((16, 8, 128), F32),
        ),
        in_specs=[hbm] * 13,
        out_specs=(vmem, vmem, vmem),
        scratch_shapes=[
            pltpu.VMEM((64, 64), jnp.int32),
            pltpu.VMEM(x_in.shape, BF16),
            pltpu.VMEM(x_in.shape, BF16),
            pltpu.VMEM(b_in.shape, BF16),
            pltpu.VMEM(b_in.shape, BF16),
            pltpu.VMEM((STEPS, HEADS, ROWS), BF16),
            pltpu.VMEM((1, HEADS), F32),
            pltpu.VMEM((1, HEADS), F32),
            pltpu.VMEM((1, HEADS), F32),
            pltpu.VMEM((1, LOCAL), F32),
            pltpu.VMEM((LOCAL // 128, 16 * ROWS, 128), F32),
            pltpu.VMEM((2, 16 * ROWS, STATE), F32),
            pltpu.VMEM((1, 8 * ROWS, STATE), F32),
            pltpu.VMEM((LOCAL // 128, 8 * ROWS, 128), F32),
            pltpu.VMEM((ALL, LOCAL), F32),
            pltpu.VMEM((ALL, LOCAL), F32),
            pltpu.VMEM((128, 128), F32),
            pltpu.VMEM((8, 64, 1024), jnp.int32),
            pltpu.VMEM((8, 64, 1024), BF16),
            pltpu.VMEM((512, 1024), BF16),
            pltpu.VMEM((512, 1024), BF16),
            pltpu.VMEM((8, ALL, 1024), BF16),
            pltpu.VMEM((16, ALL, 256), BF16),
            dma((10,)), dma((CHUNKS,)), dma((8,)), dma((4,)), dma((4,)), dma((4,)), dma((8,)), dma((8,)),
            dma((7 * CHUNKS,)), dma((7 * CHUNKS,)), dma((8 * CHUNKS,)), dma((8 * CHUNKS,)),
            dma((16,)), dma((16,)), dma((15,)), dma((15,)),
        ],
        compiler_params=pltpu.CompilerParams(
            collective_id=0, has_side_effects=True, vmem_limit_bytes=36 * 1024 * 1024
        ),
        cost_estimate=pl.CostEstimate(flops=9 * 10**8, bytes_accessed=10**7, transcendentals=0),
    )(
        *[
            pltpu.with_memory_space_constraint(a, pltpu.HBM)
            for a in (
                delta_codes, delta_exps, old_weight, state_in, x_in, z_in, b_in, c_in,
                jnp.swapaxes(dt_in, 1, 2), *vectors,
            )
        ]
    )
    mixed, final_state = pl.pallas_call(
        finish_kernel,
        out_shape=(
            jax.ShapeDtypeStruct((STEPS, ROWS, LOCAL), BF16),
            jax.ShapeDtypeStruct(state_in.shape, F32),
        ),
        in_specs=[vmem] * 3,
        out_specs=(vmem, hbm),
        scratch_shapes=[dma((4,))],
        compiler_params=pltpu.CompilerParams(vmem_limit_bytes=36 * 1024 * 1024),
        cost_estimate=pl.CostEstimate(flops=10**6, bytes_accessed=7 * 10**6, transcendentals=0),
    )(held, sums, squares)
    return mixed, final_state


def solution(mesh):
    return jax.shard_map(
        local,
        mesh=mesh,
        in_specs=(
            P(None, "tp"),
            P(("grp", "tp"), None),
            P(("grp", "tp"), None),
            P("grp", "tp", None, None),
            P(None, "grp", "tp"),
            P(None, "grp", "tp"),
            P(None, "grp", None),
            P(None, "grp", None),
            P(None, "grp", "tp"),
            P("tp"),
            P("tp"),
            P("tp"),
            P("tp"),
        ),
        out_specs=(P(None, "grp", "tp"), P("grp", "tp", None, None)),
        check_vma=False,
    )
```

```python
import functools

import jax
import jax.numpy as jnp
from jax import lax
from jax.experimental import pallas as pl
from jax.experimental.pallas import tpu as pltpu
from jax.sharding import PartitionSpec as P

MESH = pl.DeviceIdType.MESH
F32 = jnp.float32
BF16 = jnp.bfloat16
STEPS = 4
ROWS = 24
ALL = STEPS * ROWS
LOCAL = 512
STATE = 128
GROUP_WIDTH = 2048
CHUNKS = 3
CHUNK_ROWS = ROWS // CHUNKS
SENT_ROWS = STEPS * CHUNK_ROWS
HEADS = 8
CONTRACT_LAST = (((1,), (1,)), ((), ()))
CONTRACT_FIRST = (((0,), (0,)), ((), ()))


def split3(value):
    first = value.astype(BF16)
    rest = value - first.astype(F32)
    second = rest.astype(BF16)
    third = (rest - second.astype(F32)).astype(BF16)
    return first, second, third


def expand_heads(value, spread):
    parts = split3(value)
    total = jnp.dot(parts[2], spread, preferred_element_type=F32)
    total = total + jnp.dot(parts[1], spread, preferred_element_type=F32)
    return total + jnp.dot(parts[0], spread, preferred_element_type=F32)


def put(ref, first, value):
    for j in range(value.shape[1] // 128):
        ref[j, first:first + value.shape[0], :] = value[:, j * 128:(j + 1) * 128]


def pick_rows(ref, row, count):
    return jnp.concatenate(
        [ref[j, pl.ds(row, count, stride=ROWS), :] for j in range(ref.shape[0])], axis=1
    )


UNROLL = 4
OFFSETS = ((2, 0), (0, 1), (1, 0), (3, 1), (3, 0), (1, 1), (2, 1), (0, 0))
GATHER = ((0, 1), (0, 3), (0, 2), (1, 0), (1, 1), (1, 3), (1, 2))
OWN_PLANE = (0, 1, 2, 3)
OTHER_PLANE = (4, 5, 6)


def mix_kernel(
    codes_ref, exps_ref, old_ref, state_ref, x_ref, z_ref, b_ref, c_ref, dt_ref,
    bias_ref, rate_ref, skip_ref, gain_ref,
    held, sums, squares,
    exps, xs_in, zs_in, bs_in, cs_in, dts_in, bias_in, rate_in, skip_in, gain_in,
    left_rows, right_rows, read_rows, read_state, decay_rows, direct_rows, square_rows,
    codes, delta, weight, arrived, acts, parts, own_square, near_squares,
    small_sem, state_sem, codes_sem, own_sem, old_send, old_recv, delta_send, delta_recv,
    act_send, act_recv, fwd_send, fwd_recv, part_send, part_recv, square_send, square_recv,
):
    grp, tp = lax.axis_index("grp"), lax.axis_index("tp")
    z_lo, x = grp // 4, grp % 4
    y, z_hi, core = tp // 4, (tp // 2) % 2, tp % 2
    other = 1 - core
    chip = tp // 2
    partner = (grp, tp - core + other)
    mine = chip == grp
    crossed = chip == (1 - z_lo) * 4 + x

    def place(lo, xx, yy, hi, cc):
        return (lo * 4 + xx, yy * 4 + hi * 2 + cc)

    for k in range(8):
        dy, dz = OFFSETS[k]
        column = ((y + dy) % 4) * 2 + (z_hi + dz) % 2
        pltpu.make_async_copy(
            codes_ref.at[:, pl.ds(pl.multiple_of(column * 1024, 1024), 1024)], codes.at[k], codes_sem.at[k]
        ).start()

    small = [
        (exps_ref, exps), (dt_ref, dts_in), (bias_ref, bias_in), (rate_ref, rate_in), (skip_ref, skip_in),
        (x_ref, xs_in), (b_ref, bs_in), (c_ref, cs_in), (z_ref, zs_in), (gain_ref, gain_in),
    ]

    def small_copy(k):
        return pltpu.make_async_copy(small[k][0], small[k][1], small_sem.at[k])

    def state_copy(c):
        span = pl.ds(c * CHUNK_ROWS, CHUNK_ROWS)
        return pltpu.make_async_copy(state_ref.at[span], held.at[span], state_sem.at[c])

    for k in range(len(small)):
        small_copy(k).start()
    for c in range(CHUNKS):
        state_copy(c).start()

    barrier = pltpu.get_barrier_semaphore()

    def greet(where):
        pl.semaphore_signal(barrier, inc=1, device_id=where, device_id_type=MESH)

    greet(partner)
    for cc in range(2):
        for yl in range(2):
            for dz in range(2):
                where = place((z_lo + dz) % 2, x, 2 * core + yl, (z_hi + dz) % 2, cc)
                if dz == 0:
                    @pl.when(jnp.logical_not((cc == core) & (2 * core + yl == y)))
                    def _():
                        greet(where)
                else:
                    greet(where)
    for dl, dx in GATHER[:6]:
        greet(((z_lo + dl) % 2 * 4 + (x + dx) % 4, tp))
    for cc in range(2):
        greet(place(z_lo, x, y, 1 - z_hi, (core + cc) % 2))
    for dy in range(1, 4):
        greet(place(z_lo, x, (y + dy) % 4, z_hi, core))
    for lo in range(2):
        for yy in range(4):
            for hi in range(2):
                where = place(lo, chip % 4, yy, hi, core)

                @pl.when(jnp.logical_not((where[0] == grp) & (where[1] == tp)))
                def _():
                    greet(where)
    own_delta = core == y // 2
    expected = (
        1 + 8 - own_delta.astype(jnp.int32) + 6 + 2 + 3 + 16 - mine.astype(jnp.int32) - crossed.astype(jnp.int32)
    )
    own_lanes = pl.ds(pl.multiple_of(core * LOCAL, LOCAL), LOCAL)

    def act_copy(c, k):
        dl, dx = GATHER[k]
        slot, where = grp, ((z_lo + dl) % 2 * 4 + (x + dx) % 4, tp)
        if k == 6:
            slot, where = z_lo * 4 + (x + 2) % 4, ((z_lo + 1) % 2 * 4 + x, tp)
        piece = acts.at[slot, pl.ds(c * SENT_ROWS, SENT_ROWS), own_lanes]
        return pltpu.make_async_remote_copy(
            src_ref=piece, dst_ref=piece,
            send_sem=act_send.at[c * 7 + k], recv_sem=act_recv.at[c * 7 + k],
            device_id=where, device_id_type=MESH,
        )

    def fwd_copy(c, k):
        slot = grp
        if k < 7:
            dl, dx = GATHER[k]
            slot = (z_lo + dl) % 2 * 4 + (x + 4 - dx) % 4
        piece = acts.at[slot, pl.ds(c * SENT_ROWS, SENT_ROWS), own_lanes]
        return pltpu.make_async_remote_copy(
            src_ref=piece, dst_ref=piece,
            send_sem=fwd_send.at[c * 8 + k], recv_sem=fwd_recv.at[c * 8 + k],
            device_id=partner, device_id_type=MESH,
        )

    def square_copy(k):
        if k < 3:
            other_chip, other_core = ((0, 1), (1, 0), (1, 1))[k]
            where = place(z_lo, x, y, (z_hi + other_chip) % 2, (core + other_core) % 2)
            source, target = own_square, near_squares.at[k]
        else:
            where = place(z_lo, x, (y + k - 2) % 4, z_hi, core)
            source = target = squares.at[y]
        return pltpu.make_async_remote_copy(
            src_ref=source, dst_ref=target,
            send_sem=square_send.at[k], recv_sem=square_recv.at[k],
            device_id=where, device_id_type=MESH,
        )

    def feature_row(slab, cc):
        dz, yl = slab // 2, slab % 2
        lo, hi = (z_lo + dz) % 2, (z_hi + dz) % 2
        row = ((lo * 4 + x) * 2 + cc) * 512 + yl * 256 + hi * 128
        return pl.ds(pl.multiple_of(row, 128), 128)

    def own_copy(slab):
        return pltpu.make_async_copy(
            old_ref.at[feature_row(slab, core)],
            weight.at[pl.ds(slab * 128, 128), pl.ds(pl.multiple_of(core * LOCAL, LOCAL), LOCAL)],
            own_sem.at[slab],
        )

    def old_copy(slab):
        return pltpu.make_async_remote_copy(
            src_ref=old_ref.at[feature_row(slab, other)],
            dst_ref=weight.at[pl.ds(slab * 128, 128), pl.ds(pl.multiple_of(core * LOCAL, LOCAL), LOCAL)],
            send_sem=old_send.at[slab], recv_sem=old_recv.at[slab],
            device_id=partner, device_id_type=MESH,
        )

    def delta_copy(k, half):
        dy, dz = OFFSETS[k]
        slot = half * 8 + dz * 4 + (y % 2) * 2 + core
        return pltpu.make_async_remote_copy(
            src_ref=delta.at[k, pl.ds(half * 32, 32)], dst_ref=arrived.at[pl.ds(pl.multiple_of(slot * 32, 32), 32)],
            send_sem=delta_send.at[half * 8 + k], recv_sem=delta_recv.at[slot],
            device_id=place((z_lo + dz) % 2, x, (y + dy) % 4, (z_hi + dz) % 2, y // 2), device_id_type=MESH,
        )

    def delta_self(half):
        slot = half * 8 + (y % 2) * 2 + core
        return pltpu.make_async_copy(
            delta.at[7, pl.ds(half * 32, 32)], arrived.at[pl.ds(pl.multiple_of(slot * 32, 32), 32)],
            delta_recv.at[slot],
        )

    small_copy(0).wait()
    scale = jnp.where(
        exps[...] == -14, 2.0**-14, jnp.where(exps[...] == -13, 2.0**-13, 2.0**-12)
    ).astype(BF16)
    block_at = lax.broadcasted_iota(jnp.int32, (64, 1024), 0)
    lane_block = lax.broadcasted_iota(jnp.int32, (64, 1024), 1) // 128
    for k in range(8):
        dy, dz = OFFSETS[k]
        column = ((y + dy) % 4) * 2 + (z_hi + dz) % 2
        pltpu.make_async_copy(codes.at[k], codes.at[k], codes_sem.at[k]).wait()
        pick = (block_at == lane_block + column * 8).astype(BF16)
        wide = jnp.dot(scale, pick, preferred_element_type=F32)
        delta[k] = (codes[k].astype(F32) * wide).astype(BF16)
        if k == 1:
            pl.semaphore_wait(barrier, expected)
            delta_copy(0, 0).start()
        if 1 <= k < 7:
            delta_copy(k, 0).start()

    @pl.when(own_delta)
    def _():
        for half in range(2):
            delta_self(half).start()

    @pl.when(jnp.logical_not(own_delta))
    def _():
        for half in range(2):
            delta_copy(7, half).start()

    for k in range(7):
        delta_copy(k, 1).start()
    for slab in range(4):
        own_copy(slab).start()
        old_copy(slab).start()

    for k in range(1, len(small)):
        small_copy(k).wait()
    group = tp // 4
    group_lanes = pl.ds(pl.multiple_of(group * STATE, STATE), STATE)
    head_of = lax.broadcasted_iota(jnp.int32, (HEADS, LOCAL), 1) // (LOCAL // HEADS)
    spread = (head_of == lax.broadcasted_iota(jnp.int32, (HEADS, LOCAL), 0)).astype(BF16)
    bias = expand_heads(jnp.broadcast_to(bias_in[...], (8, HEADS)), spread)[0:1]
    rate = expand_heads(jnp.broadcast_to(rate_in[...], (8, HEADS)), spread)[0:1]
    skip = expand_heads(jnp.broadcast_to(skip_in[...], (8, HEADS)), spread)[0:1]
    sizes, logs = [], []
    for s in range(STEPS):
        raw = lax.dot_general(dts_in[s], spread, CONTRACT_FIRST, preferred_element_type=F32) + bias
        sizes.append(jnp.maximum(raw, 0.0) + jnp.log1p(jnp.exp(-jnp.abs(raw))))
        own = sizes[s] * rate
        logs.append(own if s == 0 else logs[-1] + own)
    xs = [xs_in[s].astype(F32) for s in range(STEPS)]
    bs = [bs_in[s, :, group_lanes].astype(F32) for s in range(STEPS)]
    cs = [cs_in[s, :, group_lanes].astype(F32) for s in range(STEPS)]
    right_rows[...] = jnp.zeros(right_rows.shape, F32)
    read_rows[...] = jnp.zeros(read_rows.shape, F32)
    for s in range(STEPS):
        right_rows[0, s * ROWS:(s + 1) * ROWS, :] = bs[s]
        right_rows[0, (4 + s) * ROWS:(5 + s) * ROWS, :] = bs[s]
        read_rows[0, s * ROWS:(s + 1) * ROWS, :] = cs[s]
    right_rows[1, 8 * ROWS:11 * ROWS, :] = jnp.ones((3 * ROWS, STATE), F32)
    for s in range(STEPS):
        decay_rows[s * ROWS:(s + 1) * ROWS, :] = jnp.exp(-logs[s])
        direct = skip * xs[s]
        for u in range(s + 1):
            coef = sizes[u] if u == s else sizes[u] * jnp.exp(logs[u] - logs[s])
            term = coef * xs[u]
            direct = direct + term * jnp.sum(bs[u] * cs[s], axis=1, keepdims=True)
            if s == STEPS - 1:
                high = term.astype(BF16).astype(F32)
                put(left_rows, u * ROWS, high)
                put(left_rows, (4 + u) * ROWS, term - high)
        direct_rows[s * ROWS:(s + 1) * ROWS, :] = direct
    last = decay_rows[3 * ROWS:4 * ROWS, :]
    for at_row, part in enumerate(split3(last)):
        put(left_rows, (8 + at_row) * ROWS, part.astype(F32))
    put(left_rows, 11 * ROWS, jnp.zeros((5 * ROWS, LOCAL), F32))
    square_rows[ALL:, :] = jnp.zeros((128 - ALL, 128), F32)

    def read_one(row):
        value = held[row].reshape(LOCAL, STATE)
        high = value.astype(BF16)
        low = (value - high.astype(F32)).astype(BF16)
        both = jnp.concatenate([high, low], axis=1)
        reader = pick_rows(read_rows, row, 8).astype(BF16)
        reader = jnp.concatenate([reader, reader], axis=1)
        read = lax.dot_general(reader, both, CONTRACT_LAST, preferred_element_type=F32)
        for j in range(LOCAL // 128):
            read_state[j, pl.ds(row, 8, stride=ROWS), :] = read[:, j * 128:(j + 1) * 128]

    def update_one(row):
        left = pick_rows(left_rows, row, 16).astype(BF16)
        right = pick_rows(right_rows, row, 16).astype(BF16)
        update = lax.dot_general(left, right, CONTRACT_FIRST, preferred_element_type=F32)
        value = held[row].reshape(LOCAL, STATE)
        held[row] = (update[:, STATE:] * value + update[:, :STATE]).reshape(held.shape[1:])

    def over_rows(first, count, unroll, one):
        def some(i, carry):
            for j in range(unroll):
                one(first + i * unroll + j)
            return carry

        lax.fori_loop(0, count // unroll, some, 0)

    for c in range(CHUNKS):
        state_copy(c).wait()
        over_rows(c * CHUNK_ROWS, CHUNK_ROWS, UNROLL, read_one)
        pieces = []
        for s in range(STEPS):
            span = slice(s * ROWS + c * CHUNK_ROWS, s * ROWS + (c + 1) * CHUNK_ROWS)
            read = jnp.concatenate([read_state[j, span, :] for j in range(LOCAL // 128)], axis=1)
            z = zs_in[s].astype(F32)[c * CHUNK_ROWS:(c + 1) * CHUNK_ROWS]
            read_out = decay_rows[span, :] * read + direct_rows[span, :]
            pieces.append(read_out * (z / (1.0 + jnp.exp(-z))))
        gated = jnp.concatenate(pieces, axis=0)
        acts[grp, c * SENT_ROWS:(c + 1) * SENT_ROWS, own_lanes] = (gated * gain_in[...]).astype(BF16)
        for k in OWN_PLANE:
            act_copy(c, k).start()
        fwd_copy(c, 7).start()
        total = jnp.sum(gated * gated, axis=1, keepdims=True)
        square_rows[c * SENT_ROWS:(c + 1) * SENT_ROWS, :] = jnp.broadcast_to(total, (SENT_ROWS, 128))
    for c in range(CHUNKS):
        for k in (4, 5):
            act_copy(c, k).start()
    own_square[...] = jnp.transpose(square_rows[...])[0:8]
    for k in range(3):
        square_copy(k).start()

    for c in range(CHUNKS):
        over_rows(c * CHUNK_ROWS, CHUNK_ROWS, UNROLL, update_one)
        for k in OWN_PLANE:
            act_copy(c, k).wait_recv()
            fwd_copy(c, k).start()
            if k == 2:
                act_copy(c, 6).start()
    for k in range(3):
        square_copy(k).wait_recv()
    squares[y] = own_square[...] + near_squares[0] + near_squares[1] + near_squares[2]
    for k in range(3, 6):
        square_copy(k).start()

    def part_copy(half, plane, dz, i):
        g = (z_lo + plane) % 2 * 4 + i
        dest = (g, ((z_lo + dz) % 2 * 4 + x) * 2 + core)
        at = ((half * 2 + plane) * 2 + dz) * 4 + i
        slot = (half * 2 + (z_hi + dz) % 2) * 8 + y * 2 + dz
        remote = lambda: pltpu.make_async_remote_copy(
            src_ref=parts.at[at], dst_ref=sums.at[slot],
            send_sem=part_send.at[at], recv_sem=part_recv.at[slot],
            device_id=dest, device_id_type=MESH,
        )
        local = lambda: pltpu.make_async_copy(parts.at[at], sums.at[slot], part_recv.at[slot])
        here = (dest[0] == grp) & (dest[1] == tp)
        return at, remote, local, here

    for slab in range(4):
        own_copy(slab).wait()
        old_copy(slab).wait_recv()
    for half in range(2):
        for slot in range(half * 8, half * 8 + 8):
            rows = arrived.at[pl.ds(slot * 32, 32)]
            pltpu.make_async_copy(rows, rows, delta_recv.at[slot]).wait()
        fresh = []
        for q in range(8):
            first = q * 64 + half * 32
            coming = half * 256 + q * 32
            fresh.append(
                (weight[first:first + 32, :].astype(F32) + arrived[coming:coming + 32, :].astype(F32)).astype(BF16)
            )
        fresh = jnp.concatenate(fresh, axis=0)
        for plane in range(2):
            if half == 0:
                if plane == 1:
                    for c in range(CHUNKS):
                        for k in OTHER_PLANE:
                            act_copy(c, k).wait_recv()
                            fwd_copy(c, k).start()
                for c in range(CHUNKS):
                    for k in ((7, 0, 1, 2), (3, 4, 5, 6))[plane]:
                        fwd_copy(c, k).wait_recv()
            for pair in range(2):
                start = (z_lo + plane) % 2 * 4 + pair * 2
                lhs = acts[pl.ds(start, 2)].reshape(2 * ALL, 1024)
                got = lax.dot_general(lhs, fresh, CONTRACT_LAST, preferred_element_type=F32)
                for part in range(2):
                    for dz in range(2):
                        at, remote, local, here = part_copy(half, plane, dz, pair * 2 + part)
                        parts[at] = got[part * ALL:(part + 1) * ALL, dz * 128:dz * 128 + 128].astype(BF16)

                        @pl.when(here)
                        def _():
                            local().start()

                        @pl.when(jnp.logical_not(here))
                        def _():
                            remote().start()

    for k in range(3, 6):
        square_copy(k).wait_recv()
    for slot in range(32):
        pltpu.make_async_copy(sums.at[slot], sums.at[slot], part_recv.at[slot]).wait()

    for k in range(7):
        for half in range(2):
            delta_copy(k, half).wait_send()
    for c in range(CHUNKS):
        for k in range(7):
            act_copy(c, k).wait_send()
        for k in range(8):
            fwd_copy(c, k).wait_send()

    @pl.when(jnp.logical_not(own_delta))
    def _():
        for half in range(2):
            delta_copy(7, half).wait_send()
    for slab in range(4):
        old_copy(slab).wait_send()
    for k in range(6):
        square_copy(k).wait_send()
    for half in range(2):
        for plane in range(2):
            for dz in range(2):
                for i in range(4):
                    _, remote, _, here = part_copy(half, plane, dz, i)

                    @pl.when(jnp.logical_not(here))
                    def _():
                        remote().wait_send()


def finish_kernel(held, sums, squares, out_ref, final_ref, sem):
    copies = [
        pltpu.make_async_copy(held.at[pl.ds(c * 6, 6)], final_ref.at[pl.ds(c * 6, 6)], sem.at[c])
        for c in range(4)
    ]
    for copy in copies:
        copy.start()
    factors = []
    for yy in range(4):
        inverse = lax.rsqrt(squares[yy] * (1.0 / GROUP_WIDTH) + 1e-05)
        factors.append(jnp.transpose(jnp.concatenate([inverse] * 16, axis=0))[0:ALL, 0:1])
    lane = lax.broadcasted_iota(jnp.int32, (256, 256), 1)
    source = (lane // 32) % 2 * 128 + lane // 128 * 64 + (lane // 64) % 2 * 32 + lane % 32
    order = (lax.broadcasted_iota(jnp.int32, (256, 256), 0) == source).astype(BF16)
    for hi in range(2):
        totals = []
        for half in range(2):
            total = None
            for yy in range(4):
                slot = (half * 2 + hi) * 8 + yy * 2
                pair = (sums[slot].astype(F32) + sums[slot + 1].astype(F32)) * factors[yy]
                total = pair if total is None else total + pair
            totals.append(total.astype(BF16))
        total = jnp.dot(jnp.concatenate(totals, axis=1), order, preferred_element_type=F32)
        for s in range(STEPS):
            rows = jnp.concatenate(
                [
                    total[c * SENT_ROWS + s * CHUNK_ROWS:c * SENT_ROWS + (s + 1) * CHUNK_ROWS]
                    for c in range(CHUNKS)
                ],
                axis=0,
            ).astype(BF16)
            for yl in range(2):
                at = yl * 256 + hi * 128
                out_ref[s, :, at:at + 128] = rows[:, yl * 128:(yl + 1) * 128]
    for copy in copies:
        copy.wait()


def local(
    old_weight, delta_codes, delta_exps, state_in, x_in, z_in, b_in, c_in, dt_in,
    dt_bias, a_rate, skip_gain, norm_gain,
):
    vmem = pl.BlockSpec(memory_space=pltpu.VMEM)
    hbm = pl.BlockSpec(memory_space=pltpu.HBM)
    dma = pltpu.SemaphoreType.DMA
    vectors = [v.reshape(1, -1) for v in (dt_bias, a_rate, skip_gain, norm_gain)]
    held, sums, squares = pl.pallas_call(
        mix_kernel,
        out_shape=(
            pltpu.VMEM(state_in.shape, F32),
            pltpu.VMEM((32, ALL, 128), BF16),
            pltpu.VMEM((4, 8, 128), F32),
        ),
        in_specs=[hbm] * 13,
        out_specs=(vmem, vmem, vmem),
        scratch_shapes=[
            pltpu.VMEM((64, 64), jnp.int32),
            pltpu.VMEM(x_in.shape, BF16),
            pltpu.VMEM(x_in.shape, BF16),
            pltpu.VMEM(b_in.shape, BF16),
            pltpu.VMEM(b_in.shape, BF16),
            pltpu.VMEM((STEPS, HEADS, ROWS), BF16),
            pltpu.VMEM((1, HEADS), F32),
            pltpu.VMEM((1, HEADS), F32),
            pltpu.VMEM((1, HEADS), F32),
            pltpu.VMEM((1, LOCAL), F32),
            pltpu.VMEM((LOCAL // 128, 16 * ROWS, 128), F32),
            pltpu.VMEM((2, 16 * ROWS, STATE), F32),
            pltpu.VMEM((1, 8 * ROWS, STATE), F32),
            pltpu.VMEM((LOCAL // 128, 8 * ROWS, 128), F32),
            pltpu.VMEM((ALL, LOCAL), F32),
            pltpu.VMEM((ALL, LOCAL), F32),
            pltpu.VMEM((128, 128), F32),
            pltpu.VMEM((8, 64, 1024), jnp.int32),
            pltpu.VMEM((8, 64, 1024), BF16),
            pltpu.VMEM((512, 1024), BF16),
            pltpu.VMEM((512, 1024), BF16),
            pltpu.VMEM((8, ALL, 1024), BF16),
            pltpu.VMEM((32, ALL, 128), BF16),
            pltpu.VMEM((8, 128), F32),
            pltpu.VMEM((3, 8, 128), F32),
            dma((10,)), dma((CHUNKS,)), dma((8,)), dma((4,)), dma((4,)), dma((4,)), dma((16,)), dma((16,)),
            dma((7 * CHUNKS,)), dma((7 * CHUNKS,)), dma((8 * CHUNKS,)), dma((8 * CHUNKS,)),
            dma((32,)), dma((32,)), dma((6,)), dma((6,)),
        ],
        compiler_params=pltpu.CompilerParams(
            collective_id=0, has_side_effects=True, vmem_limit_bytes=36 * 1024 * 1024
        ),
        cost_estimate=pl.CostEstimate(flops=9 * 10**8, bytes_accessed=10**7, transcendentals=0),
    )(
        *[
            pltpu.with_memory_space_constraint(a, pltpu.HBM)
            for a in (
                delta_codes, delta_exps, old_weight, state_in, x_in, z_in, b_in, c_in,
                jnp.swapaxes(dt_in, 1, 2), *vectors,
            )
        ]
    )
    mixed, final_state = pl.pallas_call(
        finish_kernel,
        out_shape=(
            jax.ShapeDtypeStruct((STEPS, ROWS, LOCAL), BF16),
            jax.ShapeDtypeStruct(state_in.shape, F32),
        ),
        in_specs=[vmem] * 3,
        out_specs=(vmem, hbm),
        scratch_shapes=[dma((4,))],
        compiler_params=pltpu.CompilerParams(vmem_limit_bytes=36 * 1024 * 1024),
        cost_estimate=pl.CostEstimate(flops=10**6, bytes_accessed=7 * 10**6, transcendentals=0),
    )(held, sums, squares)
    return mixed, final_state


def solution(mesh):
    return jax.shard_map(
        local,
        mesh=mesh,
        in_specs=(
            P(None, "tp"),
            P(("grp", "tp"), None),
            P(("grp", "tp"), None),
            P("grp", "tp", None, None),
            P(None, "grp", "tp"),
            P(None, "grp", "tp"),
            P(None, "grp", None),
            P(None, "grp", None),
            P(None, "grp", "tp"),
            P("tp"),
            P("tp"),
            P("tp"),
            P("tp"),
        ),
        out_specs=(P(None, "grp", "tp"), P("grp", "tp", None, None)),
        check_vma=False,
    )
```

```python
import functools

import jax
import jax.numpy as jnp
from jax import lax
from jax.experimental import pallas as pl
from jax.experimental.pallas import tpu as pltpu
from jax.sharding import PartitionSpec as P

MESH = pl.DeviceIdType.MESH
F32 = jnp.float32
BF16 = jnp.bfloat16
STEPS = 4
ROWS = 24
ALL = STEPS * ROWS
LOCAL = 512
STATE = 128
GROUP_WIDTH = 2048
CHUNKS = 3
CHUNK_ROWS = ROWS // CHUNKS
SENT_ROWS = STEPS * CHUNK_ROWS
HEADS = 8
CONTRACT_LAST = (((1,), (1,)), ((), ()))
CONTRACT_FIRST = (((0,), (0,)), ((), ()))


def split3(value):
    first = value.astype(BF16)
    rest = value - first.astype(F32)
    second = rest.astype(BF16)
    third = (rest - second.astype(F32)).astype(BF16)
    return first, second, third


def expand_heads(value, spread):
    parts = split3(value)
    total = jnp.dot(parts[2], spread, preferred_element_type=F32)
    total = total + jnp.dot(parts[1], spread, preferred_element_type=F32)
    return total + jnp.dot(parts[0], spread, preferred_element_type=F32)


def put(ref, first, value):
    for j in range(value.shape[1] // 128):
        ref[j, first:first + value.shape[0], :] = value[:, j * 128:(j + 1) * 128]


def pick_rows(ref, row, count):
    return jnp.concatenate(
        [ref[j, pl.ds(row, count, stride=ROWS), :] for j in range(ref.shape[0])], axis=1
    )


UNROLL = 4
OFFSETS = ((2, 0), (0, 1), (1, 0), (3, 1), (3, 0), (1, 1), (2, 1), (0, 0))
GATHER = ((0, 1), (0, 3), (0, 2), (1, 0), (1, 1), (1, 3), (1, 2))
OWN_PLANE = (0, 1, 2, 3)
OTHER_PLANE = (4, 5, 6)


def mix_kernel(
    codes_ref, exps_ref, old_ref, state_ref, x_ref, z_ref, b_ref, c_ref, dt_ref,
    bias_ref, rate_ref, skip_ref, gain_ref,
    held, sums, squares,
    exps, xs_in, zs_in, bs_in, cs_in, dts_in, bias_in, rate_in, skip_in, gain_in,
    left_rows, right_rows, read_rows, read_state, decay_rows, direct_rows, square_rows,
    codes, delta, weight, arrived, acts, parts, own_square, near_squares,
    small_sem, state_sem, codes_sem, own_sem, old_send, old_recv, delta_send, delta_recv,
    act_send, act_recv, fwd_send, fwd_recv, part_send, part_recv, square_send, square_recv,
):
    grp, tp = lax.axis_index("grp"), lax.axis_index("tp")
    z_lo, x = grp // 4, grp % 4
    y, z_hi, core = tp // 4, (tp // 2) % 2, tp % 2
    other = 1 - core
    chip = tp // 2
    partner = (grp, tp - core + other)
    mine = chip == grp
    crossed = chip == (1 - z_lo) * 4 + x

    def place(lo, xx, yy, hi, cc):
        return (lo * 4 + xx, yy * 4 + hi * 2 + cc)

    for k in range(8):
        dy, dz = OFFSETS[k]
        column = ((y + dy) % 4) * 2 + (z_hi + dz) % 2
        pltpu.make_async_copy(
            codes_ref.at[:, pl.ds(pl.multiple_of(column * 1024, 1024), 1024)], codes.at[k], codes_sem.at[k]
        ).start()

    small = [
        (exps_ref, exps), (dt_ref, dts_in), (bias_ref, bias_in), (rate_ref, rate_in), (skip_ref, skip_in),
        (x_ref, xs_in), (b_ref, bs_in), (c_ref, cs_in), (z_ref, zs_in), (gain_ref, gain_in),
    ]

    def small_copy(k):
        return pltpu.make_async_copy(small[k][0], small[k][1], small_sem.at[k])

    def state_copy(c):
        span = pl.ds(c * CHUNK_ROWS, CHUNK_ROWS)
        return pltpu.make_async_copy(state_ref.at[span], held.at[span], state_sem.at[c])

    for k in range(len(small)):
        small_copy(k).start()

    barrier = pltpu.get_barrier_semaphore()

    def greet(where):
        pl.semaphore_signal(barrier, inc=1, device_id=where, device_id_type=MESH)

    greet(partner)
    for cc in range(2):
        for yl in range(2):
            for dz in range(2):
                where = place((z_lo + dz) % 2, x, 2 * core + yl, (z_hi + dz) % 2, cc)
                if dz == 0:
                    @pl.when(jnp.logical_not((cc == core) & (2 * core + yl == y)))
                    def _():
                        greet(where)
                else:
                    greet(where)
    for dl, dx in GATHER[:6]:
        greet(((z_lo + dl) % 2 * 4 + (x + dx) % 4, tp))
    for cc in range(2):
        greet(place(z_lo, x, y, 1 - z_hi, (core + cc) % 2))
    for dy in range(1, 4):
        greet(place(z_lo, x, (y + dy) % 4, z_hi, core))
    for lo in range(2):
        for yy in range(4):
            for hi in range(2):
                where = place(lo, chip % 4, yy, hi, core)

                @pl.when(jnp.logical_not((where[0] == grp) & (where[1] == tp)))
                def _():
                    greet(where)
    own_delta = core == y // 2
    expected = (
        1 + 8 - own_delta.astype(jnp.int32) + 6 + 2 + 3 + 16 - mine.astype(jnp.int32) - crossed.astype(jnp.int32)
    )
    own_lanes = pl.ds(pl.multiple_of(core * LOCAL, LOCAL), LOCAL)

    def act_copy(c, k):
        dl, dx = GATHER[k]
        slot, where = grp, ((z_lo + dl) % 2 * 4 + (x + dx) % 4, tp)
        if k == 6:
            slot, where = z_lo * 4 + (x + 2) % 4, ((z_lo + 1) % 2 * 4 + x, tp)
        piece = acts.at[slot, pl.ds(c * SENT_ROWS, SENT_ROWS), own_lanes]
        return pltpu.make_async_remote_copy(
            src_ref=piece, dst_ref=piece,
            send_sem=act_send.at[c * 7 + k], recv_sem=act_recv.at[c * 7 + k],
            device_id=where, device_id_type=MESH,
        )

    def fwd_copy(c, k):
        slot = grp
        if k < 7:
            dl, dx = GATHER[k]
            slot = (z_lo + dl) % 2 * 4 + (x + 4 - dx) % 4
        piece = acts.at[slot, pl.ds(c * SENT_ROWS, SENT_ROWS), own_lanes]
        return pltpu.make_async_remote_copy(
            src_ref=piece, dst_ref=piece,
            send_sem=fwd_send.at[c * 8 + k], recv_sem=fwd_recv.at[c * 8 + k],
            device_id=partner, device_id_type=MESH,
        )

    def square_copy(k):
        if k < 3:
            other_chip, other_core = ((0, 1), (1, 0), (1, 1))[k]
            where = place(z_lo, x, y, (z_hi + other_chip) % 2, (core + other_core) % 2)
            source, target = own_square, near_squares.at[k]
        else:
            where = place(z_lo, x, (y + k - 2) % 4, z_hi, core)
            source = target = squares.at[y]
        return pltpu.make_async_remote_copy(
            src_ref=source, dst_ref=target,
            send_sem=square_send.at[k], recv_sem=square_recv.at[k],
            device_id=where, device_id_type=MESH,
        )

    def feature_row(slab, cc):
        dz, yl = slab // 2, slab % 2
        lo, hi = (z_lo + dz) % 2, (z_hi + dz) % 2
        row = ((lo * 4 + x) * 2 + cc) * 512 + yl * 256 + hi * 128
        return pl.ds(pl.multiple_of(row, 128), 128)

    def own_copy(slab):
        return pltpu.make_async_copy(
            old_ref.at[feature_row(slab, core)],
            weight.at[pl.ds(slab * 128, 128), pl.ds(pl.multiple_of(core * LOCAL, LOCAL), LOCAL)],
            own_sem.at[slab],
        )

    def old_copy(slab):
        return pltpu.make_async_remote_copy(
            src_ref=old_ref.at[feature_row(slab, other)],
            dst_ref=weight.at[pl.ds(slab * 128, 128), pl.ds(pl.multiple_of(core * LOCAL, LOCAL), LOCAL)],
            send_sem=old_send.at[slab], recv_sem=old_recv.at[slab],
            device_id=partner, device_id_type=MESH,
        )

    def delta_copy(k, half):
        dy, dz = OFFSETS[k]
        slot = half * 8 + dz * 4 + (y % 2) * 2 + core
        return pltpu.make_async_remote_copy(
            src_ref=delta.at[k, pl.ds(half * 32, 32)], dst_ref=arrived.at[pl.ds(pl.multiple_of(slot * 32, 32), 32)],
            send_sem=delta_send.at[half * 8 + k], recv_sem=delta_recv.at[slot],
            device_id=place((z_lo + dz) % 2, x, (y + dy) % 4, (z_hi + dz) % 2, y // 2), device_id_type=MESH,
        )

    def delta_self(half):
        slot = half * 8 + (y % 2) * 2 + core
        return pltpu.make_async_copy(
            delta.at[7, pl.ds(half * 32, 32)], arrived.at[pl.ds(pl.multiple_of(slot * 32, 32), 32)],
            delta_recv.at[slot],
        )

    small_copy(0).wait()
    scale = jnp.where(
        exps[...] == -14, 2.0**-14, jnp.where(exps[...] == -13, 2.0**-13, 2.0**-12)
    ).astype(BF16)
    block_at = lax.broadcasted_iota(jnp.int32, (64, 1024), 0)
    lane_block = lax.broadcasted_iota(jnp.int32, (64, 1024), 1) // 128
    for k in range(8):
        dy, dz = OFFSETS[k]
        column = ((y + dy) % 4) * 2 + (z_hi + dz) % 2
        pltpu.make_async_copy(codes.at[k], codes.at[k], codes_sem.at[k]).wait()
        if k == 3:
            for c in range(CHUNKS):
                state_copy(c).start()
        pick = (block_at == lane_block + column * 8).astype(BF16)
        wide = jnp.dot(scale, pick, preferred_element_type=F32)
        delta[k] = (codes[k].astype(F32) * wide).astype(BF16)

    for k in range(1, len(small)):
        small_copy(k).wait()
    group = tp // 4
    group_lanes = pl.ds(pl.multiple_of(group * STATE, STATE), STATE)
    head_of = lax.broadcasted_iota(jnp.int32, (HEADS, LOCAL), 1) // (LOCAL // HEADS)
    spread = (head_of == lax.broadcasted_iota(jnp.int32, (HEADS, LOCAL), 0)).astype(BF16)
    bias = expand_heads(jnp.broadcast_to(bias_in[...], (8, HEADS)), spread)[0:1]
    rate = expand_heads(jnp.broadcast_to(rate_in[...], (8, HEADS)), spread)[0:1]
    skip = expand_heads(jnp.broadcast_to(skip_in[...], (8, HEADS)), spread)[0:1]
    sizes, logs = [], []
    for s in range(STEPS):
        raw = lax.dot_general(dts_in[s], spread, CONTRACT_FIRST, preferred_element_type=F32) + bias
        sizes.append(jnp.maximum(raw, 0.0) + jnp.log1p(jnp.exp(-jnp.abs(raw))))
        own = sizes[s] * rate
        logs.append(own if s == 0 else logs[-1] + own)
    xs = [xs_in[s].astype(F32) for s in range(STEPS)]
    bs = [bs_in[s, :, group_lanes].astype(F32) for s in range(STEPS)]
    cs = [cs_in[s, :, group_lanes].astype(F32) for s in range(STEPS)]
    right_rows[...] = jnp.zeros(right_rows.shape, F32)
    read_rows[...] = jnp.zeros(read_rows.shape, F32)
    for s in range(STEPS):
        right_rows[0, s * ROWS:(s + 1) * ROWS, :] = bs[s]
        right_rows[0, (4 + s) * ROWS:(5 + s) * ROWS, :] = bs[s]
        read_rows[0, s * ROWS:(s + 1) * ROWS, :] = cs[s]
    right_rows[1, 8 * ROWS:11 * ROWS, :] = jnp.ones((3 * ROWS, STATE), F32)
    for s in range(STEPS):
        decay_rows[s * ROWS:(s + 1) * ROWS, :] = jnp.exp(-logs[s])
        direct = skip * xs[s]
        for u in range(s + 1):
            coef = sizes[u] if u == s else sizes[u] * jnp.exp(logs[u] - logs[s])
            term = coef * xs[u]
            direct = direct + term * jnp.sum(bs[u] * cs[s], axis=1, keepdims=True)
            if s == STEPS - 1:
                high = term.astype(BF16).astype(F32)
                put(left_rows, u * ROWS, high)
                put(left_rows, (4 + u) * ROWS, term - high)
        direct_rows[s * ROWS:(s + 1) * ROWS, :] = direct
    last = decay_rows[3 * ROWS:4 * ROWS, :]
    for at_row, part in enumerate(split3(last)):
        put(left_rows, (8 + at_row) * ROWS, part.astype(F32))
    put(left_rows, 11 * ROWS, jnp.zeros((5 * ROWS, LOCAL), F32))
    square_rows[ALL:, :] = jnp.zeros((128 - ALL, 128), F32)

    pl.semaphore_wait(barrier, expected)
    for k in range(7):
        delta_copy(k, 0).start()

    @pl.when(own_delta)
    def _():
        for half in range(2):
            delta_self(half).start()

    @pl.when(jnp.logical_not(own_delta))
    def _():
        for half in range(2):
            delta_copy(7, half).start()

    for k in range(7):
        delta_copy(k, 1).start()
    for slab in range(4):
        own_copy(slab).start()
        old_copy(slab).start()

    def read_one(row):
        value = held[row].reshape(LOCAL, STATE)
        high = value.astype(BF16)
        low = (value - high.astype(F32)).astype(BF16)
        both = jnp.concatenate([high, low], axis=1)
        reader = pick_rows(read_rows, row, 8).astype(BF16)
        reader = jnp.concatenate([reader, reader], axis=1)
        read = lax.dot_general(reader, both, CONTRACT_LAST, preferred_element_type=F32)
        for j in range(LOCAL // 128):
            read_state[j, pl.ds(row, 8, stride=ROWS), :] = read[:, j * 128:(j + 1) * 128]

    def update_one(row):
        left = pick_rows(left_rows, row, 16).astype(BF16)
        right = pick_rows(right_rows, row, 16).astype(BF16)
        update = lax.dot_general(left, right, CONTRACT_FIRST, preferred_element_type=F32)
        value = held[row].reshape(LOCAL, STATE)
        held[row] = (update[:, STATE:] * value + update[:, :STATE]).reshape(held.shape[1:])

    def over_rows(first, count, unroll, one):
        def some(i, carry):
            for j in range(unroll):
                one(first + i * unroll + j)
            return carry

        lax.fori_loop(0, count // unroll, some, 0)

    for c in range(CHUNKS):
        state_copy(c).wait()
        over_rows(c * CHUNK_ROWS, CHUNK_ROWS, UNROLL, read_one)
        pieces = []
        for s in range(STEPS):
            span = slice(s * ROWS + c * CHUNK_ROWS, s * ROWS + (c + 1) * CHUNK_ROWS)
            read = jnp.concatenate([read_state[j, span, :] for j in range(LOCAL // 128)], axis=1)
            z = zs_in[s].astype(F32)[c * CHUNK_ROWS:(c + 1) * CHUNK_ROWS]
            read_out = decay_rows[span, :] * read + direct_rows[span, :]
            pieces.append(read_out * (z / (1.0 + jnp.exp(-z))))
        gated = jnp.concatenate(pieces, axis=0)
        acts[grp, c * SENT_ROWS:(c + 1) * SENT_ROWS, own_lanes] = (gated * gain_in[...]).astype(BF16)
        for k in OWN_PLANE:
            act_copy(c, k).start()
        fwd_copy(c, 7).start()
        total = jnp.sum(gated * gated, axis=1, keepdims=True)
        square_rows[c * SENT_ROWS:(c + 1) * SENT_ROWS, :] = jnp.broadcast_to(total, (SENT_ROWS, 128))
    for c in range(CHUNKS):
        for k in (4, 5):
            act_copy(c, k).start()
    own_square[...] = jnp.transpose(square_rows[...])[0:8]
    for k in range(3):
        square_copy(k).start()

    for c in range(CHUNKS):
        over_rows(c * CHUNK_ROWS, CHUNK_ROWS, UNROLL, update_one)
        for k in OWN_PLANE:
            act_copy(c, k).wait_recv()
            fwd_copy(c, k).start()
            if k == 2:
                act_copy(c, 6).start()

    def part_copy(half, plane, dz, i):
        g = (z_lo + plane) % 2 * 4 + i
        dest = (g, ((z_lo + dz) % 2 * 4 + x) * 2 + core)
        at = ((half * 2 + plane) * 2 + dz) * 4 + i
        slot = (half * 2 + (z_hi + dz) % 2) * 8 + y * 2 + dz
        remote = lambda: pltpu.make_async_remote_copy(
            src_ref=parts.at[at], dst_ref=sums.at[slot],
            send_sem=part_send.at[at], recv_sem=part_recv.at[slot],
            device_id=dest, device_id_type=MESH,
        )
        local = lambda: pltpu.make_async_copy(parts.at[at], sums.at[slot], part_recv.at[slot])
        here = (dest[0] == grp) & (dest[1] == tp)
        return at, remote, local, here

    for slab in range(4):
        own_copy(slab).wait()
        old_copy(slab).wait_recv()
    for half in range(2):
        for slot in range(half * 8, half * 8 + 8):
            rows = arrived.at[pl.ds(slot * 32, 32)]
            pltpu.make_async_copy(rows, rows, delta_recv.at[slot]).wait()
        fresh = []
        for q in range(8):
            first = q * 64 + half * 32
            coming = half * 256 + q * 32
            fresh.append(
                (weight[first:first + 32, :].astype(F32) + arrived[coming:coming + 32, :].astype(F32)).astype(BF16)
            )
        fresh = jnp.concatenate(fresh, axis=0)
        for plane in range(2):
            if half == 0:
                if plane == 1:
                    for c in range(CHUNKS):
                        for k in OTHER_PLANE:
                            act_copy(c, k).wait_recv()
                            fwd_copy(c, k).start()
                for c in range(CHUNKS):
                    for k in ((7, 0, 1, 2), (3, 4, 5, 6))[plane]:
                        fwd_copy(c, k).wait_recv()
            for pair in range(1):
                start = (z_lo + plane) % 2 * 4
                lhs = acts[pl.ds(start, 4)].reshape(4 * ALL, 1024)
                got = lax.dot_general(lhs, fresh, CONTRACT_LAST, preferred_element_type=F32)
                for part in range(4):
                    for dz in range(2):
                        at, remote, local, here = part_copy(half, plane, dz, pair * 2 + part)
                        parts[at] = got[part * ALL:(part + 1) * ALL, dz * 128:dz * 128 + 128].astype(BF16)

                        @pl.when(here)
                        def _():
                            local().start()

                        @pl.when(jnp.logical_not(here))
                        def _():
                            remote().start()

    for k in range(3):
        square_copy(k).wait_recv()
    squares[y] = own_square[...] + near_squares[0] + near_squares[1] + near_squares[2]
    for k in range(3, 6):
        square_copy(k).start()
    for k in range(3, 6):
        square_copy(k).wait_recv()
    for slot in range(32):
        pltpu.make_async_copy(sums.at[slot], sums.at[slot], part_recv.at[slot]).wait()

    for k in range(7):
        for half in range(2):
            delta_copy(k, half).wait_send()
    for c in range(CHUNKS):
        for k in range(7):
            act_copy(c, k).wait_send()
        for k in range(8):
            fwd_copy(c, k).wait_send()

    @pl.when(jnp.logical_not(own_delta))
    def _():
        for half in range(2):
            delta_copy(7, half).wait_send()
    for slab in range(4):
        old_copy(slab).wait_send()
    for k in range(6):
        square_copy(k).wait_send()
    for half in range(2):
        for plane in range(2):
            for dz in range(2):
                for i in range(4):
                    _, remote, _, here = part_copy(half, plane, dz, i)

                    @pl.when(jnp.logical_not(here))
                    def _():
                        remote().wait_send()


def finish_kernel(held, sums, squares, out_ref, final_ref, sem):
    copies = [
        pltpu.make_async_copy(held.at[pl.ds(c * 6, 6)], final_ref.at[pl.ds(c * 6, 6)], sem.at[c])
        for c in range(4)
    ]
    for copy in copies:
        copy.start()
    factors = []
    for yy in range(4):
        inverse = lax.rsqrt(squares[yy] * (1.0 / GROUP_WIDTH) + 1e-05)
        factors.append(jnp.transpose(jnp.concatenate([inverse] * 16, axis=0))[0:ALL, 0:1])
    lane = lax.broadcasted_iota(jnp.int32, (256, 256), 1)
    source = (lane // 32) % 2 * 128 + lane // 128 * 64 + (lane // 64) % 2 * 32 + lane % 32
    order = (lax.broadcasted_iota(jnp.int32, (256, 256), 0) == source).astype(BF16)
    for hi in range(2):
        totals = []
        for half in range(2):
            total = None
            for yy in range(4):
                slot = (half * 2 + hi) * 8 + yy * 2
                pair = (sums[slot].astype(F32) + sums[slot + 1].astype(F32)) * factors[yy]
                total = pair if total is None else total + pair
            totals.append(total.astype(BF16))
        total = jnp.dot(jnp.concatenate(totals, axis=1), order, preferred_element_type=F32)
        for s in range(STEPS):
            rows = jnp.concatenate(
                [
                    total[c * SENT_ROWS + s * CHUNK_ROWS:c * SENT_ROWS + (s + 1) * CHUNK_ROWS]
                    for c in range(CHUNKS)
                ],
                axis=0,
            ).astype(BF16)
            for yl in range(2):
                at = yl * 256 + hi * 128
                out_ref[s, :, at:at + 128] = rows[:, yl * 128:(yl + 1) * 128]
    for copy in copies:
        copy.wait()


def local(
    old_weight, delta_codes, delta_exps, state_in, x_in, z_in, b_in, c_in, dt_in,
    dt_bias, a_rate, skip_gain, norm_gain,
):
    vmem = pl.BlockSpec(memory_space=pltpu.VMEM)
    hbm = pl.BlockSpec(memory_space=pltpu.HBM)
    dma = pltpu.SemaphoreType.DMA
    vectors = [v.reshape(1, -1) for v in (dt_bias, a_rate, skip_gain, norm_gain)]
    held, sums, squares = pl.pallas_call(
        mix_kernel,
        out_shape=(
            pltpu.VMEM(state_in.shape, F32),
            pltpu.VMEM((32, ALL, 128), BF16),
            pltpu.VMEM((4, 8, 128), F32),
        ),
        in_specs=[hbm] * 13,
        out_specs=(vmem, vmem, vmem),
        scratch_shapes=[
            pltpu.VMEM((64, 64), jnp.int32),
            pltpu.VMEM(x_in.shape, BF16),
            pltpu.VMEM(x_in.shape, BF16),
            pltpu.VMEM(b_in.shape, BF16),
            pltpu.VMEM(b_in.shape, BF16),
            pltpu.VMEM((STEPS, HEADS, ROWS), BF16),
            pltpu.VMEM((1, HEADS), F32),
            pltpu.VMEM((1, HEADS), F32),
            pltpu.VMEM((1, HEADS), F32),
            pltpu.VMEM((1, LOCAL), F32),
            pltpu.VMEM((LOCAL // 128, 16 * ROWS, 128), F32),
            pltpu.VMEM((2, 16 * ROWS, STATE), F32),
            pltpu.VMEM((1, 8 * ROWS, STATE), F32),
            pltpu.VMEM((LOCAL // 128, 8 * ROWS, 128), F32),
            pltpu.VMEM((ALL, LOCAL), F32),
            pltpu.VMEM((ALL, LOCAL), F32),
            pltpu.VMEM((128, 128), F32),
            pltpu.VMEM((8, 64, 1024), jnp.int32),
            pltpu.VMEM((8, 64, 1024), BF16),
            pltpu.VMEM((512, 1024), BF16),
            pltpu.VMEM((512, 1024), BF16),
            pltpu.VMEM((8, ALL, 1024), BF16),
            pltpu.VMEM((32, ALL, 128), BF16),
            pltpu.VMEM((8, 128), F32),
            pltpu.VMEM((3, 8, 128), F32),
            dma((10,)), dma((CHUNKS,)), dma((8,)), dma((4,)), dma((4,)), dma((4,)), dma((16,)), dma((16,)),
            dma((7 * CHUNKS,)), dma((7 * CHUNKS,)), dma((8 * CHUNKS,)), dma((8 * CHUNKS,)),
            dma((32,)), dma((32,)), dma((6,)), dma((6,)),
        ],
        compiler_params=pltpu.CompilerParams(
            collective_id=0, has_side_effects=True, vmem_limit_bytes=36 * 1024 * 1024
        ),
        cost_estimate=pl.CostEstimate(flops=9 * 10**8, bytes_accessed=10**7, transcendentals=0),
    )(
        *[
            pltpu.with_memory_space_constraint(a, pltpu.HBM)
            for a in (
                delta_codes, delta_exps, old_weight, state_in, x_in, z_in, b_in, c_in,
                jnp.swapaxes(dt_in, 1, 2), *vectors,
            )
        ]
    )
    mixed, final_state = pl.pallas_call(
        finish_kernel,
        out_shape=(
            jax.ShapeDtypeStruct((STEPS, ROWS, LOCAL), BF16),
            jax.ShapeDtypeStruct(state_in.shape, F32),
        ),
        in_specs=[vmem] * 3,
        out_specs=(vmem, hbm),
        scratch_shapes=[dma((4,))],
        compiler_params=pltpu.CompilerParams(vmem_limit_bytes=36 * 1024 * 1024),
        cost_estimate=pl.CostEstimate(flops=10**6, bytes_accessed=7 * 10**6, transcendentals=0),
    )(held, sums, squares)
    return mixed, final_state


def solution(mesh):
    return jax.shard_map(
        local,
        mesh=mesh,
        in_specs=(
            P(None, "tp"),
            P(("grp", "tp"), None),
            P(("grp", "tp"), None),
            P("grp", "tp", None, None),
            P(None, "grp", "tp"),
            P(None, "grp", "tp"),
            P(None, "grp", None),
            P(None, "grp", None),
            P(None, "grp", "tp"),
            P("tp"),
            P("tp"),
            P("tp"),
            P("tp"),
        ),
        out_specs=(P(None, "grp", "tp"), P("grp", "tp", None, None)),
        check_vma=False,
    )
```

```python
import functools

import jax
import jax.numpy as jnp
from jax import lax
from jax.experimental import pallas as pl
from jax.experimental.pallas import tpu as pltpu
from jax.sharding import PartitionSpec as P

MESH = pl.DeviceIdType.MESH
F32 = jnp.float32
BF16 = jnp.bfloat16
STEPS = 4
ROWS = 24
ALL = STEPS * ROWS
LOCAL = 512
STATE = 128
GROUP_WIDTH = 2048
CHUNKS = 3
CHUNK_ROWS = ROWS // CHUNKS
SENT_ROWS = STEPS * CHUNK_ROWS
HEADS = 8
CONTRACT_LAST = (((1,), (1,)), ((), ()))
CONTRACT_FIRST = (((0,), (0,)), ((), ()))


def split3(value):
    first = value.astype(BF16)
    rest = value - first.astype(F32)
    second = rest.astype(BF16)
    third = (rest - second.astype(F32)).astype(BF16)
    return first, second, third


def expand_heads(value, spread):
    parts = split3(value)
    total = jnp.dot(parts[2], spread, preferred_element_type=F32)
    total = total + jnp.dot(parts[1], spread, preferred_element_type=F32)
    return total + jnp.dot(parts[0], spread, preferred_element_type=F32)


def put(ref, first, value):
    for j in range(value.shape[1] // 128):
        ref[j, first:first + value.shape[0], :] = value[:, j * 128:(j + 1) * 128]


def pick_rows(ref, row, count):
    return jnp.concatenate(
        [ref[j, pl.ds(row, count, stride=ROWS), :] for j in range(ref.shape[0])], axis=1
    )


UNROLL = 4
PART_ORDER = ((1, 0), (1, 1), (3, 0), (3, 1), (2, 0), (2, 1), (0, 0), (0, 1))
OFFSETS = ((2, 0), (0, 1), (1, 0), (3, 1), (3, 0), (1, 1), (2, 1), (0, 0))
GATHER = ((0, 1), (0, 3), (0, 2), (1, 0), (1, 1), (1, 3), (1, 2))
OWN_PLANE = (0, 1, 2, 3)
OTHER_PLANE = (4, 5, 6)


def mix_kernel(
    codes_ref, exps_ref, old_ref, state_ref, x_ref, z_ref, b_ref, c_ref, dt_ref,
    bias_ref, rate_ref, skip_ref, gain_ref,
    held, sums, squares,
    exps, xs_in, zs_in, bs_in, cs_in, dts_in, bias_in, rate_in, skip_in, gain_in,
    left_rows, right_rows, read_rows, read_state, decay_rows, direct_rows, square_rows,
    codes, delta, weight, arrived, acts, parts, own_square, near_squares,
    small_sem, state_sem, codes_sem, own_sem, old_send, old_recv, delta_send, delta_recv,
    act_send, act_recv, fwd_send, fwd_recv, part_send, part_recv, square_send, square_recv,
):
    grp, tp = lax.axis_index("grp"), lax.axis_index("tp")
    z_lo, x = grp // 4, grp % 4
    y, z_hi, core = tp // 4, (tp // 2) % 2, tp % 2
    other = 1 - core
    chip = tp // 2
    partner = (grp, tp - core + other)
    mine = chip == grp
    crossed = chip == (1 - z_lo) * 4 + x

    def place(lo, xx, yy, hi, cc):
        return (lo * 4 + xx, yy * 4 + hi * 2 + cc)

    for k in range(8):
        dy, dz = OFFSETS[k]
        column = ((y + dy) % 4) * 2 + (z_hi + dz) % 2
        pltpu.make_async_copy(
            codes_ref.at[:, pl.ds(pl.multiple_of(column * 1024, 1024), 1024)], codes.at[k], codes_sem.at[k]
        ).start()

    small = [
        (exps_ref, exps), (dt_ref, dts_in), (bias_ref, bias_in), (rate_ref, rate_in), (skip_ref, skip_in),
        (x_ref, xs_in), (b_ref, bs_in), (c_ref, cs_in), (z_ref, zs_in), (gain_ref, gain_in),
    ]

    def small_copy(k):
        return pltpu.make_async_copy(small[k][0], small[k][1], small_sem.at[k])

    def state_copy(c):
        span = pl.ds(c * CHUNK_ROWS, CHUNK_ROWS)
        return pltpu.make_async_copy(state_ref.at[span], held.at[span], state_sem.at[c])

    for k in range(len(small)):
        small_copy(k).start()

    barrier = pltpu.get_barrier_semaphore()

    def greet(where):
        pl.semaphore_signal(barrier, inc=1, device_id=where, device_id_type=MESH)

    greet(partner)
    for cc in range(2):
        for yl in range(2):
            for dz in range(2):
                where = place((z_lo + dz) % 2, x, 2 * core + yl, (z_hi + dz) % 2, cc)
                if dz == 0:
                    @pl.when(jnp.logical_not((cc == core) & (2 * core + yl == y)))
                    def _():
                        greet(where)
                else:
                    greet(where)
    for dl, dx in GATHER[:6]:
        greet(((z_lo + dl) % 2 * 4 + (x + dx) % 4, tp))
    for cc in range(2):
        greet(place(z_lo, x, y, 1 - z_hi, (core + cc) % 2))
    for dy in range(1, 4):
        greet(place(z_lo, x, (y + dy) % 4, z_hi, core))
    for lo in range(2):
        for yy in range(4):
            for hi in range(2):
                where = place(lo, chip % 4, yy, hi, core)

                @pl.when(jnp.logical_not((where[0] == grp) & (where[1] == tp)))
                def _():
                    greet(where)
    own_delta = core == y // 2
    expected = (
        1 + 8 - own_delta.astype(jnp.int32) + 6 + 2 + 3 + 16 - mine.astype(jnp.int32) - crossed.astype(jnp.int32)
    )
    own_lanes = pl.ds(pl.multiple_of(core * LOCAL, LOCAL), LOCAL)

    def act_copy(c, k):
        dl, dx = GATHER[k]
        slot, where = grp, ((z_lo + dl) % 2 * 4 + (x + dx) % 4, tp)
        if k == 6:
            slot, where = z_lo * 4 + (x + 2) % 4, ((z_lo + 1) % 2 * 4 + x, tp)
        piece = acts.at[slot, pl.ds(c * SENT_ROWS, SENT_ROWS), own_lanes]
        return pltpu.make_async_remote_copy(
            src_ref=piece, dst_ref=piece,
            send_sem=act_send, recv_sem=act_recv.at[c * 7 + k],
            device_id=where, device_id_type=MESH,
        )

    def fwd_copy(c, k):
        slot = grp
        if k < 7:
            dl, dx = GATHER[k]
            slot = (z_lo + dl) % 2 * 4 + (x + 4 - dx) % 4
        piece = acts.at[slot, pl.ds(c * SENT_ROWS, SENT_ROWS), own_lanes]
        return pltpu.make_async_remote_copy(
            src_ref=piece, dst_ref=piece,
            send_sem=fwd_send, recv_sem=fwd_recv.at[0 if k in (7, 0, 1, 2) else 1],
            device_id=partner, device_id_type=MESH,
        )

    def square_copy(k):
        if k < 3:
            other_chip, other_core = ((0, 1), (1, 0), (1, 1))[k]
            where = place(z_lo, x, y, (z_hi + other_chip) % 2, (core + other_core) % 2)
            source, target = own_square, near_squares.at[k]
        else:
            where = place(z_lo, x, (y + k - 2) % 4, z_hi, core)
            source = target = squares.at[y]
        return pltpu.make_async_remote_copy(
            src_ref=source, dst_ref=target,
            send_sem=square_send.at[k], recv_sem=square_recv.at[k],
            device_id=where, device_id_type=MESH,
        )

    def feature_row(slab, cc):
        dz, yl = slab // 2, slab % 2
        lo, hi = (z_lo + dz) % 2, (z_hi + dz) % 2
        row = ((lo * 4 + x) * 2 + cc) * 512 + yl * 256 + hi * 128
        return pl.ds(pl.multiple_of(row, 128), 128)

    def own_copy(slab):
        return pltpu.make_async_copy(
            old_ref.at[feature_row(slab, core)],
            weight.at[pl.ds(slab * 128, 128), pl.ds(pl.multiple_of(core * LOCAL, LOCAL), LOCAL)],
            own_sem.at[slab],
        )

    def old_copy(slab):
        return pltpu.make_async_remote_copy(
            src_ref=old_ref.at[feature_row(slab, other)],
            dst_ref=weight.at[pl.ds(slab * 128, 128), pl.ds(pl.multiple_of(core * LOCAL, LOCAL), LOCAL)],
            send_sem=old_send.at[slab], recv_sem=old_recv.at[slab],
            device_id=partner, device_id_type=MESH,
        )

    def delta_copy(k, half):
        dy, dz = OFFSETS[k]
        slot = half * 8 + dz * 4 + (y % 2) * 2 + core
        return pltpu.make_async_remote_copy(
            src_ref=delta.at[k, pl.ds(half * 32, 32)], dst_ref=arrived.at[pl.ds(pl.multiple_of(slot * 32, 32), 32)],
            send_sem=delta_send.at[0 if k < 7 else 1 + half], recv_sem=delta_recv.at[half],
            device_id=place((z_lo + dz) % 2, x, (y + dy) % 4, (z_hi + dz) % 2, y // 2), device_id_type=MESH,
        )

    def delta_self(half):
        slot = half * 8 + (y % 2) * 2 + core
        return pltpu.make_async_copy(
            delta.at[7, pl.ds(half * 32, 32)], arrived.at[pl.ds(pl.multiple_of(slot * 32, 32), 32)],
            delta_recv.at[half],
        )

    small_copy(0).wait()
    scale = jnp.where(
        exps[...] == -14, 2.0**-14, jnp.where(exps[...] == -13, 2.0**-13, 2.0**-12)
    ).astype(BF16)
    block_at = lax.broadcasted_iota(jnp.int32, (64, 1024), 0)
    lane_block = lax.broadcasted_iota(jnp.int32, (64, 1024), 1) // 128
    for k in range(8):
        dy, dz = OFFSETS[k]
        column = ((y + dy) % 4) * 2 + (z_hi + dz) % 2
        pltpu.make_async_copy(codes.at[k], codes.at[k], codes_sem.at[k]).wait()
        if k == 3:
            for c in range(CHUNKS):
                state_copy(c).start()
        pick = (block_at == lane_block + column * 8).astype(BF16)
        wide = jnp.dot(scale, pick, preferred_element_type=F32)
        delta[k] = (codes[k].astype(F32) * wide).astype(BF16)

    for k in range(1, len(small)):
        small_copy(k).wait()
    group = tp // 4
    group_lanes = pl.ds(pl.multiple_of(group * STATE, STATE), STATE)
    head_of = lax.broadcasted_iota(jnp.int32, (HEADS, LOCAL), 1) // (LOCAL // HEADS)
    spread = (head_of == lax.broadcasted_iota(jnp.int32, (HEADS, LOCAL), 0)).astype(BF16)
    bias = expand_heads(jnp.broadcast_to(bias_in[...], (8, HEADS)), spread)[0:1]
    rate = expand_heads(jnp.broadcast_to(rate_in[...], (8, HEADS)), spread)[0:1]
    skip = expand_heads(jnp.broadcast_to(skip_in[...], (8, HEADS)), spread)[0:1]
    sizes, logs = [], []
    for s in range(STEPS):
        raw = lax.dot_general(dts_in[s], spread, CONTRACT_FIRST, preferred_element_type=F32) + bias
        sizes.append(jnp.maximum(raw, 0.0) + jnp.log1p(jnp.exp(-jnp.abs(raw))))
        own = sizes[s] * rate
        logs.append(own if s == 0 else logs[-1] + own)
    xs = [xs_in[s].astype(F32) for s in range(STEPS)]
    bs = [bs_in[s, :, group_lanes].astype(F32) for s in range(STEPS)]
    cs = [cs_in[s, :, group_lanes].astype(F32) for s in range(STEPS)]
    right_rows[...] = jnp.zeros(right_rows.shape, F32)
    read_rows[...] = jnp.zeros(read_rows.shape, F32)
    for s in range(STEPS):
        right_rows[0, s * ROWS:(s + 1) * ROWS, :] = bs[s]
        right_rows[0, (4 + s) * ROWS:(5 + s) * ROWS, :] = bs[s]
        read_rows[0, s * ROWS:(s + 1) * ROWS, :] = cs[s]
    right_rows[1, 8 * ROWS:11 * ROWS, :] = jnp.ones((3 * ROWS, STATE), F32)
    for s in range(STEPS):
        decay_rows[s * ROWS:(s + 1) * ROWS, :] = jnp.exp(-logs[s])
        direct = skip * xs[s]
        for u in range(s + 1):
            coef = sizes[u] if u == s else sizes[u] * jnp.exp(logs[u] - logs[s])
            term = coef * xs[u]
            direct = direct + term * jnp.sum(bs[u] * cs[s], axis=1, keepdims=True)
            if s == STEPS - 1:
                high = term.astype(BF16).astype(F32)
                put(left_rows, u * ROWS, high)
                put(left_rows, (4 + u) * ROWS, term - high)
        direct_rows[s * ROWS:(s + 1) * ROWS, :] = direct
    last = decay_rows[3 * ROWS:4 * ROWS, :]
    for at_row, part in enumerate(split3(last)):
        put(left_rows, (8 + at_row) * ROWS, part.astype(F32))
    put(left_rows, 11 * ROWS, jnp.zeros((5 * ROWS, LOCAL), F32))
    square_rows[ALL:, :] = jnp.zeros((128 - ALL, 128), F32)

    pl.semaphore_wait(barrier, expected)
    for k in range(7):
        delta_copy(k, 0).start()

    def read_one(row):
        value = held[row].reshape(LOCAL, STATE)
        high = value.astype(BF16)
        low = (value - high.astype(F32)).astype(BF16)
        both = jnp.concatenate([high, low], axis=1)
        reader = pick_rows(read_rows, row, 8).astype(BF16)
        reader = jnp.concatenate([reader, reader], axis=1)
        read = lax.dot_general(reader, both, CONTRACT_LAST, preferred_element_type=F32)
        for j in range(LOCAL // 128):
            read_state[j, pl.ds(row, 8, stride=ROWS), :] = read[:, j * 128:(j + 1) * 128]

    def update_one(row):
        left = pick_rows(left_rows, row, 16).astype(BF16)
        right = pick_rows(right_rows, row, 16).astype(BF16)
        update = lax.dot_general(left, right, CONTRACT_FIRST, preferred_element_type=F32)
        value = held[row].reshape(LOCAL, STATE)
        held[row] = (update[:, STATE:] * value + update[:, :STATE]).reshape(held.shape[1:])

    def over_rows(first, count, unroll, one):
        def some(i, carry):
            for j in range(unroll):
                one(first + i * unroll + j)
            return carry

        lax.fori_loop(0, count // unroll, some, 0)

    for c in range(CHUNKS):
        state_copy(c).wait()
        over_rows(c * CHUNK_ROWS, CHUNK_ROWS, UNROLL, read_one)
        pieces = []
        for s in range(STEPS):
            span = slice(s * ROWS + c * CHUNK_ROWS, s * ROWS + (c + 1) * CHUNK_ROWS)
            read = jnp.concatenate([read_state[j, span, :] for j in range(LOCAL // 128)], axis=1)
            z = zs_in[s].astype(F32)[c * CHUNK_ROWS:(c + 1) * CHUNK_ROWS]
            read_out = decay_rows[span, :] * read + direct_rows[span, :]
            pieces.append(read_out * (z / (1.0 + jnp.exp(-z))))
        gated = jnp.concatenate(pieces, axis=0)
        acts[grp, c * SENT_ROWS:(c + 1) * SENT_ROWS, own_lanes] = (gated * gain_in[...]).astype(BF16)
        for k in OWN_PLANE:
            act_copy(c, k).start()
        fwd_copy(c, 7).start()
        total = jnp.sum(gated * gated, axis=1, keepdims=True)
        square_rows[c * SENT_ROWS:(c + 1) * SENT_ROWS, :] = jnp.broadcast_to(total, (SENT_ROWS, 128))
    @pl.when(own_delta)
    def _():
        for half in range(2):
            delta_self(half).start()

    @pl.when(jnp.logical_not(own_delta))
    def _():
        for half in range(2):
            delta_copy(7, half).start()

    for k in range(7):
        delta_copy(k, 1).start()
    for slab in range(4):
        own_copy(slab).start()
        old_copy(slab).start()

    for c in range(CHUNKS):
        for k in (4, 5):
            act_copy(c, k).start()
    own_square[...] = jnp.transpose(square_rows[...])[0:8]
    for k in range(3):
        square_copy(k).start()

    for c in range(CHUNKS):
        over_rows(c * CHUNK_ROWS, CHUNK_ROWS, UNROLL, update_one)
        for k in OWN_PLANE:
            act_copy(c, k).wait_recv()
            fwd_copy(c, k).start()
            if k == 2:
                act_copy(c, 6).start()

    def part_copy(half, plane, dz, i):
        g = (z_lo + plane) % 2 * 4 + i
        dest = (g, ((z_lo + dz) % 2 * 4 + x) * 2 + core)
        at = ((half * 2 + plane) * 2 + dz) * 4 + i
        slot = (half * 2 + (z_hi + dz) % 2) * 8 + y * 2 + dz
        remote = lambda: pltpu.make_async_remote_copy(
            src_ref=parts.at[at], dst_ref=sums.at[slot],
            send_sem=part_send.at[at], recv_sem=part_recv,
            device_id=dest, device_id_type=MESH,
        )
        local = lambda: pltpu.make_async_copy(parts.at[at], sums.at[slot], part_recv)
        here = (dest[0] == grp) & (dest[1] == tp)
        return at, remote, local, here

    for slab in range(4):
        own_copy(slab).wait()
        old_copy(slab).wait_recv()
    for half in range(2):
        rows = arrived.at[pl.ds(half * 256, 256)]
        pltpu.make_async_copy(rows, rows, delta_recv.at[half]).wait()
        fresh = []
        for q in range(8):
            first = q * 64 + half * 32
            coming = half * 256 + q * 32
            fresh.append(
                (weight[first:first + 32, :].astype(F32) + arrived[coming:coming + 32, :].astype(F32)).astype(BF16)
            )
        fresh = jnp.concatenate(fresh, axis=0)
        for plane in range(2):
            if half == 0:
                if plane == 1:
                    for c in range(CHUNKS):
                        for k in OTHER_PLANE:
                            act_copy(c, k).wait_recv()
                            fwd_copy(c, k).start()
                other_lanes = pl.ds(pl.multiple_of(other * LOCAL, LOCAL), LOCAL)
                rows = acts.at[pl.ds((z_lo + plane) % 2 * 4, 4), :, other_lanes]
                pltpu.make_async_copy(rows, rows, fwd_recv.at[plane]).wait()
            for pair in range(1):
                start = (z_lo + plane) % 2 * 4
                lhs = acts[pl.ds(start, 4)].reshape(4 * ALL, 1024)
                got = lax.dot_general(lhs, fresh, CONTRACT_LAST, preferred_element_type=F32)
                for part in range(4):
                    for dz in range(2):
                        at = ((half * 2 + plane) * 2 + dz) * 4 + part
                        parts[at] = got[part * ALL:(part + 1) * ALL, dz * 128:dz * 128 + 128].astype(BF16)
                for dx, dz in PART_ORDER:
                    _, remote, local, here = part_copy(half, plane, dz, (x + dx) % 4)

                    @pl.when(here)
                    def _():
                        local().start()

                    @pl.when(jnp.logical_not(here))
                    def _():
                        remote().start()

    for k in range(3):
        square_copy(k).wait_recv()
    squares[y] = own_square[...] + near_squares[0] + near_squares[1] + near_squares[2]
    for k in range(3, 6):
        square_copy(k).start()
    for k in range(3, 6):
        square_copy(k).wait_recv()
    pltpu.make_async_copy(delta.at[pl.ds(0, 7)], delta.at[pl.ds(0, 7)], delta_send.at[0]).wait()
    for count, sem in ((7, act_send), (8, fwd_send)):
        rows = acts.at[pl.ds(0, count), :, own_lanes]
        pltpu.make_async_copy(rows, rows, sem).wait()

    @pl.when(jnp.logical_not(own_delta))
    def _():
        for half in range(2):
            delta_copy(7, half).wait_send()
    for slab in range(4):
        old_copy(slab).wait_send()
    for k in range(6):
        square_copy(k).wait_send()
    for half in range(2):
        for plane in range(2):
            for dz in range(2):
                for i in range(4):
                    _, remote, _, here = part_copy(half, plane, dz, i)

                    @pl.when(jnp.logical_not(here))
                    def _():
                        remote().wait_send()
    pltpu.make_async_copy(sums, sums, part_recv).wait()


def finish_kernel(held, sums, squares, out_ref, final_ref, sem):
    copies = [
        pltpu.make_async_copy(held.at[pl.ds(c * 6, 6)], final_ref.at[pl.ds(c * 6, 6)], sem.at[c])
        for c in range(4)
    ]
    for copy in copies:
        copy.start()
    factors = []
    for yy in range(4):
        inverse = lax.rsqrt(squares[yy] * (1.0 / GROUP_WIDTH) + 1e-05)
        factors.append(jnp.transpose(jnp.concatenate([inverse] * 16, axis=0))[0:ALL, 0:1])
    lane = lax.broadcasted_iota(jnp.int32, (256, 256), 1)
    source = (lane // 32) % 2 * 128 + lane // 128 * 64 + (lane // 64) % 2 * 32 + lane % 32
    order = (lax.broadcasted_iota(jnp.int32, (256, 256), 0) == source).astype(BF16)
    for hi in range(2):
        totals = []
        for half in range(2):
            total = None
            for yy in range(4):
                slot = (half * 2 + hi) * 8 + yy * 2
                pair = (sums[slot].astype(F32) + sums[slot + 1].astype(F32)) * factors[yy]
                total = pair if total is None else total + pair
            totals.append(total.astype(BF16))
        total = jnp.dot(jnp.concatenate(totals, axis=1), order, preferred_element_type=F32)
        for s in range(STEPS):
            rows = jnp.concatenate(
                [
                    total[c * SENT_ROWS + s * CHUNK_ROWS:c * SENT_ROWS + (s + 1) * CHUNK_ROWS]
                    for c in range(CHUNKS)
                ],
                axis=0,
            ).astype(BF16)
            for yl in range(2):
                at = yl * 256 + hi * 128
                out_ref[s, :, at:at + 128] = rows[:, yl * 128:(yl + 1) * 128]
    for copy in copies:
        copy.wait()


def local(
    old_weight, delta_codes, delta_exps, state_in, x_in, z_in, b_in, c_in, dt_in,
    dt_bias, a_rate, skip_gain, norm_gain,
):
    vmem = pl.BlockSpec(memory_space=pltpu.VMEM)
    hbm = pl.BlockSpec(memory_space=pltpu.HBM)
    dma = pltpu.SemaphoreType.DMA
    vectors = [v.reshape(1, -1) for v in (dt_bias, a_rate, skip_gain, norm_gain)]
    held, sums, squares = pl.pallas_call(
        mix_kernel,
        out_shape=(
            pltpu.VMEM(state_in.shape, F32),
            pltpu.VMEM((32, ALL, 128), BF16),
            pltpu.VMEM((4, 8, 128), F32),
        ),
        in_specs=[hbm] * 13,
        out_specs=(vmem, vmem, vmem),
        scratch_shapes=[
            pltpu.VMEM((64, 64), jnp.int32),
            pltpu.VMEM(x_in.shape, BF16),
            pltpu.VMEM(x_in.shape, BF16),
            pltpu.VMEM(b_in.shape, BF16),
            pltpu.VMEM(b_in.shape, BF16),
            pltpu.VMEM((STEPS, HEADS, ROWS), BF16),
            pltpu.VMEM((1, HEADS), F32),
            pltpu.VMEM((1, HEADS), F32),
            pltpu.VMEM((1, HEADS), F32),
            pltpu.VMEM((1, LOCAL), F32),
            pltpu.VMEM((LOCAL // 128, 16 * ROWS, 128), F32),
            pltpu.VMEM((2, 16 * ROWS, STATE), F32),
            pltpu.VMEM((1, 8 * ROWS, STATE), F32),
            pltpu.VMEM((LOCAL // 128, 8 * ROWS, 128), F32),
            pltpu.VMEM((ALL, LOCAL), F32),
            pltpu.VMEM((ALL, LOCAL), F32),
            pltpu.VMEM((128, 128), F32),
            pltpu.VMEM((8, 64, 1024), jnp.int32),
            pltpu.VMEM((8, 64, 1024), BF16),
            pltpu.VMEM((512, 1024), BF16),
            pltpu.VMEM((512, 1024), BF16),
            pltpu.VMEM((8, ALL, 1024), BF16),
            pltpu.VMEM((32, ALL, 128), BF16),
            pltpu.VMEM((8, 128), F32),
            pltpu.VMEM((3, 8, 128), F32),
            dma((10,)), dma((CHUNKS,)), dma((8,)), dma((4,)), dma((4,)), dma((4,)), dma((3,)), dma((2,)),
            dma, dma((7 * CHUNKS,)), dma, dma((2,)),
            dma((32,)), dma, dma((6,)), dma((6,)),
        ],
        compiler_params=pltpu.CompilerParams(
            collective_id=0, has_side_effects=True, vmem_limit_bytes=36 * 1024 * 1024
        ),
        cost_estimate=pl.CostEstimate(flops=9 * 10**8, bytes_accessed=10**7, transcendentals=0),
    )(
        *[
            pltpu.with_memory_space_constraint(a, pltpu.HBM)
            for a in (
                delta_codes, delta_exps, old_weight, state_in, x_in, z_in, b_in, c_in,
                jnp.swapaxes(dt_in, 1, 2), *vectors,
            )
        ]
    )
    mixed, final_state = pl.pallas_call(
        finish_kernel,
        out_shape=(
            jax.ShapeDtypeStruct((STEPS, ROWS, LOCAL), BF16),
            jax.ShapeDtypeStruct(state_in.shape, F32),
        ),
        in_specs=[vmem] * 3,
        out_specs=(vmem, hbm),
        scratch_shapes=[dma((4,))],
        compiler_params=pltpu.CompilerParams(vmem_limit_bytes=36 * 1024 * 1024),
        cost_estimate=pl.CostEstimate(flops=10**6, bytes_accessed=7 * 10**6, transcendentals=0),
    )(held, sums, squares)
    return mixed, final_state


def solution(mesh):
    return jax.shard_map(
        local,
        mesh=mesh,
        in_specs=(
            P(None, "tp"),
            P(("grp", "tp"), None),
            P(("grp", "tp"), None),
            P("grp", "tp", None, None),
            P(None, "grp", "tp"),
            P(None, "grp", "tp"),
            P(None, "grp", None),
            P(None, "grp", None),
            P(None, "grp", "tp"),
            P("tp"),
            P("tp"),
            P("tp"),
            P("tp"),
        ),
        out_specs=(P(None, "grp", "tp"), P("grp", "tp", None, None)),
        check_vma=False,
    )
```

```python
import functools

import jax
import jax.numpy as jnp
from jax import lax
from jax.experimental import pallas as pl
from jax.experimental.pallas import tpu as pltpu
from jax.sharding import PartitionSpec as P

MESH = pl.DeviceIdType.MESH
F32 = jnp.float32
BF16 = jnp.bfloat16
STEPS = 4
ROWS = 24
ALL = STEPS * ROWS
LOCAL = 512
STATE = 128
GROUP_WIDTH = 2048
CHUNKS = 3
CHUNK_ROWS = ROWS // CHUNKS
SENT_ROWS = STEPS * CHUNK_ROWS
HEADS = 8
CONTRACT_LAST = (((1,), (1,)), ((), ()))
CONTRACT_FIRST = (((0,), (0,)), ((), ()))


def split3(value):
    first = value.astype(BF16)
    rest = value - first.astype(F32)
    second = rest.astype(BF16)
    third = (rest - second.astype(F32)).astype(BF16)
    return first, second, third


def expand_heads(value, spread):
    parts = split3(value)
    total = jnp.dot(parts[2], spread, preferred_element_type=F32)
    total = total + jnp.dot(parts[1], spread, preferred_element_type=F32)
    return total + jnp.dot(parts[0], spread, preferred_element_type=F32)


def put(ref, first, value):
    for j in range(value.shape[1] // 128):
        ref[j, first:first + value.shape[0], :] = value[:, j * 128:(j + 1) * 128]


def pick_rows(ref, row, count):
    return jnp.concatenate(
        [ref[j, pl.ds(row, count, stride=ROWS), :] for j in range(ref.shape[0])], axis=1
    )


UNROLL = 4
PART_ORDER = ((1, 0), (1, 1), (3, 0), (3, 1), (2, 0), (2, 1), (0, 0), (0, 1))
OFFSETS = ((2, 0), (0, 1), (1, 0), (3, 1), (3, 0), (1, 1), (2, 1), (0, 0))
GATHER = ((0, 1), (0, 3), (0, 2), (1, 0), (1, 1), (1, 3), (1, 2))
OWN_PLANE = (0, 1, 2, 3)
OTHER_PLANE = (4, 5, 6)


def mix_kernel(
    codes_ref, exps_ref, old_ref, state_ref, x_ref, z_ref, b_ref, c_ref, dt_ref,
    bias_ref, rate_ref, skip_ref, gain_ref,
    held, sums, squares,
    exps, xs_in, zs_in, bs_in, cs_in, dts_in, bias_in, rate_in, skip_in, gain_in,
    left_rows, right_rows, read_rows, read_state, decay_rows, direct_rows, square_rows,
    codes, delta, weight, arrived, acts, parts, own_square, near_squares,
    small_sem, state_sem, codes_sem, own_sem, old_send, old_recv, delta_send, delta_recv,
    act_send, act_recv, fwd_send, fwd_recv, part_send, part_recv, square_send, square_recv,
):
    grp, tp = lax.axis_index("grp"), lax.axis_index("tp")
    z_lo, x = grp // 4, grp % 4
    y, z_hi, core = tp // 4, (tp // 2) % 2, tp % 2
    other = 1 - core
    chip = tp // 2
    partner = (grp, tp - core + other)
    mine = chip == grp
    crossed = chip == (1 - z_lo) * 4 + x

    def place(lo, xx, yy, hi, cc):
        return (lo * 4 + xx, yy * 4 + hi * 2 + cc)

    for k in range(8):
        dy, dz = OFFSETS[k]
        column = ((y + dy) % 4) * 2 + (z_hi + dz) % 2
        pltpu.make_async_copy(
            codes_ref.at[:, pl.ds(pl.multiple_of(column * 1024, 1024), 1024)], codes.at[k], codes_sem.at[k]
        ).start()

    small = [
        (exps_ref, exps), (dt_ref, dts_in), (bias_ref, bias_in), (rate_ref, rate_in), (skip_ref, skip_in),
        (x_ref, xs_in), (b_ref, bs_in), (c_ref, cs_in), (z_ref, zs_in), (gain_ref, gain_in),
    ]

    def small_copy(k):
        return pltpu.make_async_copy(small[k][0], small[k][1], small_sem.at[k])

    def state_copy(c):
        span = pl.ds(c * CHUNK_ROWS, CHUNK_ROWS)
        return pltpu.make_async_copy(state_ref.at[span], held.at[span], state_sem.at[c])

    for k in range(len(small)):
        small_copy(k).start()

    barrier = pltpu.get_barrier_semaphore()

    def greet(where):
        pl.semaphore_signal(barrier, inc=1, device_id=where, device_id_type=MESH)

    greet(partner)
    for cc in range(2):
        for yl in range(2):
            for dz in range(2):
                where = place((z_lo + dz) % 2, x, 2 * core + yl, (z_hi + dz) % 2, cc)
                if dz == 0:
                    @pl.when(jnp.logical_not((cc == core) & (2 * core + yl == y)))
                    def _():
                        greet(where)
                else:
                    greet(where)
    for dl, dx in GATHER[:6]:
        greet(((z_lo + dl) % 2 * 4 + (x + dx) % 4, tp))
    for cc in range(2):
        greet(place(z_lo, x, y, 1 - z_hi, (core + cc) % 2))
    for dy in range(1, 4):
        greet(place(z_lo, x, (y + dy) % 4, z_hi, core))
    for lo in range(2):
        for yy in range(4):
            for hi in range(2):
                where = place(lo, chip % 4, yy, hi, core)

                @pl.when(jnp.logical_not((where[0] == grp) & (where[1] == tp)))
                def _():
                    greet(where)
    own_delta = core == y // 2
    expected = (
        1 + 8 - own_delta.astype(jnp.int32) + 6 + 2 + 3 + 16 - mine.astype(jnp.int32) - crossed.astype(jnp.int32)
    )
    own_lanes = pl.ds(pl.multiple_of(core * LOCAL, LOCAL), LOCAL)

    def act_copy(c, k):
        dl, dx = GATHER[k]
        slot, where = grp, ((z_lo + dl) % 2 * 4 + (x + dx) % 4, tp)
        if k == 6:
            slot, where = z_lo * 4 + (x + 2) % 4, ((z_lo + 1) % 2 * 4 + x, tp)
        piece = acts.at[slot, pl.ds(c * SENT_ROWS, SENT_ROWS), own_lanes]
        return pltpu.make_async_remote_copy(
            src_ref=piece, dst_ref=piece,
            send_sem=act_send, recv_sem=act_recv.at[c * 7 + k],
            device_id=where, device_id_type=MESH,
        )

    def fwd_copy(c, k):
        slot = grp
        if k < 7:
            dl, dx = GATHER[k]
            slot = (z_lo + dl) % 2 * 4 + (x + 4 - dx) % 4
        piece = acts.at[slot, pl.ds(c * SENT_ROWS, SENT_ROWS), own_lanes]
        return pltpu.make_async_remote_copy(
            src_ref=piece, dst_ref=piece,
            send_sem=fwd_send, recv_sem=fwd_recv.at[0 if k in (7, 0, 1, 2) else 1],
            device_id=partner, device_id_type=MESH,
        )

    def square_copy(k):
        if k < 3:
            other_chip, other_core = ((0, 1), (1, 0), (1, 1))[k]
            where = place(z_lo, x, y, (z_hi + other_chip) % 2, (core + other_core) % 2)
            source, target = own_square, near_squares.at[k]
        else:
            where = place(z_lo, x, (y + k - 2) % 4, z_hi, core)
            source = target = squares.at[y]
        return pltpu.make_async_remote_copy(
            src_ref=source, dst_ref=target,
            send_sem=square_send.at[k], recv_sem=square_recv.at[k],
            device_id=where, device_id_type=MESH,
        )

    def feature_row(slab, cc):
        dz, yl = slab // 2, slab % 2
        lo, hi = (z_lo + dz) % 2, (z_hi + dz) % 2
        row = ((lo * 4 + x) * 2 + cc) * 512 + yl * 256 + hi * 128
        return pl.ds(pl.multiple_of(row, 128), 128)

    def own_copy(slab):
        return pltpu.make_async_copy(
            old_ref.at[feature_row(slab, core)],
            weight.at[pl.ds(slab * 128, 128), pl.ds(pl.multiple_of(core * LOCAL, LOCAL), LOCAL)],
            own_sem,
        )

    def old_copy(slab):
        return pltpu.make_async_remote_copy(
            src_ref=old_ref.at[feature_row(slab, other)],
            dst_ref=weight.at[pl.ds(slab * 128, 128), pl.ds(pl.multiple_of(core * LOCAL, LOCAL), LOCAL)],
            send_sem=old_send, recv_sem=old_recv,
            device_id=partner, device_id_type=MESH,
        )

    def delta_copy(k, half):
        dy, dz = OFFSETS[k]
        slot = half * 8 + dz * 4 + (y % 2) * 2 + core
        return pltpu.make_async_remote_copy(
            src_ref=delta.at[k, pl.ds(half * 32, 32)], dst_ref=arrived.at[pl.ds(pl.multiple_of(slot * 32, 32), 32)],
            send_sem=delta_send.at[0 if k < 7 else 1 + half], recv_sem=delta_recv.at[half],
            device_id=place((z_lo + dz) % 2, x, (y + dy) % 4, (z_hi + dz) % 2, y // 2), device_id_type=MESH,
        )

    def delta_self(half):
        slot = half * 8 + (y % 2) * 2 + core
        return pltpu.make_async_copy(
            delta.at[7, pl.ds(half * 32, 32)], arrived.at[pl.ds(pl.multiple_of(slot * 32, 32), 32)],
            delta_recv.at[half],
        )

    small_copy(0).wait()
    scale = jnp.where(
        exps[...] == -14, 2.0**-14, jnp.where(exps[...] == -13, 2.0**-13, 2.0**-12)
    ).astype(BF16)
    block_at = lax.broadcasted_iota(jnp.int32, (64, 1024), 0)
    lane_block = lax.broadcasted_iota(jnp.int32, (64, 1024), 1) // 128
    for k in range(8):
        dy, dz = OFFSETS[k]
        column = ((y + dy) % 4) * 2 + (z_hi + dz) % 2
        pltpu.make_async_copy(codes.at[k], codes.at[k], codes_sem.at[k]).wait()
        if k == 3:
            for c in range(CHUNKS):
                state_copy(c).start()
        pick = (block_at == lane_block + column * 8).astype(BF16)
        wide = jnp.dot(scale, pick, preferred_element_type=F32)
        delta[k] = (codes[k].astype(F32) * wide).astype(BF16)

    for k in range(1, len(small)):
        small_copy(k).wait()
    group = tp // 4
    group_lanes = pl.ds(pl.multiple_of(group * STATE, STATE), STATE)
    head_of = lax.broadcasted_iota(jnp.int32, (HEADS, LOCAL), 1) // (LOCAL // HEADS)
    spread = (head_of == lax.broadcasted_iota(jnp.int32, (HEADS, LOCAL), 0)).astype(BF16)
    bias = expand_heads(jnp.broadcast_to(bias_in[...], (8, HEADS)), spread)[0:1]
    rate = expand_heads(jnp.broadcast_to(rate_in[...], (8, HEADS)), spread)[0:1]
    skip = expand_heads(jnp.broadcast_to(skip_in[...], (8, HEADS)), spread)[0:1]
    sizes, logs = [], []
    for s in range(STEPS):
        raw = lax.dot_general(dts_in[s], spread, CONTRACT_FIRST, preferred_element_type=F32) + bias
        sizes.append(jnp.maximum(raw, 0.0) + jnp.log1p(jnp.exp(-jnp.abs(raw))))
        own = sizes[s] * rate
        logs.append(own if s == 0 else logs[-1] + own)
    xs = [xs_in[s].astype(F32) for s in range(STEPS)]
    bs = [bs_in[s, :, group_lanes].astype(F32) for s in range(STEPS)]
    cs = [cs_in[s, :, group_lanes].astype(F32) for s in range(STEPS)]
    right_rows[...] = jnp.zeros(right_rows.shape, F32)
    read_rows[...] = jnp.zeros(read_rows.shape, F32)
    for s in range(STEPS):
        right_rows[0, s * ROWS:(s + 1) * ROWS, :] = bs[s]
        right_rows[0, (4 + s) * ROWS:(5 + s) * ROWS, :] = bs[s]
        read_rows[0, s * ROWS:(s + 1) * ROWS, :] = cs[s]
    right_rows[1, 8 * ROWS:11 * ROWS, :] = jnp.ones((3 * ROWS, STATE), F32)
    for s in range(STEPS):
        decay_rows[s * ROWS:(s + 1) * ROWS, :] = jnp.exp(-logs[s])
        direct = skip * xs[s]
        for u in range(s + 1):
            coef = sizes[u] if u == s else sizes[u] * jnp.exp(logs[u] - logs[s])
            term = coef * xs[u]
            direct = direct + term * jnp.sum(bs[u] * cs[s], axis=1, keepdims=True)
            if s == STEPS - 1:
                high = term.astype(BF16).astype(F32)
                put(left_rows, u * ROWS, high)
                put(left_rows, (4 + u) * ROWS, term - high)
        direct_rows[s * ROWS:(s + 1) * ROWS, :] = direct
    last = decay_rows[3 * ROWS:4 * ROWS, :]
    for at_row, part in enumerate(split3(last)):
        put(left_rows, (8 + at_row) * ROWS, part.astype(F32))
    put(left_rows, 11 * ROWS, jnp.zeros((5 * ROWS, LOCAL), F32))
    square_rows[ALL:, :] = jnp.zeros((128 - ALL, 128), F32)

    pl.semaphore_wait(barrier, expected)
    for k in range(7):
        delta_copy(k, 0).start()

    def read_one(row):
        value = held[row].reshape(LOCAL, STATE)
        high = value.astype(BF16)
        low = (value - high.astype(F32)).astype(BF16)
        both = jnp.concatenate([high, low], axis=1)
        reader = pick_rows(read_rows, row, 8).astype(BF16)
        reader = jnp.concatenate([reader, reader], axis=1)
        read = lax.dot_general(reader, both, CONTRACT_LAST, preferred_element_type=F32)
        for j in range(LOCAL // 128):
            read_state[j, pl.ds(row, 8, stride=ROWS), :] = read[:, j * 128:(j + 1) * 128]

    def update_one(row):
        left = pick_rows(left_rows, row, 16).astype(BF16)
        right = pick_rows(right_rows, row, 16).astype(BF16)
        update = lax.dot_general(left, right, CONTRACT_FIRST, preferred_element_type=F32)
        value = held[row].reshape(LOCAL, STATE)
        held[row] = (update[:, STATE:] * value + update[:, :STATE]).reshape(held.shape[1:])

    def over_rows(first, count, unroll, one):
        def some(i, carry):
            for j in range(unroll):
                one(first + i * unroll + j)
            return carry

        lax.fori_loop(0, count // unroll, some, 0)

    for c in range(CHUNKS):
        state_copy(c).wait()
        over_rows(c * CHUNK_ROWS, CHUNK_ROWS, UNROLL, read_one)
        pieces = []
        for s in range(STEPS):
            span = slice(s * ROWS + c * CHUNK_ROWS, s * ROWS + (c + 1) * CHUNK_ROWS)
            read = jnp.concatenate([read_state[j, span, :] for j in range(LOCAL // 128)], axis=1)
            z = zs_in[s].astype(F32)[c * CHUNK_ROWS:(c + 1) * CHUNK_ROWS]
            read_out = decay_rows[span, :] * read + direct_rows[span, :]
            pieces.append(read_out * (z / (1.0 + jnp.exp(-z))))
        gated = jnp.concatenate(pieces, axis=0)
        acts[grp, c * SENT_ROWS:(c + 1) * SENT_ROWS, own_lanes] = (gated * gain_in[...]).astype(BF16)
        for k in range(6):
            act_copy(c, k).start()
        fwd_copy(c, 7).start()
        total = jnp.sum(gated * gated, axis=1, keepdims=True)
        square_rows[c * SENT_ROWS:(c + 1) * SENT_ROWS, :] = jnp.broadcast_to(total, (SENT_ROWS, 128))
    @pl.when(own_delta)
    def _():
        for half in range(2):
            delta_self(half).start()

    @pl.when(jnp.logical_not(own_delta))
    def _():
        for half in range(2):
            delta_copy(7, half).start()

    for k in range(7):
        delta_copy(k, 1).start()
    for slab in range(4):
        own_copy(slab).start()
        old_copy(slab).start()

    own_square[...] = jnp.transpose(square_rows[...])[0:8]
    for k in range(3):
        square_copy(k).start()

    over_rows(0, ROWS, UNROLL, update_one)
    for c in range(CHUNKS):
        for k in OWN_PLANE:
            act_copy(c, k).wait_recv()
            fwd_copy(c, k).start()
            if k == 2:
                act_copy(c, 6).start()

    def part_copy(half, plane, dz, dx):
        i = (x + dx) % 4
        g = (z_lo + plane) % 2 * 4 + i
        alone = 1 + half * 2 + dz if plane == 0 and dx == 0 else 0
        dest = (g, ((z_lo + dz) % 2 * 4 + x) * 2 + core)
        at = ((half * 2 + plane) * 2 + dz) * 4 + i
        slot = (half * 2 + (z_hi + dz) % 2) * 8 + y * 2 + dz
        remote = lambda: pltpu.make_async_remote_copy(
            src_ref=parts.at[at], dst_ref=sums.at[slot],
            send_sem=part_send.at[alone], recv_sem=part_recv,
            device_id=dest, device_id_type=MESH,
        )
        local = lambda: pltpu.make_async_copy(parts.at[at], sums.at[slot], part_recv)
        here = (dest[0] == grp) & (dest[1] == tp)
        return remote, local, here

    for which, sem in ((core, own_sem), (other, old_recv)):
        rows = weight.at[:, pl.ds(pl.multiple_of(which * LOCAL, LOCAL), LOCAL)]
        pltpu.make_async_copy(rows, rows, sem).wait()
    for half in range(2):
        rows = arrived.at[pl.ds(half * 256, 256)]
        pltpu.make_async_copy(rows, rows, delta_recv.at[half]).wait()
        fresh = []
        for q in range(8):
            first = q * 64 + half * 32
            coming = half * 256 + q * 32
            fresh.append(
                (weight[first:first + 32, :].astype(F32) + arrived[coming:coming + 32, :].astype(F32)).astype(BF16)
            )
        fresh = jnp.concatenate(fresh, axis=0)
        for plane in range(2):
            if half == 0:
                if plane == 1:
                    for c in range(CHUNKS):
                        for k in OTHER_PLANE:
                            act_copy(c, k).wait_recv()
                            fwd_copy(c, k).start()
                other_lanes = pl.ds(pl.multiple_of(other * LOCAL, LOCAL), LOCAL)
                rows = acts.at[pl.ds((z_lo + plane) % 2 * 4, 4), :, other_lanes]
                pltpu.make_async_copy(rows, rows, fwd_recv.at[plane]).wait()
            for pair in range(1):
                start = (z_lo + plane) % 2 * 4
                lhs = acts[pl.ds(start, 4)].reshape(4 * ALL, 1024)
                got = lax.dot_general(lhs, fresh, CONTRACT_LAST, preferred_element_type=F32)
                for part in range(4):
                    for dz in range(2):
                        at = ((half * 2 + plane) * 2 + dz) * 4 + part
                        parts[at] = got[part * ALL:(part + 1) * ALL, dz * 128:dz * 128 + 128].astype(BF16)
                for dx, dz in PART_ORDER:
                    remote, local, here = part_copy(half, plane, dz, dx)
                    if plane == 1 or dx > 0:
                        remote().start()
                        continue

                    @pl.when(here)
                    def _():
                        local().start()

                    @pl.when(jnp.logical_not(here))
                    def _():
                        remote().start()

    for k in range(3):
        square_copy(k).wait_recv()
    squares[y] = own_square[...] + near_squares[0] + near_squares[1] + near_squares[2]
    for k in range(3, 6):
        square_copy(k).start()
    for k in range(3, 6):
        square_copy(k).wait_recv()
    pltpu.make_async_copy(delta.at[pl.ds(0, 7)], delta.at[pl.ds(0, 7)], delta_send.at[0]).wait()
    for count, sem in ((7, act_send), (8, fwd_send)):
        rows = acts.at[pl.ds(0, count), :, own_lanes]
        pltpu.make_async_copy(rows, rows, sem).wait()

    @pl.when(jnp.logical_not(own_delta))
    def _():
        for half in range(2):
            delta_copy(7, half).wait_send()
    rows = weight.at[:, own_lanes]
    pltpu.make_async_copy(rows, rows, old_send).wait()
    for k in range(6):
        square_copy(k).wait_send()
    pltpu.make_async_copy(parts.at[pl.ds(0, 28)], parts.at[pl.ds(0, 28)], part_send.at[0]).wait()
    for half in range(2):
        for dz in range(2):
            remote, _, here = part_copy(half, 0, dz, 0)

            @pl.when(jnp.logical_not(here))
            def _():
                remote().wait_send()
    pltpu.make_async_copy(sums, sums, part_recv).wait()


def finish_kernel(held, sums, squares, out_ref, final_ref, sem):
    copies = [
        pltpu.make_async_copy(held.at[pl.ds(c * 6, 6)], final_ref.at[pl.ds(c * 6, 6)], sem.at[c])
        for c in range(4)
    ]
    for copy in copies:
        copy.start()
    factors = []
    for yy in range(4):
        inverse = lax.rsqrt(squares[yy] * (1.0 / GROUP_WIDTH) + 1e-05)
        factors.append(jnp.transpose(jnp.concatenate([inverse] * 16, axis=0))[0:ALL, 0:1])
    lane = lax.broadcasted_iota(jnp.int32, (256, 256), 1)
    source = (lane // 32) % 2 * 128 + lane // 128 * 64 + (lane // 64) % 2 * 32 + lane % 32
    order = (lax.broadcasted_iota(jnp.int32, (256, 256), 0) == source).astype(BF16)
    for hi in range(2):
        totals = []
        for half in range(2):
            total = None
            for yy in range(4):
                slot = (half * 2 + hi) * 8 + yy * 2
                pair = (sums[slot].astype(F32) + sums[slot + 1].astype(F32)) * factors[yy]
                total = pair if total is None else total + pair
            totals.append(total.astype(BF16))
        total = jnp.dot(jnp.concatenate(totals, axis=1), order, preferred_element_type=F32)
        for s in range(STEPS):
            rows = jnp.concatenate(
                [
                    total[c * SENT_ROWS + s * CHUNK_ROWS:c * SENT_ROWS + (s + 1) * CHUNK_ROWS]
                    for c in range(CHUNKS)
                ],
                axis=0,
            ).astype(BF16)
            for yl in range(2):
                at = yl * 256 + hi * 128
                out_ref[s, :, at:at + 128] = rows[:, yl * 128:(yl + 1) * 128]
    for copy in copies:
        copy.wait()


def local(
    old_weight, delta_codes, delta_exps, state_in, x_in, z_in, b_in, c_in, dt_in,
    dt_bias, a_rate, skip_gain, norm_gain,
):
    vmem = pl.BlockSpec(memory_space=pltpu.VMEM)
    hbm = pl.BlockSpec(memory_space=pltpu.HBM)
    dma = pltpu.SemaphoreType.DMA
    vectors = [v.reshape(1, -1) for v in (dt_bias, a_rate, skip_gain, norm_gain)]
    held, sums, squares = pl.pallas_call(
        mix_kernel,
        out_shape=(
            pltpu.VMEM(state_in.shape, F32),
            pltpu.VMEM((32, ALL, 128), BF16),
            pltpu.VMEM((4, 8, 128), F32),
        ),
        in_specs=[hbm] * 13,
        out_specs=(vmem, vmem, vmem),
        scratch_shapes=[
            pltpu.VMEM((64, 64), jnp.int32),
            pltpu.VMEM(x_in.shape, BF16),
            pltpu.VMEM(x_in.shape, BF16),
            pltpu.VMEM(b_in.shape, BF16),
            pltpu.VMEM(b_in.shape, BF16),
            pltpu.VMEM((STEPS, HEADS, ROWS), BF16),
            pltpu.VMEM((1, HEADS), F32),
            pltpu.VMEM((1, HEADS), F32),
            pltpu.VMEM((1, HEADS), F32),
            pltpu.VMEM((1, LOCAL), F32),
            pltpu.VMEM((LOCAL // 128, 16 * ROWS, 128), F32),
            pltpu.VMEM((2, 16 * ROWS, STATE), F32),
            pltpu.VMEM((1, 8 * ROWS, STATE), F32),
            pltpu.VMEM((LOCAL // 128, 8 * ROWS, 128), F32),
            pltpu.VMEM((ALL, LOCAL), F32),
            pltpu.VMEM((ALL, LOCAL), F32),
            pltpu.VMEM((128, 128), F32),
            pltpu.VMEM((8, 64, 1024), jnp.int32),
            pltpu.VMEM((8, 64, 1024), BF16),
            pltpu.VMEM((512, 1024), BF16),
            pltpu.VMEM((512, 1024), BF16),
            pltpu.VMEM((8, ALL, 1024), BF16),
            pltpu.VMEM((32, ALL, 128), BF16),
            pltpu.VMEM((8, 128), F32),
            pltpu.VMEM((3, 8, 128), F32),
            dma((10,)), dma((CHUNKS,)), dma((8,)), dma, dma, dma, dma((3,)), dma((2,)),
            dma, dma((7 * CHUNKS,)), dma, dma((2,)),
            dma((5,)), dma, dma((6,)), dma((6,)),
        ],
        compiler_params=pltpu.CompilerParams(
            collective_id=0, has_side_effects=True, vmem_limit_bytes=36 * 1024 * 1024
        ),
        cost_estimate=pl.CostEstimate(flops=9 * 10**8, bytes_accessed=10**7, transcendentals=0),
    )(
        *[
            pltpu.with_memory_space_constraint(a, pltpu.HBM)
            for a in (
                delta_codes, delta_exps, old_weight, state_in, x_in, z_in, b_in, c_in,
                jnp.swapaxes(dt_in, 1, 2), *vectors,
            )
        ]
    )
    mixed, final_state = pl.pallas_call(
        finish_kernel,
        out_shape=(
            jax.ShapeDtypeStruct((STEPS, ROWS, LOCAL), BF16),
            jax.ShapeDtypeStruct(state_in.shape, F32),
        ),
        in_specs=[vmem] * 3,
        out_specs=(vmem, hbm),
        scratch_shapes=[dma((4,))],
        compiler_params=pltpu.CompilerParams(vmem_limit_bytes=36 * 1024 * 1024),
        cost_estimate=pl.CostEstimate(flops=10**6, bytes_accessed=7 * 10**6, transcendentals=0),
    )(held, sums, squares)
    return mixed, final_state


def solution(mesh):
    return jax.shard_map(
        local,
        mesh=mesh,
        in_specs=(
            P(None, "tp"),
            P(("grp", "tp"), None),
            P(("grp", "tp"), None),
            P("grp", "tp", None, None),
            P(None, "grp", "tp"),
            P(None, "grp", "tp"),
            P(None, "grp", None),
            P(None, "grp", None),
            P(None, "grp", "tp"),
            P("tp"),
            P("tp"),
            P("tp"),
            P("tp"),
        ),
        out_specs=(P(None, "grp", "tp"), P("grp", "tp", None, None)),
        check_vma=False,
    )
```

```python
import functools

import jax
import jax.numpy as jnp
from jax import lax
from jax.experimental import pallas as pl
from jax.experimental.pallas import tpu as pltpu
from jax.sharding import PartitionSpec as P

MESH = pl.DeviceIdType.MESH
F32 = jnp.float32
BF16 = jnp.bfloat16
STEPS = 4
ROWS = 24
ALL = STEPS * ROWS
LOCAL = 512
STATE = 128
GROUP_WIDTH = 2048
CHUNKS = 3
CHUNK_ROWS = ROWS // CHUNKS
SENT_ROWS = STEPS * CHUNK_ROWS
HEADS = 8
CONTRACT_LAST = (((1,), (1,)), ((), ()))
CONTRACT_FIRST = (((0,), (0,)), ((), ()))


def split3(value):
    first = value.astype(BF16)
    rest = value - first.astype(F32)
    second = rest.astype(BF16)
    third = (rest - second.astype(F32)).astype(BF16)
    return first, second, third


def expand_heads(value, spread):
    parts = split3(value)
    total = jnp.dot(parts[2], spread, preferred_element_type=F32)
    total = total + jnp.dot(parts[1], spread, preferred_element_type=F32)
    return total + jnp.dot(parts[0], spread, preferred_element_type=F32)


def put(ref, first, value):
    for j in range(value.shape[1] // 128):
        ref[j, first:first + value.shape[0], :] = value[:, j * 128:(j + 1) * 128]


def pick_rows(ref, row, count):
    return jnp.concatenate(
        [ref[j, pl.ds(row, count, stride=ROWS), :] for j in range(ref.shape[0])], axis=1
    )


UNROLL = 8
PART_ORDER = ((1, 0), (1, 1), (3, 0), (3, 1), (2, 0), (2, 1), (0, 0), (0, 1))
OFFSETS = ((2, 0), (0, 1), (1, 0), (3, 1), (3, 0), (1, 1), (2, 1), (0, 0))
GATHER = ((0, 1), (0, 3), (0, 2), (1, 0), (1, 1), (1, 3), (1, 2))
OWN_PLANE = (0, 1, 2, 3)
OTHER_PLANE = (4, 5, 6)


def mix_kernel(
    codes_ref, exps_ref, old_ref, state_ref, x_ref, z_ref, b_ref, c_ref, dt_ref,
    bias_ref, rate_ref, skip_ref, gain_ref,
    held, sums, squares,
    exps, xs_in, zs_in, bs_in, cs_in, dts_in, bias_in, rate_in, skip_in, gain_in,
    left_rows, right_rows, read_rows, read_state, decay_rows, direct_rows, square_rows,
    codes, delta, weight, arrived, acts, parts, own_square, near_squares,
    small_sem, state_sem, codes_sem, own_sem, old_send, old_recv, delta_send, delta_recv,
    act_send, act_recv, fwd_send, fwd_recv, part_send, part_recv, square_send, square_recv,
):
    grp, tp = lax.axis_index("grp"), lax.axis_index("tp")
    z_lo, x = grp // 4, grp % 4
    y, z_hi, core = tp // 4, (tp // 2) % 2, tp % 2
    other = 1 - core
    chip = tp // 2
    partner = (grp, tp - core + other)
    mine = chip == grp
    crossed = chip == (1 - z_lo) * 4 + x

    def place(lo, xx, yy, hi, cc):
        return (lo * 4 + xx, yy * 4 + hi * 2 + cc)

    for k in range(8):
        dy, dz = OFFSETS[k]
        column = ((y + dy) % 4) * 2 + (z_hi + dz) % 2
        pltpu.make_async_copy(
            codes_ref.at[:, pl.ds(pl.multiple_of(column * 1024, 1024), 1024)], codes.at[k], codes_sem.at[k]
        ).start()

    small = [
        (exps_ref, exps), (dt_ref, dts_in), (bias_ref, bias_in), (rate_ref, rate_in), (skip_ref, skip_in),
        (x_ref, xs_in), (b_ref, bs_in), (c_ref, cs_in), (z_ref, zs_in), (gain_ref, gain_in),
    ]

    def small_copy(k):
        return pltpu.make_async_copy(small[k][0], small[k][1], small_sem.at[k])

    def state_copy(c):
        span = pl.ds(c * CHUNK_ROWS, CHUNK_ROWS)
        return pltpu.make_async_copy(state_ref.at[span], held.at[span], state_sem.at[c])

    for k in range(len(small)):
        small_copy(k).start()

    barrier = pltpu.get_barrier_semaphore()

    def greet(where):
        pl.semaphore_signal(barrier, inc=1, device_id=where, device_id_type=MESH)

    greet(partner)
    for cc in range(2):
        for yl in range(2):
            for dz in range(2):
                where = place((z_lo + dz) % 2, x, 2 * core + yl, (z_hi + dz) % 2, cc)
                if dz == 0:
                    @pl.when(jnp.logical_not((cc == core) & (2 * core + yl == y)))
                    def _():
                        greet(where)
                else:
                    greet(where)
    for dl, dx in GATHER[:6]:
        greet(((z_lo + dl) % 2 * 4 + (x + dx) % 4, tp))
    for cc in range(2):
        greet(place(z_lo, x, y, 1 - z_hi, (core + cc) % 2))
    for dy in range(1, 4):
        greet(place(z_lo, x, (y + dy) % 4, z_hi, core))
    for lo in range(2):
        for yy in range(4):
            for hi in range(2):
                where = place(lo, chip % 4, yy, hi, core)

                @pl.when(jnp.logical_not((where[0] == grp) & (where[1] == tp)))
                def _():
                    greet(where)
    own_delta = core == y // 2
    expected = (
        1 + 8 - own_delta.astype(jnp.int32) + 6 + 2 + 3 + 16 - mine.astype(jnp.int32) - crossed.astype(jnp.int32)
    )
    own_lanes = pl.ds(pl.multiple_of(core * LOCAL, LOCAL), LOCAL)

    def act_copy(c, k):
        dl, dx = GATHER[k]
        slot, where = grp, ((z_lo + dl) % 2 * 4 + (x + dx) % 4, tp)
        if k == 6:
            slot, where = z_lo * 4 + (x + 2) % 4, ((z_lo + 1) % 2 * 4 + x, tp)
        piece = acts.at[slot, pl.ds(c * SENT_ROWS, SENT_ROWS), own_lanes]
        return pltpu.make_async_remote_copy(
            src_ref=piece, dst_ref=piece,
            send_sem=act_send, recv_sem=act_recv.at[c * 7 + k],
            device_id=where, device_id_type=MESH,
        )

    def fwd_copy(c, k):
        slot = grp
        if k < 7:
            dl, dx = GATHER[k]
            slot = (z_lo + dl) % 2 * 4 + (x + 4 - dx) % 4
        piece = acts.at[slot, pl.ds(c * SENT_ROWS, SENT_ROWS), own_lanes]
        return pltpu.make_async_remote_copy(
            src_ref=piece, dst_ref=piece,
            send_sem=fwd_send, recv_sem=fwd_recv.at[0 if k in (7, 0, 1, 2) else 1],
            device_id=partner, device_id_type=MESH,
        )

    def square_copy(k):
        if k < 3:
            other_chip, other_core = ((0, 1), (1, 0), (1, 1))[k]
            where = place(z_lo, x, y, (z_hi + other_chip) % 2, (core + other_core) % 2)
            source, target = own_square, near_squares.at[k]
        else:
            where = place(z_lo, x, (y + k - 2) % 4, z_hi, core)
            source = target = squares.at[y]
        return pltpu.make_async_remote_copy(
            src_ref=source, dst_ref=target,
            send_sem=square_send.at[k], recv_sem=square_recv.at[k],
            device_id=where, device_id_type=MESH,
        )

    def feature_row(slab, cc):
        dz, yl = slab // 2, slab % 2
        lo, hi = (z_lo + dz) % 2, (z_hi + dz) % 2
        row = ((lo * 4 + x) * 2 + cc) * 512 + yl * 256 + hi * 128
        return pl.ds(pl.multiple_of(row, 128), 128)

    def own_copy(slab):
        return pltpu.make_async_copy(
            old_ref.at[feature_row(slab, core)],
            weight.at[pl.ds(slab * 128, 128), pl.ds(pl.multiple_of(core * LOCAL, LOCAL), LOCAL)],
            own_sem,
        )

    def old_copy(slab):
        return pltpu.make_async_remote_copy(
            src_ref=old_ref.at[feature_row(slab, other)],
            dst_ref=weight.at[pl.ds(slab * 128, 128), pl.ds(pl.multiple_of(core * LOCAL, LOCAL), LOCAL)],
            send_sem=old_send, recv_sem=old_recv,
            device_id=partner, device_id_type=MESH,
        )

    def delta_copy(k, half):
        dy, dz = OFFSETS[k]
        slot = half * 8 + dz * 4 + (y % 2) * 2 + core
        return pltpu.make_async_remote_copy(
            src_ref=delta.at[k, pl.ds(half * 32, 32)], dst_ref=arrived.at[pl.ds(pl.multiple_of(slot * 32, 32), 32)],
            send_sem=delta_send.at[0 if k < 7 else 1 + half], recv_sem=delta_recv.at[half],
            device_id=place((z_lo + dz) % 2, x, (y + dy) % 4, (z_hi + dz) % 2, y // 2), device_id_type=MESH,
        )

    def delta_self(half):
        slot = half * 8 + (y % 2) * 2 + core
        return pltpu.make_async_copy(
            delta.at[7, pl.ds(half * 32, 32)], arrived.at[pl.ds(pl.multiple_of(slot * 32, 32), 32)],
            delta_recv.at[half],
        )

    small_copy(0).wait()
    scale = jnp.where(
        exps[...] == -14, 2.0**-14, jnp.where(exps[...] == -13, 2.0**-13, 2.0**-12)
    ).astype(BF16)
    block_at = lax.broadcasted_iota(jnp.int32, (64, 1024), 0)
    lane_block = lax.broadcasted_iota(jnp.int32, (64, 1024), 1) // 128
    for k in range(8):
        dy, dz = OFFSETS[k]
        column = ((y + dy) % 4) * 2 + (z_hi + dz) % 2
        pltpu.make_async_copy(codes.at[k], codes.at[k], codes_sem.at[k]).wait()
        if k == 3:
            for c in range(CHUNKS):
                state_copy(c).start()
        pick = (block_at == lane_block + column * 8).astype(BF16)
        wide = jnp.dot(scale, pick, preferred_element_type=F32)
        delta[k] = (codes[k].astype(F32) * wide).astype(BF16)

    for k in range(1, len(small)):
        small_copy(k).wait()
    group = tp // 4
    group_lanes = pl.ds(pl.multiple_of(group * STATE, STATE), STATE)
    head_of = lax.broadcasted_iota(jnp.int32, (HEADS, LOCAL), 1) // (LOCAL // HEADS)
    spread = (head_of == lax.broadcasted_iota(jnp.int32, (HEADS, LOCAL), 0)).astype(BF16)
    bias = expand_heads(jnp.broadcast_to(bias_in[...], (8, HEADS)), spread)[0:1]
    rate = expand_heads(jnp.broadcast_to(rate_in[...], (8, HEADS)), spread)[0:1]
    skip = expand_heads(jnp.broadcast_to(skip_in[...], (8, HEADS)), spread)[0:1]
    sizes, logs = [], []
    for s in range(STEPS):
        raw = lax.dot_general(dts_in[s], spread, CONTRACT_FIRST, preferred_element_type=F32) + bias
        sizes.append(jnp.maximum(raw, 0.0) + jnp.log1p(jnp.exp(-jnp.abs(raw))))
        own = sizes[s] * rate
        logs.append(own if s == 0 else logs[-1] + own)
    xs = [xs_in[s].astype(F32) for s in range(STEPS)]
    bs = [bs_in[s, :, group_lanes].astype(F32) for s in range(STEPS)]
    cs = [cs_in[s, :, group_lanes].astype(F32) for s in range(STEPS)]
    right_rows[...] = jnp.zeros(right_rows.shape, F32)
    read_rows[...] = jnp.zeros(read_rows.shape, F32)
    for s in range(STEPS):
        right_rows[0, s * ROWS:(s + 1) * ROWS, :] = bs[s]
        right_rows[0, (4 + s) * ROWS:(5 + s) * ROWS, :] = bs[s]
        read_rows[0, s * ROWS:(s + 1) * ROWS, :] = cs[s]
    right_rows[1, 8 * ROWS:11 * ROWS, :] = jnp.ones((3 * ROWS, STATE), F32)
    for s in range(STEPS):
        decay_rows[s * ROWS:(s + 1) * ROWS, :] = jnp.exp(-logs[s])
        direct = skip * xs[s]
        for u in range(s + 1):
            coef = sizes[u] if u == s else sizes[u] * jnp.exp(logs[u] - logs[s])
            term = coef * xs[u]
            direct = direct + term * jnp.sum(bs[u] * cs[s], axis=1, keepdims=True)
            if s == STEPS - 1:
                high = term.astype(BF16).astype(F32)
                put(left_rows, u * ROWS, high)
                put(left_rows, (4 + u) * ROWS, term - high)
        direct_rows[s * ROWS:(s + 1) * ROWS, :] = direct
    last = decay_rows[3 * ROWS:4 * ROWS, :]
    for at_row, part in enumerate(split3(last)):
        put(left_rows, (8 + at_row) * ROWS, part.astype(F32))
    put(left_rows, 11 * ROWS, jnp.zeros((5 * ROWS, LOCAL), F32))
    square_rows[ALL:, :] = jnp.zeros((128 - ALL, 128), F32)

    pl.semaphore_wait(barrier, expected)
    for k in range(7):
        delta_copy(k, 0).start()

    def read_one(row):
        value = held[row].reshape(LOCAL, STATE)
        high = value.astype(BF16)
        low = (value - high.astype(F32)).astype(BF16)
        both = jnp.concatenate([high, low], axis=1)
        reader = pick_rows(read_rows, row, 8).astype(BF16)
        reader = jnp.concatenate([reader, reader], axis=1)
        read = lax.dot_general(reader, both, CONTRACT_LAST, preferred_element_type=F32)
        for j in range(LOCAL // 128):
            read_state[j, pl.ds(row, 8, stride=ROWS), :] = read[:, j * 128:(j + 1) * 128]

    def update_one(row):
        left = pick_rows(left_rows, row, 16).astype(BF16)
        right = pick_rows(right_rows, row, 16).astype(BF16)
        update = lax.dot_general(left, right, CONTRACT_FIRST, preferred_element_type=F32)
        value = held[row].reshape(LOCAL, STATE)
        held[row] = (update[:, STATE:] * value + update[:, :STATE]).reshape(held.shape[1:])

    def over_rows(first, count, unroll, one):
        def some(i, carry):
            for j in range(unroll):
                one(first + i * unroll + j)
            return carry

        lax.fori_loop(0, count // unroll, some, 0)

    for c in range(CHUNKS):
        state_copy(c).wait()
        over_rows(c * CHUNK_ROWS, CHUNK_ROWS, UNROLL, read_one)
        pieces = []
        for s in range(STEPS):
            span = slice(s * ROWS + c * CHUNK_ROWS, s * ROWS + (c + 1) * CHUNK_ROWS)
            read = jnp.concatenate([read_state[j, span, :] for j in range(LOCAL // 128)], axis=1)
            z = zs_in[s].astype(F32)[c * CHUNK_ROWS:(c + 1) * CHUNK_ROWS]
            read_out = decay_rows[span, :] * read + direct_rows[span, :]
            pieces.append(read_out * (z / (1.0 + jnp.exp(-z))))
        gated = jnp.concatenate(pieces, axis=0)
        acts[grp, c * SENT_ROWS:(c + 1) * SENT_ROWS, own_lanes] = (gated * gain_in[...]).astype(BF16)
        for k in range(6):
            act_copy(c, k).start()
        fwd_copy(c, 7).start()
        total = jnp.sum(gated * gated, axis=1, keepdims=True)
        square_rows[c * SENT_ROWS:(c + 1) * SENT_ROWS, :] = jnp.broadcast_to(total, (SENT_ROWS, 128))
    @pl.when(own_delta)
    def _():
        for half in range(2):
            delta_self(half).start()

    @pl.when(jnp.logical_not(own_delta))
    def _():
        for half in range(2):
            delta_copy(7, half).start()

    for k in range(7):
        delta_copy(k, 1).start()
    for slab in range(4):
        own_copy(slab).start()
        old_copy(slab).start()

    own_square[...] = jnp.transpose(square_rows[...])[0:8]
    for k in range(3):
        square_copy(k).start()

    over_rows(0, ROWS, UNROLL, update_one)
    for c in range(CHUNKS):
        for k in OWN_PLANE:
            act_copy(c, k).wait_recv()
            fwd_copy(c, k).start()
            if k == 2:
                act_copy(c, 6).start()

    def part_copy(half, plane, dz, dx):
        i = (x + dx) % 4
        g = (z_lo + plane) % 2 * 4 + i
        alone = 1 + half * 2 + dz if plane == 0 and dx == 0 else 0
        dest = (g, ((z_lo + dz) % 2 * 4 + x) * 2 + core)
        at = ((half * 2 + plane) * 2 + dz) * 4 + i
        slot = (half * 2 + (z_hi + dz) % 2) * 8 + y * 2 + dz
        remote = lambda: pltpu.make_async_remote_copy(
            src_ref=parts.at[at], dst_ref=sums.at[slot],
            send_sem=part_send.at[alone], recv_sem=part_recv,
            device_id=dest, device_id_type=MESH,
        )
        local = lambda: pltpu.make_async_copy(parts.at[at], sums.at[slot], part_recv)
        here = (dest[0] == grp) & (dest[1] == tp)
        return remote, local, here

    for which, sem in ((core, own_sem), (other, old_recv)):
        rows = weight.at[:, pl.ds(pl.multiple_of(which * LOCAL, LOCAL), LOCAL)]
        pltpu.make_async_copy(rows, rows, sem).wait()
    for half in range(2):
        rows = arrived.at[pl.ds(half * 256, 256)]
        pltpu.make_async_copy(rows, rows, delta_recv.at[half]).wait()
        fresh = []
        for q in range(8):
            first = q * 64 + half * 32
            coming = half * 256 + q * 32
            fresh.append(
                (weight[first:first + 32, :].astype(F32) + arrived[coming:coming + 32, :].astype(F32)).astype(BF16)
            )
        fresh = jnp.concatenate(fresh, axis=0)
        for plane in range(2):
            if half == 0:
                if plane == 1:
                    for c in range(CHUNKS):
                        for k in OTHER_PLANE:
                            act_copy(c, k).wait_recv()
                            fwd_copy(c, k).start()
                other_lanes = pl.ds(pl.multiple_of(other * LOCAL, LOCAL), LOCAL)
                rows = acts.at[pl.ds((z_lo + plane) % 2 * 4, 4), :, other_lanes]
                pltpu.make_async_copy(rows, rows, fwd_recv.at[plane]).wait()
            for pair in range(1):
                start = (z_lo + plane) % 2 * 4
                lhs = acts[pl.ds(start, 4)].reshape(4 * ALL, 1024)
                got = lax.dot_general(lhs, fresh, CONTRACT_LAST, preferred_element_type=F32)
                for part in range(4):
                    for dz in range(2):
                        at = ((half * 2 + plane) * 2 + dz) * 4 + part
                        parts[at] = got[part * ALL:(part + 1) * ALL, dz * 128:dz * 128 + 128].astype(BF16)
                for dx, dz in PART_ORDER:
                    remote, local, here = part_copy(half, plane, dz, dx)
                    if plane == 1 or dx > 0:
                        remote().start()
                        continue

                    @pl.when(here)
                    def _():
                        local().start()

                    @pl.when(jnp.logical_not(here))
                    def _():
                        remote().start()

    for k in range(3):
        square_copy(k).wait_recv()
    squares[y] = own_square[...] + near_squares[0] + near_squares[1] + near_squares[2]
    for k in range(3, 6):
        square_copy(k).start()
    for k in range(3, 6):
        square_copy(k).wait_recv()
    pltpu.make_async_copy(delta.at[pl.ds(0, 7)], delta.at[pl.ds(0, 7)], delta_send.at[0]).wait()
    for count, sem in ((7, act_send), (8, fwd_send)):
        rows = acts.at[pl.ds(0, count), :, own_lanes]
        pltpu.make_async_copy(rows, rows, sem).wait()

    @pl.when(jnp.logical_not(own_delta))
    def _():
        for half in range(2):
            delta_copy(7, half).wait_send()
    rows = weight.at[:, own_lanes]
    pltpu.make_async_copy(rows, rows, old_send).wait()
    for k in range(6):
        square_copy(k).wait_send()
    pltpu.make_async_copy(parts.at[pl.ds(0, 28)], parts.at[pl.ds(0, 28)], part_send.at[0]).wait()
    for half in range(2):
        for dz in range(2):
            remote, _, here = part_copy(half, 0, dz, 0)

            @pl.when(jnp.logical_not(here))
            def _():
                remote().wait_send()
    pltpu.make_async_copy(sums, sums, part_recv).wait()


def finish_kernel(held, sums, squares, out_ref, final_ref, sem):
    copies = [
        pltpu.make_async_copy(held.at[pl.ds(c * 6, 6)], final_ref.at[pl.ds(c * 6, 6)], sem.at[c])
        for c in range(4)
    ]
    for copy in copies:
        copy.start()
    factors = []
    for yy in range(4):
        inverse = lax.rsqrt(squares[yy] * (1.0 / GROUP_WIDTH) + 1e-05)
        factors.append(jnp.transpose(jnp.concatenate([inverse] * 16, axis=0))[0:ALL, 0:1])
    lane = lax.broadcasted_iota(jnp.int32, (256, 256), 1)
    source = (lane // 32) % 2 * 128 + lane // 128 * 64 + (lane // 64) % 2 * 32 + lane % 32
    order = (lax.broadcasted_iota(jnp.int32, (256, 256), 0) == source).astype(BF16)
    for hi in range(2):
        totals = []
        for half in range(2):
            total = None
            for yy in range(4):
                slot = (half * 2 + hi) * 8 + yy * 2
                pair = (sums[slot].astype(F32) + sums[slot + 1].astype(F32)) * factors[yy]
                total = pair if total is None else total + pair
            totals.append(total.astype(BF16))
        total = jnp.dot(jnp.concatenate(totals, axis=1), order, preferred_element_type=F32)
        for s in range(STEPS):
            rows = jnp.concatenate(
                [
                    total[c * SENT_ROWS + s * CHUNK_ROWS:c * SENT_ROWS + (s + 1) * CHUNK_ROWS]
                    for c in range(CHUNKS)
                ],
                axis=0,
            ).astype(BF16)
            for yl in range(2):
                at = yl * 256 + hi * 128
                out_ref[s, :, at:at + 128] = rows[:, yl * 128:(yl + 1) * 128]
    for copy in copies:
        copy.wait()


def local(
    old_weight, delta_codes, delta_exps, state_in, x_in, z_in, b_in, c_in, dt_in,
    dt_bias, a_rate, skip_gain, norm_gain,
):
    vmem = pl.BlockSpec(memory_space=pltpu.VMEM)
    hbm = pl.BlockSpec(memory_space=pltpu.HBM)
    dma = pltpu.SemaphoreType.DMA
    vectors = [v.reshape(1, -1) for v in (dt_bias, a_rate, skip_gain, norm_gain)]
    held, sums, squares = pl.pallas_call(
        mix_kernel,
        out_shape=(
            pltpu.VMEM(state_in.shape, F32),
            pltpu.VMEM((32, ALL, 128), BF16),
            pltpu.VMEM((4, 8, 128), F32),
        ),
        in_specs=[hbm] * 13,
        out_specs=(vmem, vmem, vmem),
        scratch_shapes=[
            pltpu.VMEM((64, 64), jnp.int32),
            pltpu.VMEM(x_in.shape, BF16),
            pltpu.VMEM(x_in.shape, BF16),
            pltpu.VMEM(b_in.shape, BF16),
            pltpu.VMEM(b_in.shape, BF16),
            pltpu.VMEM((STEPS, HEADS, ROWS), BF16),
            pltpu.VMEM((1, HEADS), F32),
            pltpu.VMEM((1, HEADS), F32),
            pltpu.VMEM((1, HEADS), F32),
            pltpu.VMEM((1, LOCAL), F32),
            pltpu.VMEM((LOCAL // 128, 16 * ROWS, 128), F32),
            pltpu.VMEM((2, 16 * ROWS, STATE), F32),
            pltpu.VMEM((1, 8 * ROWS, STATE), F32),
            pltpu.VMEM((LOCAL // 128, 8 * ROWS, 128), F32),
            pltpu.VMEM((ALL, LOCAL), F32),
            pltpu.VMEM((ALL, LOCAL), F32),
            pltpu.VMEM((128, 128), F32),
            pltpu.VMEM((8, 64, 1024), jnp.int32),
            pltpu.VMEM((8, 64, 1024), BF16),
            pltpu.VMEM((512, 1024), BF16),
            pltpu.VMEM((512, 1024), BF16),
            pltpu.VMEM((8, ALL, 1024), BF16),
            pltpu.VMEM((32, ALL, 128), BF16),
            pltpu.VMEM((8, 128), F32),
            pltpu.VMEM((3, 8, 128), F32),
            dma((10,)), dma((CHUNKS,)), dma((8,)), dma, dma, dma, dma((3,)), dma((2,)),
            dma, dma((7 * CHUNKS,)), dma, dma((2,)),
            dma((5,)), dma, dma((6,)), dma((6,)),
        ],
        compiler_params=pltpu.CompilerParams(
            collective_id=0, has_side_effects=True, vmem_limit_bytes=36 * 1024 * 1024
        ),
        cost_estimate=pl.CostEstimate(flops=9 * 10**8, bytes_accessed=10**7, transcendentals=0),
    )(
        *[
            pltpu.with_memory_space_constraint(a, pltpu.HBM)
            for a in (
                delta_codes, delta_exps, old_weight, state_in, x_in, z_in, b_in, c_in,
                jnp.swapaxes(dt_in, 1, 2), *vectors,
            )
        ]
    )
    mixed, final_state = pl.pallas_call(
        finish_kernel,
        out_shape=(
            jax.ShapeDtypeStruct((STEPS, ROWS, LOCAL), BF16),
            jax.ShapeDtypeStruct(state_in.shape, F32),
        ),
        in_specs=[vmem] * 3,
        out_specs=(vmem, hbm),
        scratch_shapes=[dma((4,))],
        compiler_params=pltpu.CompilerParams(vmem_limit_bytes=36 * 1024 * 1024),
        cost_estimate=pl.CostEstimate(flops=10**6, bytes_accessed=7 * 10**6, transcendentals=0),
    )(held, sums, squares)
    return mixed, final_state


def solution(mesh):
    return jax.shard_map(
        local,
        mesh=mesh,
        in_specs=(
            P(None, "tp"),
            P(("grp", "tp"), None),
            P(("grp", "tp"), None),
            P("grp", "tp", None, None),
            P(None, "grp", "tp"),
            P(None, "grp", "tp"),
            P(None, "grp", None),
            P(None, "grp", None),
            P(None, "grp", "tp"),
            P("tp"),
            P("tp"),
            P("tp"),
            P("tp"),
        ),
        out_specs=(P(None, "grp", "tp"), P("grp", "tp", None, None)),
        check_vma=False,
    )
```

```python
import functools

import jax
import jax.numpy as jnp
from jax import lax
from jax.experimental import pallas as pl
from jax.experimental.pallas import tpu as pltpu
from jax.sharding import PartitionSpec as P

MESH = pl.DeviceIdType.MESH
F32 = jnp.float32
BF16 = jnp.bfloat16
STEPS = 4
ROWS = 24
ALL = STEPS * ROWS
LOCAL = 512
STATE = 128
GROUP_WIDTH = 2048
CHUNKS = 3
CHUNK_ROWS = ROWS // CHUNKS
SENT_ROWS = STEPS * CHUNK_ROWS
HEADS = 8
CONTRACT_LAST = (((1,), (1,)), ((), ()))
CONTRACT_FIRST = (((0,), (0,)), ((), ()))


def split3(value):
    first = value.astype(BF16)
    rest = value - first.astype(F32)
    second = rest.astype(BF16)
    third = (rest - second.astype(F32)).astype(BF16)
    return first, second, third


def expand_heads(value, spread):
    parts = split3(value)
    total = jnp.dot(parts[2], spread, preferred_element_type=F32)
    total = total + jnp.dot(parts[1], spread, preferred_element_type=F32)
    return total + jnp.dot(parts[0], spread, preferred_element_type=F32)


def put(ref, first, value):
    for j in range(value.shape[1] // 128):
        ref[j, first:first + value.shape[0], :] = value[:, j * 128:(j + 1) * 128]


def pick_rows(ref, row, count):
    return jnp.concatenate(
        [ref[j, pl.ds(row, count, stride=ROWS), :] for j in range(ref.shape[0])], axis=1
    )


UNROLL = 8
PART_ORDER = ((1, 0), (1, 1), (3, 0), (3, 1), (2, 0), (2, 1), (0, 0), (0, 1))
OFFSETS = ((2, 0), (0, 1), (1, 0), (3, 1), (3, 0), (1, 1), (2, 1), (0, 0))
GATHER = ((0, 1), (0, 3), (0, 2), (1, 0), (1, 1), (1, 3), (1, 2))
OWN_PLANE = (0, 1, 2, 3)
OTHER_PLANE = (4, 5, 6)


def mix_kernel(
    codes_ref, exps_ref, old_ref, state_ref, x_ref, z_ref, b_ref, c_ref, dt_ref,
    bias_ref, rate_ref, skip_ref, gain_ref,
    held, sums, squares,
    exps, xs_in, zs_in, bs_in, cs_in, dts_in, bias_in, rate_in, skip_in, gain_in,
    left_rows, right_rows, read_rows, read_state, decay_rows, direct_rows, square_rows,
    codes, delta, weight, arrived, acts, parts, own_square, near_squares,
    small_sem, state_sem, codes_sem, own_sem, old_send, old_recv, delta_send, delta_recv,
    act_send, act_recv, fwd_send, fwd_recv, part_send, part_recv, square_send, square_recv,
):
    grp, tp = lax.axis_index("grp"), lax.axis_index("tp")
    z_lo, x = grp // 4, grp % 4
    y, z_hi, core = tp // 4, (tp // 2) % 2, tp % 2
    other = 1 - core
    chip = tp // 2
    partner = (grp, tp - core + other)
    mine = chip == grp
    crossed = chip == (1 - z_lo) * 4 + x

    def place(lo, xx, yy, hi, cc):
        return (lo * 4 + xx, yy * 4 + hi * 2 + cc)

    for k in range(8):
        dy, dz = OFFSETS[k]
        column = ((y + dy) % 4) * 2 + (z_hi + dz) % 2
        pltpu.make_async_copy(
            codes_ref.at[:, pl.ds(pl.multiple_of(column * 1024, 1024), 1024)], codes.at[k], codes_sem.at[k]
        ).start()

    small = [
        (exps_ref, exps), (dt_ref, dts_in), (bias_ref, bias_in), (rate_ref, rate_in), (skip_ref, skip_in),
        (x_ref, xs_in), (b_ref, bs_in), (c_ref, cs_in), (z_ref, zs_in), (gain_ref, gain_in),
    ]

    def small_copy(k):
        return pltpu.make_async_copy(small[k][0], small[k][1], small_sem.at[k])

    def state_copy(c):
        span = pl.ds(c * CHUNK_ROWS, CHUNK_ROWS)
        return pltpu.make_async_copy(state_ref.at[span], held.at[span], state_sem.at[c])

    for k in range(len(small)):
        small_copy(k).start()

    barrier = pltpu.get_barrier_semaphore()

    def greet(where):
        pl.semaphore_signal(barrier, inc=1, device_id=where, device_id_type=MESH)

    greet(partner)
    for cc in range(2):
        for yl in range(2):
            for dz in range(2):
                where = place((z_lo + dz) % 2, x, 2 * core + yl, (z_hi + dz) % 2, cc)
                if dz == 0:
                    @pl.when(jnp.logical_not((cc == core) & (2 * core + yl == y)))
                    def _():
                        greet(where)
                else:
                    greet(where)
    for dl, dx in GATHER[:6]:
        greet(((z_lo + dl) % 2 * 4 + (x + dx) % 4, tp))
    for cc in range(2):
        greet(place(z_lo, x, y, 1 - z_hi, (core + cc) % 2))
    for dy in range(1, 4):
        greet(place(z_lo, x, (y + dy) % 4, z_hi, core))
    for lo in range(2):
        for yy in range(4):
            for hi in range(2):
                where = place(lo, chip % 4, yy, hi, core)

                @pl.when(jnp.logical_not((where[0] == grp) & (where[1] == tp)))
                def _():
                    greet(where)
    own_delta = core == y // 2
    expected = (
        1 + 8 - own_delta.astype(jnp.int32) + 6 + 2 + 3 + 16 - mine.astype(jnp.int32) - crossed.astype(jnp.int32)
    )
    own_lanes = pl.ds(pl.multiple_of(core * LOCAL, LOCAL), LOCAL)

    def act_copy(c, k):
        dl, dx = GATHER[k]
        slot, where = grp, ((z_lo + dl) % 2 * 4 + (x + dx) % 4, tp)
        if k == 6:
            slot, where = z_lo * 4 + (x + 2) % 4, ((z_lo + 1) % 2 * 4 + x, tp)
        piece = acts.at[slot, pl.ds(c * SENT_ROWS, SENT_ROWS), own_lanes]
        return pltpu.make_async_remote_copy(
            src_ref=piece, dst_ref=piece,
            send_sem=act_send, recv_sem=act_recv.at[c * 7 + k],
            device_id=where, device_id_type=MESH,
        )

    def fwd_copy(c, k):
        slot = grp
        if k < 7:
            dl, dx = GATHER[k]
            slot = (z_lo + dl) % 2 * 4 + (x + 4 - dx) % 4
        piece = acts.at[slot, pl.ds(0, ALL) if c is None else pl.ds(c * SENT_ROWS, SENT_ROWS), own_lanes]
        return pltpu.make_async_remote_copy(
            src_ref=piece, dst_ref=piece,
            send_sem=fwd_send, recv_sem=fwd_recv.at[0 if k in (7, 0, 1, 2) else 1],
            device_id=partner, device_id_type=MESH,
        )

    def square_copy(k):
        if k < 3:
            other_chip, other_core = ((0, 1), (1, 0), (1, 1))[k]
            where = place(z_lo, x, y, (z_hi + other_chip) % 2, (core + other_core) % 2)
            source, target = own_square, near_squares.at[k]
        else:
            where = place(z_lo, x, (y + k - 2) % 4, z_hi, core)
            source = target = squares.at[y]
        return pltpu.make_async_remote_copy(
            src_ref=source, dst_ref=target,
            send_sem=square_send.at[k], recv_sem=square_recv.at[k],
            device_id=where, device_id_type=MESH,
        )

    def feature_row(slab, cc):
        dz, yl = slab // 2, slab % 2
        lo, hi = (z_lo + dz) % 2, (z_hi + dz) % 2
        row = ((lo * 4 + x) * 2 + cc) * 512 + yl * 256 + hi * 128
        return pl.ds(pl.multiple_of(row, 128), 128)

    def own_copy(slab):
        return pltpu.make_async_copy(
            old_ref.at[feature_row(slab, core)],
            weight.at[pl.ds(slab * 128, 128), pl.ds(pl.multiple_of(core * LOCAL, LOCAL), LOCAL)],
            own_sem,
        )

    def old_copy(slab):
        return pltpu.make_async_remote_copy(
            src_ref=old_ref.at[feature_row(slab, other)],
            dst_ref=weight.at[pl.ds(slab * 128, 128), pl.ds(pl.multiple_of(core * LOCAL, LOCAL), LOCAL)],
            send_sem=old_send, recv_sem=old_recv,
            device_id=partner, device_id_type=MESH,
        )

    def delta_copy(k, half):
        dy, dz = OFFSETS[k]
        slot = half * 8 + dz * 4 + (y % 2) * 2 + core
        return pltpu.make_async_remote_copy(
            src_ref=delta.at[k, pl.ds(half * 32, 32)], dst_ref=arrived.at[pl.ds(pl.multiple_of(slot * 32, 32), 32)],
            send_sem=delta_send.at[0 if k < 7 else 1 + half], recv_sem=delta_recv.at[half],
            device_id=place((z_lo + dz) % 2, x, (y + dy) % 4, (z_hi + dz) % 2, y // 2), device_id_type=MESH,
        )

    def delta_self(half):
        slot = half * 8 + (y % 2) * 2 + core
        return pltpu.make_async_copy(
            delta.at[7, pl.ds(half * 32, 32)], arrived.at[pl.ds(pl.multiple_of(slot * 32, 32), 32)],
            delta_recv.at[half],
        )

    small_copy(0).wait()
    scale = jnp.where(
        exps[...] == -14, 2.0**-14, jnp.where(exps[...] == -13, 2.0**-13, 2.0**-12)
    ).astype(BF16)
    block_at = lax.broadcasted_iota(jnp.int32, (64, 1024), 0)
    lane_block = lax.broadcasted_iota(jnp.int32, (64, 1024), 1) // 128
    for k in range(8):
        dy, dz = OFFSETS[k]
        column = ((y + dy) % 4) * 2 + (z_hi + dz) % 2
        pltpu.make_async_copy(codes.at[k], codes.at[k], codes_sem.at[k]).wait()
        if k == 3:
            for c in range(CHUNKS):
                state_copy(c).start()
        pick = (block_at == lane_block + column * 8).astype(BF16)
        wide = jnp.dot(scale, pick, preferred_element_type=F32)
        delta[k] = (codes[k].astype(F32) * wide).astype(BF16)

    for k in range(1, len(small)):
        small_copy(k).wait()
    group = tp // 4
    group_lanes = pl.ds(pl.multiple_of(group * STATE, STATE), STATE)
    head_of = lax.broadcasted_iota(jnp.int32, (HEADS, LOCAL), 1) // (LOCAL // HEADS)
    spread = (head_of == lax.broadcasted_iota(jnp.int32, (HEADS, LOCAL), 0)).astype(BF16)
    bias = expand_heads(jnp.broadcast_to(bias_in[...], (8, HEADS)), spread)[0:1]
    rate = expand_heads(jnp.broadcast_to(rate_in[...], (8, HEADS)), spread)[0:1]
    skip = expand_heads(jnp.broadcast_to(skip_in[...], (8, HEADS)), spread)[0:1]
    sizes, logs = [], []
    for s in range(STEPS):
        raw = lax.dot_general(dts_in[s], spread, CONTRACT_FIRST, preferred_element_type=F32) + bias
        sizes.append(jnp.maximum(raw, 0.0) + jnp.log1p(jnp.exp(-jnp.abs(raw))))
        own = sizes[s] * rate
        logs.append(own if s == 0 else logs[-1] + own)
    xs = [xs_in[s].astype(F32) for s in range(STEPS)]
    bs = [bs_in[s, :, group_lanes].astype(F32) for s in range(STEPS)]
    cs = [cs_in[s, :, group_lanes].astype(F32) for s in range(STEPS)]
    right_rows[...] = jnp.zeros(right_rows.shape, F32)
    read_rows[...] = jnp.zeros(read_rows.shape, F32)
    for s in range(STEPS):
        right_rows[0, s * ROWS:(s + 1) * ROWS, :] = bs[s]
        right_rows[0, (4 + s) * ROWS:(5 + s) * ROWS, :] = bs[s]
        read_rows[0, s * ROWS:(s + 1) * ROWS, :] = cs[s]
    right_rows[1, 8 * ROWS:11 * ROWS, :] = jnp.ones((3 * ROWS, STATE), F32)
    for s in range(STEPS):
        decay_rows[s * ROWS:(s + 1) * ROWS, :] = jnp.exp(-logs[s])
        direct = skip * xs[s]
        for u in range(s + 1):
            coef = sizes[u] if u == s else sizes[u] * jnp.exp(logs[u] - logs[s])
            term = coef * xs[u]
            direct = direct + term * jnp.sum(bs[u] * cs[s], axis=1, keepdims=True)
            if s == STEPS - 1:
                high = term.astype(BF16).astype(F32)
                put(left_rows, u * ROWS, high)
                put(left_rows, (4 + u) * ROWS, term - high)
        direct_rows[s * ROWS:(s + 1) * ROWS, :] = direct
    last = decay_rows[3 * ROWS:4 * ROWS, :]
    for at_row, part in enumerate(split3(last)):
        put(left_rows, (8 + at_row) * ROWS, part.astype(F32))
    put(left_rows, 11 * ROWS, jnp.zeros((5 * ROWS, LOCAL), F32))
    square_rows[ALL:, :] = jnp.zeros((128 - ALL, 128), F32)

    for slab in range(4):
        own_copy(slab).start()
    pl.semaphore_wait(barrier, expected)
    for k in range(7):
        delta_copy(k, 0).start()

    def read_one(row):
        value = held[row].reshape(LOCAL, STATE)
        high = value.astype(BF16)
        low = (value - high.astype(F32)).astype(BF16)
        both = jnp.concatenate([high, low], axis=1)
        reader = pick_rows(read_rows, row, 8).astype(BF16)
        reader = jnp.concatenate([reader, reader], axis=1)
        read = lax.dot_general(reader, both, CONTRACT_LAST, preferred_element_type=F32)
        for j in range(LOCAL // 128):
            read_state[j, pl.ds(row, 8, stride=ROWS), :] = read[:, j * 128:(j + 1) * 128]

    def update_one(row):
        left = pick_rows(left_rows, row, 16).astype(BF16)
        right = pick_rows(right_rows, row, 16).astype(BF16)
        update = lax.dot_general(left, right, CONTRACT_FIRST, preferred_element_type=F32)
        value = held[row].reshape(LOCAL, STATE)
        held[row] = (update[:, STATE:] * value + update[:, :STATE]).reshape(held.shape[1:])

    def over_rows(first, count, unroll, one):
        def some(i, carry):
            for j in range(unroll):
                one(first + i * unroll + j)
            return carry

        lax.fori_loop(0, count // unroll, some, 0)

    for c in range(CHUNKS):
        state_copy(c).wait()
        over_rows(c * CHUNK_ROWS, CHUNK_ROWS, UNROLL, read_one)
        pieces = []
        for s in range(STEPS):
            span = slice(s * ROWS + c * CHUNK_ROWS, s * ROWS + (c + 1) * CHUNK_ROWS)
            read = jnp.concatenate([read_state[j, span, :] for j in range(LOCAL // 128)], axis=1)
            z = zs_in[s].astype(F32)[c * CHUNK_ROWS:(c + 1) * CHUNK_ROWS]
            read_out = decay_rows[span, :] * read + direct_rows[span, :]
            pieces.append(read_out * (z / (1.0 + jnp.exp(-z))))
        gated = jnp.concatenate(pieces, axis=0)
        acts[grp, c * SENT_ROWS:(c + 1) * SENT_ROWS, own_lanes] = (gated * gain_in[...]).astype(BF16)
        for k in range(6):
            act_copy(c, k).start()
        fwd_copy(c, 7).start()
        total = jnp.sum(gated * gated, axis=1, keepdims=True)
        square_rows[c * SENT_ROWS:(c + 1) * SENT_ROWS, :] = jnp.broadcast_to(total, (SENT_ROWS, 128))
    @pl.when(own_delta)
    def _():
        for half in range(2):
            delta_self(half).start()

    @pl.when(jnp.logical_not(own_delta))
    def _():
        for half in range(2):
            delta_copy(7, half).start()

    for k in range(7):
        delta_copy(k, 1).start()
    for slab in range(4):
        old_copy(slab).start()

    own_square[...] = jnp.transpose(square_rows[...])[0:8]
    for k in range(3):
        square_copy(k).start()

    over_rows(0, ROWS, UNROLL, update_one)
    for c in range(CHUNKS):
        for k in OWN_PLANE:
            act_copy(c, k).wait_recv()
            fwd_copy(c, k).start()
            if k == 2:
                act_copy(c, 6).start()

    def part_copy(half, plane, dz, dx):
        i = (x + dx) % 4
        g = (z_lo + plane) % 2 * 4 + i
        alone = 1 + half * 2 + dz if plane == 0 and dx == 0 else 0
        dest = (g, ((z_lo + dz) % 2 * 4 + x) * 2 + core)
        at = ((half * 2 + plane) * 2 + dz) * 4 + i
        slot = (half * 2 + (z_hi + dz) % 2) * 8 + y * 2 + dz
        remote = lambda: pltpu.make_async_remote_copy(
            src_ref=parts.at[at], dst_ref=sums.at[slot],
            send_sem=part_send.at[alone], recv_sem=part_recv,
            device_id=dest, device_id_type=MESH,
        )
        local = lambda: pltpu.make_async_copy(parts.at[at], sums.at[slot], part_recv)
        here = (dest[0] == grp) & (dest[1] == tp)
        return remote, local, here

    for which, sem in ((core, own_sem), (other, old_recv)):
        rows = weight.at[:, pl.ds(pl.multiple_of(which * LOCAL, LOCAL), LOCAL)]
        pltpu.make_async_copy(rows, rows, sem).wait()
    for half in range(2):
        rows = arrived.at[pl.ds(half * 256, 256)]
        pltpu.make_async_copy(rows, rows, delta_recv.at[half]).wait()
        fresh = []
        for q in range(8):
            first = q * 64 + half * 32
            coming = half * 256 + q * 32
            fresh.append(
                (weight[first:first + 32, :].astype(F32) + arrived[coming:coming + 32, :].astype(F32)).astype(BF16)
            )
        fresh = jnp.concatenate(fresh, axis=0)
        for plane in range(2):
            if half == 0:
                if plane == 1:
                    for k in OTHER_PLANE:
                        for c in range(CHUNKS):
                            act_copy(c, k).wait_recv()
                        fwd_copy(None, k).start()
                other_lanes = pl.ds(pl.multiple_of(other * LOCAL, LOCAL), LOCAL)
                rows = acts.at[pl.ds((z_lo + plane) % 2 * 4, 4), :, other_lanes]
                pltpu.make_async_copy(rows, rows, fwd_recv.at[plane]).wait()
            for pair in range(1):
                start = (z_lo + plane) % 2 * 4
                lhs = acts[pl.ds(start, 4)].reshape(4 * ALL, 1024)
                got = lax.dot_general(lhs, fresh, CONTRACT_LAST, preferred_element_type=F32)
                for part in range(4):
                    for dz in range(2):
                        at = ((half * 2 + plane) * 2 + dz) * 4 + part
                        parts[at] = got[part * ALL:(part + 1) * ALL, dz * 128:dz * 128 + 128].astype(BF16)
                for dx, dz in PART_ORDER:
                    remote, local, here = part_copy(half, plane, dz, dx)
                    if plane == 1 or dx > 0:
                        remote().start()
                        continue

                    @pl.when(here)
                    def _():
                        local().start()

                    @pl.when(jnp.logical_not(here))
                    def _():
                        remote().start()

    for k in range(3):
        square_copy(k).wait_recv()
    squares[y] = own_square[...] + near_squares[0] + near_squares[1] + near_squares[2]
    for k in range(3, 6):
        square_copy(k).start()
    for k in range(3, 6):
        square_copy(k).wait_recv()
    pltpu.make_async_copy(delta.at[pl.ds(0, 7)], delta.at[pl.ds(0, 7)], delta_send.at[0]).wait()
    for count, sem in ((7, act_send), (8, fwd_send)):
        rows = acts.at[pl.ds(0, count), :, own_lanes]
        pltpu.make_async_copy(rows, rows, sem).wait()

    @pl.when(jnp.logical_not(own_delta))
    def _():
        for half in range(2):
            delta_copy(7, half).wait_send()
    rows = weight.at[:, own_lanes]
    pltpu.make_async_copy(rows, rows, old_send).wait()
    for k in range(6):
        square_copy(k).wait_send()
    pltpu.make_async_copy(parts.at[pl.ds(0, 28)], parts.at[pl.ds(0, 28)], part_send.at[0]).wait()
    for half in range(2):
        for dz in range(2):
            remote, _, here = part_copy(half, 0, dz, 0)

            @pl.when(jnp.logical_not(here))
            def _():
                remote().wait_send()
    pltpu.make_async_copy(sums, sums, part_recv).wait()


def finish_kernel(held, sums, squares, out_ref, final_ref, sem):
    copies = [
        pltpu.make_async_copy(held.at[pl.ds(c * 6, 6)], final_ref.at[pl.ds(c * 6, 6)], sem.at[c])
        for c in range(4)
    ]
    for copy in copies:
        copy.start()
    factors = []
    for yy in range(4):
        inverse = lax.rsqrt(squares[yy] * (1.0 / GROUP_WIDTH) + 1e-05)
        factors.append(jnp.transpose(jnp.concatenate([inverse] * 16, axis=0))[0:ALL, 0:1])
    lane = lax.broadcasted_iota(jnp.int32, (256, 256), 1)
    source = (lane // 32) % 2 * 128 + lane // 128 * 64 + (lane // 64) % 2 * 32 + lane % 32
    order = (lax.broadcasted_iota(jnp.int32, (256, 256), 0) == source).astype(BF16)
    for hi in range(2):
        totals = []
        for half in range(2):
            total = None
            for yy in range(4):
                slot = (half * 2 + hi) * 8 + yy * 2
                pair = (sums[slot].astype(F32) + sums[slot + 1].astype(F32)) * factors[yy]
                total = pair if total is None else total + pair
            totals.append(total.astype(BF16))
        total = jnp.dot(jnp.concatenate(totals, axis=1), order, preferred_element_type=F32)
        for s in range(STEPS):
            rows = jnp.concatenate(
                [
                    total[c * SENT_ROWS + s * CHUNK_ROWS:c * SENT_ROWS + (s + 1) * CHUNK_ROWS]
                    for c in range(CHUNKS)
                ],
                axis=0,
            ).astype(BF16)
            for yl in range(2):
                at = yl * 256 + hi * 128
                out_ref[s, :, at:at + 128] = rows[:, yl * 128:(yl + 1) * 128]
    for copy in copies:
        copy.wait()


def local(
    old_weight, delta_codes, delta_exps, state_in, x_in, z_in, b_in, c_in, dt_in,
    dt_bias, a_rate, skip_gain, norm_gain,
):
    vmem = pl.BlockSpec(memory_space=pltpu.VMEM)
    hbm = pl.BlockSpec(memory_space=pltpu.HBM)
    dma = pltpu.SemaphoreType.DMA
    vectors = [v.reshape(1, -1) for v in (dt_bias, a_rate, skip_gain, norm_gain)]
    held, sums, squares = pl.pallas_call(
        mix_kernel,
        out_shape=(
            pltpu.VMEM(state_in.shape, F32),
            pltpu.VMEM((32, ALL, 128), BF16),
            pltpu.VMEM((4, 8, 128), F32),
        ),
        in_specs=[hbm] * 13,
        out_specs=(vmem, vmem, vmem),
        scratch_shapes=[
            pltpu.VMEM((64, 64), jnp.int32),
            pltpu.VMEM(x_in.shape, BF16),
            pltpu.VMEM(x_in.shape, BF16),
            pltpu.VMEM(b_in.shape, BF16),
            pltpu.VMEM(b_in.shape, BF16),
            pltpu.VMEM((STEPS, HEADS, ROWS), BF16),
            pltpu.VMEM((1, HEADS), F32),
            pltpu.VMEM((1, HEADS), F32),
            pltpu.VMEM((1, HEADS), F32),
            pltpu.VMEM((1, LOCAL), F32),
            pltpu.VMEM((LOCAL // 128, 16 * ROWS, 128), F32),
            pltpu.VMEM((2, 16 * ROWS, STATE), F32),
            pltpu.VMEM((1, 8 * ROWS, STATE), F32),
            pltpu.VMEM((LOCAL // 128, 8 * ROWS, 128), F32),
            pltpu.VMEM((ALL, LOCAL), F32),
            pltpu.VMEM((ALL, LOCAL), F32),
            pltpu.VMEM((128, 128), F32),
            pltpu.VMEM((8, 64, 1024), jnp.int32),
            pltpu.VMEM((8, 64, 1024), BF16),
            pltpu.VMEM((512, 1024), BF16),
            pltpu.VMEM((512, 1024), BF16),
            pltpu.VMEM((8, ALL, 1024), BF16),
            pltpu.VMEM((32, ALL, 128), BF16),
            pltpu.VMEM((8, 128), F32),
            pltpu.VMEM((3, 8, 128), F32),
            dma((10,)), dma((CHUNKS,)), dma((8,)), dma, dma, dma, dma((3,)), dma((2,)),
            dma, dma((7 * CHUNKS,)), dma, dma((2,)),
            dma((5,)), dma, dma((6,)), dma((6,)),
        ],
        compiler_params=pltpu.CompilerParams(
            collective_id=0, has_side_effects=True, vmem_limit_bytes=36 * 1024 * 1024
        ),
        cost_estimate=pl.CostEstimate(flops=9 * 10**8, bytes_accessed=10**7, transcendentals=0),
    )(
        *[
            pltpu.with_memory_space_constraint(a, pltpu.HBM)
            for a in (
                delta_codes, delta_exps, old_weight, state_in, x_in, z_in, b_in, c_in,
                jnp.swapaxes(dt_in, 1, 2), *vectors,
            )
        ]
    )
    mixed, final_state = pl.pallas_call(
        finish_kernel,
        out_shape=(
            jax.ShapeDtypeStruct((STEPS, ROWS, LOCAL), BF16),
            jax.ShapeDtypeStruct(state_in.shape, F32),
        ),
        in_specs=[vmem] * 3,
        out_specs=(vmem, hbm),
        scratch_shapes=[dma((4,))],
        compiler_params=pltpu.CompilerParams(vmem_limit_bytes=36 * 1024 * 1024),
        cost_estimate=pl.CostEstimate(flops=10**6, bytes_accessed=7 * 10**6, transcendentals=0),
    )(held, sums, squares)
    return mixed, final_state


def solution(mesh):
    return jax.shard_map(
        local,
        mesh=mesh,
        in_specs=(
            P(None, "tp"),
            P(("grp", "tp"), None),
            P(("grp", "tp"), None),
            P("grp", "tp", None, None),
            P(None, "grp", "tp"),
            P(None, "grp", "tp"),
            P(None, "grp", None),
            P(None, "grp", None),
            P(None, "grp", "tp"),
            P("tp"),
            P("tp"),
            P("tp"),
            P("tp"),
        ),
        out_specs=(P(None, "grp", "tp"), P("grp", "tp", None, None)),
        check_vma=False,
    )
```

```python
import functools

import jax
import jax.numpy as jnp
from jax import lax
from jax.experimental import pallas as pl
from jax.experimental.pallas import tpu as pltpu
from jax.sharding import PartitionSpec as P

MESH = pl.DeviceIdType.MESH
F32 = jnp.float32
BF16 = jnp.bfloat16
STEPS = 4
ROWS = 24
ALL = STEPS * ROWS
LOCAL = 512
STATE = 128
GROUP_WIDTH = 2048
CHUNKS = 3
CHUNK_ROWS = ROWS // CHUNKS
SENT_ROWS = STEPS * CHUNK_ROWS
HEADS = 8
CONTRACT_LAST = (((1,), (1,)), ((), ()))
CONTRACT_FIRST = (((0,), (0,)), ((), ()))


def split3(value):
    first = value.astype(BF16)
    rest = value - first.astype(F32)
    second = rest.astype(BF16)
    third = (rest - second.astype(F32)).astype(BF16)
    return first, second, third


def expand_heads(value, spread):
    parts = split3(value)
    total = jnp.dot(parts[2], spread, preferred_element_type=F32)
    total = total + jnp.dot(parts[1], spread, preferred_element_type=F32)
    return total + jnp.dot(parts[0], spread, preferred_element_type=F32)


def put(ref, first, value):
    for j in range(value.shape[1] // 128):
        ref[j, first:first + value.shape[0], :] = value[:, j * 128:(j + 1) * 128]


def pick_rows(ref, row, count):
    return jnp.concatenate(
        [ref[j, pl.ds(row, count, stride=ROWS), :] for j in range(ref.shape[0])], axis=1
    )


UNROLL = 8
PART_ORDER = ((1, 0), (1, 1), (3, 0), (3, 1), (2, 0), (2, 1), (0, 0), (0, 1))
OFFSETS = ((2, 0), (0, 1), (1, 0), (3, 1), (3, 0), (1, 1), (2, 1), (0, 0))
GATHER = ((0, 1), (0, 3), (0, 2), (1, 0), (1, 1), (1, 3), (1, 2))
OWN_PLANE = (0, 1, 2, 3)
OTHER_PLANE = (4, 5, 6)


def mix_kernel(
    codes_ref, exps_ref, old_ref, state_ref, x_ref, z_ref, b_ref, c_ref, dt_ref,
    bias_ref, rate_ref, skip_ref, gain_ref,
    held, sums, squares,
    exps, xs_in, zs_in, bs_in, cs_in, dts_in, bias_in, rate_in, skip_in, gain_in,
    left_rows, right_rows, read_rows, read_state, decay_rows, direct_rows, square_rows,
    codes, delta, weight, arrived, acts, parts, own_square, near_squares,
    small_sem, state_sem, codes_sem, own_sem, old_send, old_recv, delta_send, delta_recv,
    act_send, act_recv, fwd_send, fwd_recv, part_send, part_recv, square_send, square_recv,
):
    grp, tp = lax.axis_index("grp"), lax.axis_index("tp")
    z_lo, x = grp // 4, grp % 4
    y, z_hi, core = tp // 4, (tp // 2) % 2, tp % 2
    other = 1 - core
    chip = tp // 2
    partner = (grp, tp - core + other)
    mine = chip == grp
    crossed = chip == (1 - z_lo) * 4 + x

    def place(lo, xx, yy, hi, cc):
        return (lo * 4 + xx, yy * 4 + hi * 2 + cc)

    for k in range(8):
        dy, dz = OFFSETS[k]
        column = ((y + dy) % 4) * 2 + (z_hi + dz) % 2
        pltpu.make_async_copy(
            codes_ref.at[:, pl.ds(pl.multiple_of(column * 1024, 1024), 1024)], codes.at[k], codes_sem.at[k]
        ).start()

    small = [
        (exps_ref, exps), (dt_ref, dts_in), (bias_ref, bias_in), (rate_ref, rate_in), (skip_ref, skip_in),
        (x_ref, xs_in), (b_ref, bs_in), (c_ref, cs_in), (z_ref, zs_in), (gain_ref, gain_in),
    ]

    def small_copy(k):
        return pltpu.make_async_copy(small[k][0], small[k][1], small_sem.at[k])

    def state_copy(c):
        span = pl.ds(c * CHUNK_ROWS, CHUNK_ROWS)
        return pltpu.make_async_copy(state_ref.at[span], held.at[span], state_sem.at[c])

    for k in range(len(small)):
        small_copy(k).start()

    barrier = pltpu.get_barrier_semaphore()

    def greet(where):
        pl.semaphore_signal(barrier, inc=1, device_id=where, device_id_type=MESH)

    greet(partner)
    for cc in range(2):
        for yl in range(2):
            for dz in range(2):
                where = place((z_lo + dz) % 2, x, 2 * core + yl, (z_hi + dz) % 2, cc)
                if dz == 0:
                    @pl.when(jnp.logical_not((cc == core) & (2 * core + yl == y)))
                    def _():
                        greet(where)
                else:
                    greet(where)
    for dl, dx in GATHER[:6]:
        greet(((z_lo + dl) % 2 * 4 + (x + dx) % 4, tp))
    for cc in range(2):
        greet(place(z_lo, x, y, 1 - z_hi, (core + cc) % 2))
    for dy in range(1, 4):
        greet(place(z_lo, x, (y + dy) % 4, z_hi, core))
    for lo in range(2):
        for yy in range(4):
            for hi in range(2):
                where = place(lo, chip % 4, yy, hi, core)

                @pl.when(jnp.logical_not((where[0] == grp) & (where[1] == tp)))
                def _():
                    greet(where)
    own_delta = core == y // 2
    expected = (
        1 + 8 - own_delta.astype(jnp.int32) + 6 + 2 + 3 + 16 - mine.astype(jnp.int32) - crossed.astype(jnp.int32)
    )
    own_lanes = pl.ds(pl.multiple_of(core * LOCAL, LOCAL), LOCAL)

    def act_copy(c, k):
        dl, dx = GATHER[k]
        slot, where = grp, ((z_lo + dl) % 2 * 4 + (x + dx) % 4, tp)
        if k == 6:
            slot, where = z_lo * 4 + (x + 2) % 4, ((z_lo + 1) % 2 * 4 + x, tp)
        piece = acts.at[slot, pl.ds(c * SENT_ROWS, SENT_ROWS), own_lanes]
        return pltpu.make_async_remote_copy(
            src_ref=piece, dst_ref=piece,
            send_sem=act_send, recv_sem=act_recv.at[c * 7 + k],
            device_id=where, device_id_type=MESH,
        )

    def fwd_copy(c, k):
        slot = grp
        if k < 7:
            dl, dx = GATHER[k]
            slot = (z_lo + dl) % 2 * 4 + (x + 4 - dx) % 4
        piece = acts.at[slot, pl.ds(0, ALL) if c is None else pl.ds(c * SENT_ROWS, SENT_ROWS), own_lanes]
        return pltpu.make_async_remote_copy(
            src_ref=piece, dst_ref=piece,
            send_sem=fwd_send, recv_sem=fwd_recv.at[0 if k in (7, 0, 1, 2) else 1],
            device_id=partner, device_id_type=MESH,
        )

    def square_copy(k):
        if k < 3:
            other_chip, other_core = ((0, 1), (1, 0), (1, 1))[k]
            where = place(z_lo, x, y, (z_hi + other_chip) % 2, (core + other_core) % 2)
            source, target = own_square, near_squares.at[k]
        else:
            where = place(z_lo, x, (y + k - 2) % 4, z_hi, core)
            source = target = squares.at[y]
        return pltpu.make_async_remote_copy(
            src_ref=source, dst_ref=target,
            send_sem=square_send.at[k], recv_sem=square_recv.at[k],
            device_id=where, device_id_type=MESH,
        )

    def feature_row(slab, cc):
        dz, yl = slab // 2, slab % 2
        lo, hi = (z_lo + dz) % 2, (z_hi + dz) % 2
        row = ((lo * 4 + x) * 2 + cc) * 512 + yl * 256 + hi * 128
        return pl.ds(pl.multiple_of(row, 128), 128)

    def own_copy(slab):
        return pltpu.make_async_copy(
            old_ref.at[feature_row(slab, core)],
            weight.at[pl.ds(slab * 128, 128), pl.ds(pl.multiple_of(core * LOCAL, LOCAL), LOCAL)],
            own_sem,
        )

    def old_copy(slab):
        return pltpu.make_async_remote_copy(
            src_ref=old_ref.at[feature_row(slab, other)],
            dst_ref=weight.at[pl.ds(slab * 128, 128), pl.ds(pl.multiple_of(core * LOCAL, LOCAL), LOCAL)],
            send_sem=old_send, recv_sem=old_recv,
            device_id=partner, device_id_type=MESH,
        )

    def delta_copy(k, half):
        dy, dz = OFFSETS[k]
        slot = half * 8 + dz * 4 + (y % 2) * 2 + core
        return pltpu.make_async_remote_copy(
            src_ref=delta.at[k, pl.ds(half * 32, 32)], dst_ref=arrived.at[pl.ds(pl.multiple_of(slot * 32, 32), 32)],
            send_sem=delta_send.at[0 if k < 7 else 1 + half], recv_sem=delta_recv.at[half],
            device_id=place((z_lo + dz) % 2, x, (y + dy) % 4, (z_hi + dz) % 2, y // 2), device_id_type=MESH,
        )

    def delta_self(half):
        slot = half * 8 + (y % 2) * 2 + core
        return pltpu.make_async_copy(
            delta.at[7, pl.ds(half * 32, 32)], arrived.at[pl.ds(pl.multiple_of(slot * 32, 32), 32)],
            delta_recv.at[half],
        )

    small_copy(0).wait()
    scale = jnp.where(
        exps[...] == -14, 2.0**-14, jnp.where(exps[...] == -13, 2.0**-13, 2.0**-12)
    ).astype(BF16)
    block_at = lax.broadcasted_iota(jnp.int32, (64, 1024), 0)
    lane_block = lax.broadcasted_iota(jnp.int32, (64, 1024), 1) // 128
    for k in range(8):
        dy, dz = OFFSETS[k]
        column = ((y + dy) % 4) * 2 + (z_hi + dz) % 2
        pltpu.make_async_copy(codes.at[k], codes.at[k], codes_sem.at[k]).wait()
        if k == 3:
            for c in range(CHUNKS):
                state_copy(c).start()
        pick = (block_at == lane_block + column * 8).astype(BF16)
        wide = jnp.dot(scale, pick, preferred_element_type=F32)
        delta[k] = (codes[k].astype(F32) * wide).astype(BF16)

    for k in range(1, len(small)):
        small_copy(k).wait()
    group = tp // 4
    group_lanes = pl.ds(pl.multiple_of(group * STATE, STATE), STATE)
    head_of = lax.broadcasted_iota(jnp.int32, (HEADS, LOCAL), 1) // (LOCAL // HEADS)
    spread = (head_of == lax.broadcasted_iota(jnp.int32, (HEADS, LOCAL), 0)).astype(BF16)
    bias = expand_heads(jnp.broadcast_to(bias_in[...], (8, HEADS)), spread)[0:1]
    rate = expand_heads(jnp.broadcast_to(rate_in[...], (8, HEADS)), spread)[0:1]
    skip = expand_heads(jnp.broadcast_to(skip_in[...], (8, HEADS)), spread)[0:1]
    sizes, logs = [], []
    for s in range(STEPS):
        raw = lax.dot_general(dts_in[s], spread, CONTRACT_FIRST, preferred_element_type=F32) + bias
        sizes.append(jnp.maximum(raw, 0.0) + jnp.log1p(jnp.exp(-jnp.abs(raw))))
        own = sizes[s] * rate
        logs.append(own if s == 0 else logs[-1] + own)
    xs = [xs_in[s].astype(F32) for s in range(STEPS)]
    bs = [bs_in[s, :, group_lanes].astype(F32) for s in range(STEPS)]
    cs = [cs_in[s, :, group_lanes].astype(F32) for s in range(STEPS)]
    right_rows[...] = jnp.zeros(right_rows.shape, F32)
    read_rows[...] = jnp.zeros(read_rows.shape, F32)
    for s in range(STEPS):
        right_rows[0, s * ROWS:(s + 1) * ROWS, :] = bs[s]
        right_rows[0, (4 + s) * ROWS:(5 + s) * ROWS, :] = bs[s]
        read_rows[0, s * ROWS:(s + 1) * ROWS, :] = cs[s]
    right_rows[1, 8 * ROWS:11 * ROWS, :] = jnp.ones((3 * ROWS, STATE), F32)
    for s in range(STEPS):
        decay_rows[s * ROWS:(s + 1) * ROWS, :] = jnp.exp(-logs[s])
        direct = skip * xs[s]
        for u in range(s + 1):
            coef = sizes[u] if u == s else sizes[u] * jnp.exp(logs[u] - logs[s])
            term = coef * xs[u]
            direct = direct + term * jnp.sum(bs[u] * cs[s], axis=1, keepdims=True)
            if s == STEPS - 1:
                high = term.astype(BF16).astype(F32)
                put(left_rows, u * ROWS, high)
                put(left_rows, (4 + u) * ROWS, term - high)
        direct_rows[s * ROWS:(s + 1) * ROWS, :] = direct
    last = decay_rows[3 * ROWS:4 * ROWS, :]
    for at_row, part in enumerate(split3(last)):
        put(left_rows, (8 + at_row) * ROWS, part.astype(F32))
    put(left_rows, 11 * ROWS, jnp.zeros((5 * ROWS, LOCAL), F32))
    square_rows[ALL:, :] = jnp.zeros((128 - ALL, 128), F32)

    for slab in range(4):
        own_copy(slab).start()
    pl.semaphore_wait(barrier, expected)
    for k in range(7):
        delta_copy(k, 0).start()

    def read_one(row):
        value = held[row].reshape(LOCAL, STATE)
        high = value.astype(BF16)
        low = (value - high.astype(F32)).astype(BF16)
        both = jnp.concatenate([high, low], axis=1)
        reader = pick_rows(read_rows, row, 8).astype(BF16)
        reader = jnp.concatenate([reader, reader], axis=1)
        read = lax.dot_general(reader, both, CONTRACT_LAST, preferred_element_type=F32)
        for j in range(LOCAL // 128):
            read_state[j, pl.ds(row, 8, stride=ROWS), :] = read[:, j * 128:(j + 1) * 128]

    def update_one(row):
        left = pick_rows(left_rows, row, 16).astype(BF16)
        right = pick_rows(right_rows, row, 16).astype(BF16)
        update = lax.dot_general(left, right, CONTRACT_FIRST, preferred_element_type=F32)
        value = held[row].reshape(LOCAL, STATE)
        held[row] = (update[:, STATE:] * value + update[:, :STATE]).reshape(held.shape[1:])

    def over_rows(first, count, unroll, one):
        def some(i, carry):
            for j in range(unroll):
                one(first + i * unroll + j)
            return carry

        lax.fori_loop(0, count // unroll, some, 0)

    for c in range(CHUNKS):
        state_copy(c).wait()
        over_rows(c * CHUNK_ROWS, CHUNK_ROWS, UNROLL, read_one)
        pieces = []
        for s in range(STEPS):
            span = slice(s * ROWS + c * CHUNK_ROWS, s * ROWS + (c + 1) * CHUNK_ROWS)
            read = jnp.concatenate([read_state[j, span, :] for j in range(LOCAL // 128)], axis=1)
            z = zs_in[s].astype(F32)[c * CHUNK_ROWS:(c + 1) * CHUNK_ROWS]
            read_out = decay_rows[span, :] * read + direct_rows[span, :]
            pieces.append(read_out * (z / (1.0 + jnp.exp(-z))))
        gated = jnp.concatenate(pieces, axis=0)
        acts[grp, c * SENT_ROWS:(c + 1) * SENT_ROWS, own_lanes] = (gated * gain_in[...]).astype(BF16)
        for k in range(6):
            act_copy(c, k).start()
        fwd_copy(c, 7).start()
        total = jnp.sum(gated * gated, axis=1, keepdims=True)
        square_rows[c * SENT_ROWS:(c + 1) * SENT_ROWS, :] = jnp.broadcast_to(total, (SENT_ROWS, 128))
    @pl.when(own_delta)
    def _():
        for half in range(2):
            delta_self(half).start()

    @pl.when(jnp.logical_not(own_delta))
    def _():
        for half in range(2):
            delta_copy(7, half).start()

    for k in range(7):
        delta_copy(k, 1).start()
    for slab in range(4):
        old_copy(slab).start()

    own_square[...] = jnp.transpose(square_rows[...])[0:8]
    for k in range(3):
        square_copy(k).start()

    over_rows(0, ROWS, UNROLL, update_one)
    for c in range(CHUNKS):
        for k in OWN_PLANE:
            act_copy(c, k).wait_recv()
            fwd_copy(c, k).start()
            if k == 2:
                act_copy(c, 6).start()

    def part_copy(half, plane, dz, dx):
        i = (x + dx) % 4
        g = (z_lo + plane) % 2 * 4 + i
        alone = 1 + half * 2 + dz if plane == 0 and dx == 0 else 0
        dest = (g, ((z_lo + dz) % 2 * 4 + x) * 2 + core)
        at = ((half * 2 + plane) * 2 + dz) * 4 + i
        slot = (half * 2 + (z_hi + dz) % 2) * 8 + y * 2 + dz
        remote = lambda: pltpu.make_async_remote_copy(
            src_ref=parts.at[at], dst_ref=sums.at[slot],
            send_sem=part_send.at[alone], recv_sem=part_recv,
            device_id=dest, device_id_type=MESH,
        )
        local = lambda: pltpu.make_async_copy(parts.at[at], sums.at[slot], part_recv)
        here = (dest[0] == grp) & (dest[1] == tp)
        return remote, local, here

    for which, sem in ((core, own_sem), (other, old_recv)):
        rows = weight.at[:, pl.ds(pl.multiple_of(which * LOCAL, LOCAL), LOCAL)]
        pltpu.make_async_copy(rows, rows, sem).wait()
    for half in range(2):
        rows = arrived.at[pl.ds(half * 256, 256)]
        pltpu.make_async_copy(rows, rows, delta_recv.at[half]).wait()
        fresh = []
        for q in range(8):
            first = q * 64 + half * 32
            coming = half * 256 + q * 32
            fresh.append(
                weight[first:first + 32, :] + arrived[coming:coming + 32, :]
            )
        fresh = jnp.concatenate(fresh, axis=0)
        for plane in range(2):
            if half == 0:
                if plane == 1:
                    for k in OTHER_PLANE:
                        for c in range(CHUNKS):
                            act_copy(c, k).wait_recv()
                        fwd_copy(None, k).start()
                other_lanes = pl.ds(pl.multiple_of(other * LOCAL, LOCAL), LOCAL)
                rows = acts.at[pl.ds((z_lo + plane) % 2 * 4, 4), :, other_lanes]
                pltpu.make_async_copy(rows, rows, fwd_recv.at[plane]).wait()
            for pair in range(1):
                start = (z_lo + plane) % 2 * 4
                lhs = acts[pl.ds(start, 4)].reshape(4 * ALL, 1024)
                got = lax.dot_general(lhs, fresh, CONTRACT_LAST, preferred_element_type=F32)
                for part in range(4):
                    for dz in range(2):
                        at = ((half * 2 + plane) * 2 + dz) * 4 + part
                        parts[at] = got[part * ALL:(part + 1) * ALL, dz * 128:dz * 128 + 128].astype(BF16)
                for dx, dz in PART_ORDER:
                    remote, local, here = part_copy(half, plane, dz, dx)
                    if plane == 1 or dx > 0:
                        remote().start()
                        continue

                    @pl.when(here)
                    def _():
                        local().start()

                    @pl.when(jnp.logical_not(here))
                    def _():
                        remote().start()

    for k in range(3):
        square_copy(k).wait_recv()
    squares[y] = own_square[...] + near_squares[0] + near_squares[1] + near_squares[2]
    for k in range(3, 6):
        square_copy(k).start()
    for k in range(3, 6):
        square_copy(k).wait_recv()
    pltpu.make_async_copy(delta.at[pl.ds(0, 7)], delta.at[pl.ds(0, 7)], delta_send.at[0]).wait()
    for count, sem in ((7, act_send), (8, fwd_send)):
        rows = acts.at[pl.ds(0, count), :, own_lanes]
        pltpu.make_async_copy(rows, rows, sem).wait()

    @pl.when(jnp.logical_not(own_delta))
    def _():
        for half in range(2):
            delta_copy(7, half).wait_send()
    rows = weight.at[:, own_lanes]
    pltpu.make_async_copy(rows, rows, old_send).wait()
    for k in range(6):
        square_copy(k).wait_send()
    pltpu.make_async_copy(parts.at[pl.ds(0, 28)], parts.at[pl.ds(0, 28)], part_send.at[0]).wait()
    for half in range(2):
        for dz in range(2):
            remote, _, here = part_copy(half, 0, dz, 0)

            @pl.when(jnp.logical_not(here))
            def _():
                remote().wait_send()
    pltpu.make_async_copy(sums, sums, part_recv).wait()


def finish_kernel(held, sums, squares, out_ref, final_ref, sem):
    copies = [
        pltpu.make_async_copy(held.at[pl.ds(c * 6, 6)], final_ref.at[pl.ds(c * 6, 6)], sem.at[c])
        for c in range(4)
    ]
    for copy in copies:
        copy.start()
    factors = []
    for yy in range(4):
        inverse = lax.rsqrt(squares[yy] * (1.0 / GROUP_WIDTH) + 1e-05)
        factors.append(jnp.transpose(jnp.concatenate([inverse] * 16, axis=0))[0:ALL, 0:1])
    lane = lax.broadcasted_iota(jnp.int32, (256, 256), 1)
    source = (lane // 32) % 2 * 128 + lane // 128 * 64 + (lane // 64) % 2 * 32 + lane % 32
    order = (lax.broadcasted_iota(jnp.int32, (256, 256), 0) == source).astype(BF16)
    for hi in range(2):
        totals = []
        for half in range(2):
            total = None
            for yy in range(4):
                slot = (half * 2 + hi) * 8 + yy * 2
                pair = (sums[slot].astype(F32) + sums[slot + 1].astype(F32)) * factors[yy]
                total = pair if total is None else total + pair
            totals.append(total.astype(BF16))
        total = jnp.dot(jnp.concatenate(totals, axis=1), order, preferred_element_type=F32)
        for s in range(STEPS):
            rows = jnp.concatenate(
                [
                    total[c * SENT_ROWS + s * CHUNK_ROWS:c * SENT_ROWS + (s + 1) * CHUNK_ROWS]
                    for c in range(CHUNKS)
                ],
                axis=0,
            ).astype(BF16)
            for yl in range(2):
                at = yl * 256 + hi * 128
                out_ref[s, :, at:at + 128] = rows[:, yl * 128:(yl + 1) * 128]
    for copy in copies:
        copy.wait()


def local(
    old_weight, delta_codes, delta_exps, state_in, x_in, z_in, b_in, c_in, dt_in,
    dt_bias, a_rate, skip_gain, norm_gain,
):
    vmem = pl.BlockSpec(memory_space=pltpu.VMEM)
    hbm = pl.BlockSpec(memory_space=pltpu.HBM)
    dma = pltpu.SemaphoreType.DMA
    vectors = [v.reshape(1, -1) for v in (dt_bias, a_rate, skip_gain, norm_gain)]
    held, sums, squares = pl.pallas_call(
        mix_kernel,
        out_shape=(
            pltpu.VMEM(state_in.shape, F32),
            pltpu.VMEM((32, ALL, 128), BF16),
            pltpu.VMEM((4, 8, 128), F32),
        ),
        in_specs=[hbm] * 13,
        out_specs=(vmem, vmem, vmem),
        scratch_shapes=[
            pltpu.VMEM((64, 64), jnp.int32),
            pltpu.VMEM(x_in.shape, BF16),
            pltpu.VMEM(x_in.shape, BF16),
            pltpu.VMEM(b_in.shape, BF16),
            pltpu.VMEM(b_in.shape, BF16),
            pltpu.VMEM((STEPS, HEADS, ROWS), BF16),
            pltpu.VMEM((1, HEADS), F32),
            pltpu.VMEM((1, HEADS), F32),
            pltpu.VMEM((1, HEADS), F32),
            pltpu.VMEM((1, LOCAL), F32),
            pltpu.VMEM((LOCAL // 128, 16 * ROWS, 128), F32),
            pltpu.VMEM((2, 16 * ROWS, STATE), F32),
            pltpu.VMEM((1, 8 * ROWS, STATE), F32),
            pltpu.VMEM((LOCAL // 128, 8 * ROWS, 128), F32),
            pltpu.VMEM((ALL, LOCAL), F32),
            pltpu.VMEM((ALL, LOCAL), F32),
            pltpu.VMEM((128, 128), F32),
            pltpu.VMEM((8, 64, 1024), jnp.int32),
            pltpu.VMEM((8, 64, 1024), BF16),
            pltpu.VMEM((512, 1024), BF16),
            pltpu.VMEM((512, 1024), BF16),
            pltpu.VMEM((8, ALL, 1024), BF16),
            pltpu.VMEM((32, ALL, 128), BF16),
            pltpu.VMEM((8, 128), F32),
            pltpu.VMEM((3, 8, 128), F32),
            dma((10,)), dma((CHUNKS,)), dma((8,)), dma, dma, dma, dma((3,)), dma((2,)),
            dma, dma((7 * CHUNKS,)), dma, dma((2,)),
            dma((5,)), dma, dma((6,)), dma((6,)),
        ],
        compiler_params=pltpu.CompilerParams(
            collective_id=0, has_side_effects=True, vmem_limit_bytes=36 * 1024 * 1024
        ),
        cost_estimate=pl.CostEstimate(flops=9 * 10**8, bytes_accessed=10**7, transcendentals=0),
    )(
        *[
            pltpu.with_memory_space_constraint(a, pltpu.HBM)
            for a in (
                delta_codes, delta_exps, old_weight, state_in, x_in, z_in, b_in, c_in,
                jnp.swapaxes(dt_in, 1, 2), *vectors,
            )
        ]
    )
    mixed, final_state = pl.pallas_call(
        finish_kernel,
        out_shape=(
            jax.ShapeDtypeStruct((STEPS, ROWS, LOCAL), BF16),
            jax.ShapeDtypeStruct(state_in.shape, F32),
        ),
        in_specs=[vmem] * 3,
        out_specs=(vmem, hbm),
        scratch_shapes=[dma((4,))],
        compiler_params=pltpu.CompilerParams(vmem_limit_bytes=36 * 1024 * 1024),
        cost_estimate=pl.CostEstimate(flops=10**6, bytes_accessed=7 * 10**6, transcendentals=0),
    )(held, sums, squares)
    return mixed, final_state


def solution(mesh):
    return jax.shard_map(
        local,
        mesh=mesh,
        in_specs=(
            P(None, "tp"),
            P(("grp", "tp"), None),
            P(("grp", "tp"), None),
            P("grp", "tp", None, None),
            P(None, "grp", "tp"),
            P(None, "grp", "tp"),
            P(None, "grp", None),
            P(None, "grp", None),
            P(None, "grp", "tp"),
            P("tp"),
            P("tp"),
            P("tp"),
            P("tp"),
        ),
        out_specs=(P(None, "grp", "tp"), P("grp", "tp", None, None)),
        check_vma=False,
    )
```
